256 devices in a mesh: dp: 256 (over z, y, x, core).
Axes of the slice: x: 4, y: 4, z: 8, core: 2. Of those that a mesh axis runs over, the one named last changes fastest.
Arguments:
- img_feats: bfloat16 [32768, 1536], P('dp'), may hold values from -30 to 30
- txt_feats: bfloat16 [32768, 4096], P('dp'), may hold values from -5 to 5
- img_head: bfloat16 [1536, 1024], replicated, may hold values from -0.12885337 to 0.12885337
- txt_head: bfloat16 [4096, 1024], replicated, may hold values from -0.07890625 to 0.07890625
- log_scale: float32 [1], replicated, may hold values from 3.4 to 4
- logit_bias: float32 [1], replicated, may hold values from -4 to -2
Outputs:
- loss: float32 [], replicated
- scalar_grads: float32 [2], replicated
- head_grad: float32 [1536, 1024], P('dp')
- text_grad: float32 [32768, 1024], P('dp')
The draws below stay inside these ranges and needn't reach their ends.
All inputs are finite; a program needn't handle non-finite values.
Results may differ from the reference program's by a relative error of at most 0.001.
Values may be sent and summed in bfloat16 or wider, within the bound.
A program may use at most 128 MiB of HBM per device.

```python
import math
import jax
import jax.numpy as jnp
from jax import lax

D_IMG = 1536
D_TXT = 4096
EMB = 1024
TOK_DEV = 128
HALF = 6
TOKENS = 32768
PAIRS = 54525952
N_DP = 256


feat_share = 0.6


head_share = 0.67


spike_gain = 6.0


clip_level = 5.0


def shared_normal(base_key, stream, out_shape):
    return jax.random.normal(jax.random.fold_in(base_key, stream), out_shape, jnp.float32)


def rising_part(base_key, top):
    direction = shared_normal(base_key, 303, (1, min(D_IMG, D_TXT)))
    blocks = TOKENS // TOK_DEV
    block_index = (jnp.arange(TOKENS) // TOK_DEV).astype(jnp.float32)
    amplitude = top * block_index / max(blocks - 1, 1)
    return amplitude[:, None] * direction


def blend_columns(common, private, share):
    padded = jnp.pad(common, ((0, 0), (0, private.shape[1] - common.shape[1])))
    inside = jnp.arange(private.shape[1]) < common.shape[1]
    return jnp.where(inside[None, :], share * padded + math.sqrt(1.0 - share * share) * private, private)


def blend_rows(common, private, share):
    padded = jnp.pad(common, ((0, private.shape[0] - common.shape[0]), (0, 0)))
    inside = jnp.arange(private.shape[0]) < common.shape[0]
    return jnp.where(inside[:, None], share * padded + math.sqrt(1.0 - share * share) * private, private)


def draw_img_feats(key, part):
    common = shared_normal(key, 101, (TOKENS, min(D_IMG, D_TXT)))
    top = 0.8
    key_base = key
    key = jax.random.fold_in(key, 11)
    private = jax.random.normal(jax.random.fold_in(key, 1), (TOKENS, D_IMG), jnp.float32)
    common = common + rising_part(key_base, top)
    blended = jnp.clip(blend_columns(common, private, feat_share), -clip_level, clip_level)
    blocks = TOKENS // TOK_DEV
    col_width = D_IMG // blocks
    pairing = jax.random.permutation(jax.random.fold_in(key, 3), blocks)
    partner = pairing[jnp.arange(TOKENS) // TOK_DEV]
    col_block = jnp.arange(D_IMG) // col_width
    boosted = jnp.where(partner[:, None] == col_block[None, :], spike_gain, 1.0)
    return (blended * boosted).astype(jnp.bfloat16)


def draw_txt_feats(key, part):
    common = shared_normal(key, 101, (TOKENS, min(D_IMG, D_TXT)))
    top = 0.8
    key_base = key
    key = jax.random.fold_in(key, 12)
    private = jax.random.normal(jax.random.fold_in(key, 1), (TOKENS, D_TXT), jnp.float32)
    common = common + rising_part(key_base, top)
    blended = jnp.clip(blend_columns(common, private, feat_share), -clip_level, clip_level)
    return blended.astype(jnp.bfloat16)


def draw_img_head(key, part):
    common = shared_normal(key, 202, (min(D_IMG, D_TXT), EMB))
    key = jax.random.fold_in(key, 13)
    private = jax.random.normal(jax.random.fold_in(key, 1), (D_IMG, EMB), jnp.float32)
    blended = jnp.clip(blend_rows(common, private, head_share), -clip_level, clip_level)
    return (blended * D_IMG ** (-0.5)).astype(jnp.bfloat16)


def draw_txt_head(key, part):
    common = shared_normal(key, 202, (min(D_IMG, D_TXT), EMB))
    key = jax.random.fold_in(key, 14)
    private = jax.random.normal(jax.random.fold_in(key, 1), (D_TXT, EMB), jnp.float32)
    blended = jnp.clip(blend_rows(common, private, head_share), -clip_level, clip_level)
    return (blended * D_TXT ** (-0.5)).astype(jnp.bfloat16)


def setup_inputs(seed: int = 0) -> dict:
    splits = jax.random.split(jax.random.key(seed), 7)
    return {
        "img_feats": draw_img_feats(jax.random.fold_in(splits[6], 71), 0),
        "txt_feats": draw_txt_feats(jax.random.fold_in(splits[6], 71), 0),
        "img_head": draw_img_head(jax.random.fold_in(splits[6], 71), 0),
        "txt_head": draw_txt_head(jax.random.fold_in(splits[6], 71), 0),
        "log_scale": jnp.clip(jax.random.uniform(splits[4], (1,), jnp.float32, 3.4, 4.0), 3.4, 4.0),
        "logit_bias": jnp.clip(jax.random.uniform(splits[5], (1,), jnp.float32, -4.0, -2.0), -4.0, -2.0),
    }


EPS = 1e-06

def normalized(feats, head):
    projected = jnp.dot(feats, head, preferred_element_type=jnp.float32)
    inv_norm = lax.rsqrt(lax.optimization_barrier(jnp.sum(projected * projected, axis=-1, keepdims=True)) + EPS)
    return (projected * inv_norm, inv_norm)

def reference(img_feats, txt_feats, img_head, txt_head, log_scale, logit_bias):
    img_unit, img_inv = normalized(img_feats, img_head)
    txt_unit, txt_inv = normalized(txt_feats, txt_head)
    img_low = img_unit.astype(jnp.bfloat16).reshape(N_DP, TOK_DEV, EMB).astype(jnp.float32)
    txt_low = txt_unit.astype(jnp.bfloat16).reshape(N_DP, TOK_DEV, EMB).astype(jnp.float32)
    temper = jnp.exp(log_scale[0])
    bias_v = logit_bias[0]
    identity = jnp.eye(TOK_DEV, dtype=jnp.float32)
    loss_sum = jnp.float32(0.0)
    cos_sum = jnp.float32(0.0)
    grad_sum = jnp.float32(0.0)
    img_dunit = jnp.zeros((N_DP, TOK_DEV, EMB), jnp.float32)
    txt_dunit = jnp.zeros((N_DP, TOK_DEV, EMB), jnp.float32)
    for offset in range(-HALF, HALF + 1):
        text_block = jnp.roll(txt_low, offset, axis=0)
        cosine = jnp.einsum('dik,djk->dij', img_low, text_block)
        logits = temper * cosine + bias_v
        target = identity * (1.0 if offset == 0 else 0.0)
        pair_sign = 2.0 * target - 1.0
        loss_sum = loss_sum - jnp.sum(jax.nn.log_sigmoid(pair_sign * logits))
        pair_grad = jax.nn.sigmoid(logits) - target
        cos_sum = cos_sum + jnp.sum(pair_grad * cosine)
        grad_sum = grad_sum + jnp.sum(pair_grad)
        weights = (temper * pair_grad).astype(jnp.bfloat16).astype(jnp.float32)
        img_dunit = img_dunit + jnp.einsum('dij,djk->dik', weights, text_block)
        txt_dunit = txt_dunit + jnp.roll(jnp.einsum('dij,dik->djk', weights, img_low), -offset, axis=0)
    img_dunit = img_dunit.reshape(TOKENS, EMB)
    txt_dunit = txt_dunit.reshape(TOKENS, EMB)
    text_grad = txt_inv * (txt_dunit - txt_unit * lax.optimization_barrier(jnp.sum(txt_unit * txt_dunit, axis=-1, keepdims=True)))
    img_dproj = img_inv * (img_dunit - img_unit * lax.optimization_barrier(jnp.sum(img_unit * img_dunit, axis=-1, keepdims=True)))
    img_dlow = img_dproj.astype(jnp.bfloat16)
    head_grad = jnp.dot(img_feats.T, img_dlow, preferred_element_type=jnp.float32) / TOK_DEV
    loss = loss_sum / PAIRS
    scalar_grads = jnp.stack([temper * cos_sum, grad_sum]) / PAIRS
    return (loss, scalar_grads, head_grad, text_grad)
```

```python
import jax
import jax.numpy as jnp
from jax import lax
from jax.experimental import pallas as pl
from jax.experimental.pallas import tpu as pltpu
from jax.sharding import PartitionSpec as P

EPS = 1e-06
B = 128
E = 1024
DI = 1536
DT = 4096
N = 256
PAIRS = 54525952
CH = 512

TXT = 0
IMG = 24
FEA = 48
DLO = 52
SIB = 56
PLN = 58
OWN = 74
IDS = 82


def kernel(
    ls_ref, lb_ref, imgf_ref, txtf_ref, imgh_ref, txth_ref,
    st_ref, hg_ref, tg_ref, tinv_ref,
    txtf, imgh, txth, feats, texts, images, unit_t, unit_i, acc_t, acc_i, inv_t, inv_i,
    dlow_t, dgat, stat, stats2, tails, part_sib, part_rcv, part, plane, owned, pieces,
    load_sem, send_sem, recv_sem,
):
    me = lax.axis_index("dp")
    core = lax.rem(me, 2)
    spot = lax.rem(me // 2, 16)
    z = me // 32
    x = lax.rem(spot, 4)
    row_first = me - 2 * x
    right_x = lax.rem(x + 1, 4)
    left_x = lax.rem(x + 3, 4)
    right = row_first + 2 * right_x
    left = row_first + 2 * left_x
    inner = (x == 1) | (x == 2)
    up = lax.rem(me + 8, N)
    down = lax.rem(me + N - 8, N)
    sib = me + 1 - 2 * core

    side = 1 - 2 * core

    def z_mate(off):
        return lax.rem(me + 32 * off + N, N)

    def quarter(off):
        return lax.rem(z + off + 8, 4)

    def plane_mate(off):
        return 32 * z + 2 * lax.rem(spot + off, 16) + core

    first_owner = 128 * core + 8 * spot
    my_row = me // 8
    src_core = my_row // 16
    src_spot = lax.rem(my_row, 16)

    def source(zz):
        return 32 * zz + 2 * src_spot + src_core

    barrier = pltpu.get_barrier_semaphore()

    def greet(dev):
        pl.semaphore_signal(barrier, inc=1, device_id={"dp": dev}, device_id_type=pl.DeviceIdType.MESH)

    for dev in [right, left, up, down, sib] + [z_mate(side), z_mate(2 * side), z_mate(-side)] + [plane_mate(o) for o in range(1, 16)]:
        greet(dev)
    for zz in range(8):
        @pl.when(source(zz) != me)
        def _():
            greet(source(zz))

    loads = {}

    def load(i, src, dst):
        loads[i] = pltpu.make_async_copy(src, dst, load_sem.at[i])
        loads[i].start()

    load(0, imgf_ref, feats.at[pl.ds(0, B)])
    load(1, txtf_ref, txtf)
    for j in range(DT // CH):
        load(2 + j, txth_ref.at[pl.ds(j * CH, CH)], txth.at[pl.ds(j * CH, CH)])
    for j in range(DI // CH):
        load(10 + j, imgh_ref.at[pl.ds(j * CH, CH)], imgh.at[pl.ds(j * CH, CH)])

    owner_is_me = (me >= first_owner) & (me < first_owner + 8)
    pl.semaphore_wait(barrier, 23 + 8 - owner_is_me.astype(jnp.int32))

    sent = []
    sent_if = []

    def copy(i, src, dst, dev):
        return pltpu.make_async_remote_copy(
            src_ref=src, dst_ref=dst, send_sem=send_sem.at[i], recv_sem=recv_sem.at[i],
            device_id={"dp": dev}, device_id_type=pl.DeviceIdType.MESH,
        )

    def send(i, src, dst, dev):
        c = copy(i, src, dst, dev)
        c.start()
        sent.append(c)

    def send_if(cond, i, src, dst, dev, landing=None):
        c = pltpu.make_async_remote_copy(
            src_ref=src, dst_ref=dst, send_sem=send_sem.at[i],
            recv_sem=recv_sem.at[i if landing is None else landing],
            device_id={"dp": dev}, device_id_type=pl.DeviceIdType.MESH,
        )

        @pl.when(cond)
        def _():
            c.start()

        sent_if.append((cond, c))

    def arrived(i, dst):
        copy(i, dst, dst, sib).wait_recv()

    def fea(n):
        return feats.at[pl.ds(n * B, B)]

    def in_row(at, q):
        return q - 4 * (at + q >= 4).astype(jnp.int32)

    def crossed(at, q):
        return q - 4 * (at + q < 4).astype(jnp.int32)

    def slot(ref, off, half=None):
        if half is None:
            return ref.at[2 * (3 + off) + core]
        return ref.at[2 * (3 + off) + core, pl.ds(half * (B // 2), B // 2)]

    def row_send(base, ref, half):
        send(base + 4 + (half or 0), slot(ref, 0, half), slot(ref, in_row(right_x, 3), half), right)
        send(base + (half or 0), slot(ref, 0, half), slot(ref, in_row(left_x, 1), half), left)

    def row_wait(base, ref, q, half):
        arrived(base + 2 * (q - 1) + (half or 0), slot(ref, in_row(x, q), half))

    def opposite_send(base, ref, half):
        at = lax.rem(x + side + 4, 4)
        send(
            base + 2 + (half or 0), slot(ref, in_row(x, 2 + side), half), slot(ref, in_row(at, 2), half),
            row_first + 2 * at,
        )

    def cross_send(base, ref, q, half):
        dev = jnp.where(x + q < 4, up, down)
        i = base + 6 + 2 * (q - 1) + (half or 0)
        src, dst = slot(ref, in_row(x, q), half), slot(ref, crossed(x, q), half)
        if q == 2:
            send_if(inner, i, src, dst, dev)
        else:
            send(i, src, dst, dev)

    def cross_wait(base, ref, q, half):
        arrived(base + 6 + 2 * (q - 1) + (half or 0), slot(ref, crossed(x, q), half))

    def cross_wait_rest(base, ref, q, half):
        @pl.when(x != (q + 1) // 2)
        def _():
            cross_wait(base, ref, q, half)

    def hand_on(base, ref, half):
        for at in (1, 2):
            @pl.when(x == at)
            def _():
                cross_wait(base, ref, 2 * at - 1, half)
        near = jnp.where(inner, x, 1)
        taken = crossed(near, 2 * near - 1)
        to = 3 * (near - 1)
        send_if(
            inner, base + 12 + (half or 0), slot(ref, taken, half), slot(ref, crossed(to, 2), half),
            row_first + 2 * to, base + 8 + (half or 0),
        )

    def sib_send(base, ref, n, off):
        send(base + 14 + n, slot(ref, off), slot(ref, off), sib)

    def sib_wait(base, ref, n, off):
        arrived(base + 14 + n, ref.at[2 * (3 + off) + 1 - core])

    def project(read, head, acc, first, count):
        acc[...] = jnp.zeros((B, E), jnp.float32)
        for j in range(count):
            loads[first + j].wait()
            acc[...] += jnp.dot(read(j), head[pl.ds(j * CH, CH), :], preferred_element_type=jnp.float32)

    def normalize(acc, unit, inv, ref):
        proj = acc[...]
        scale = lax.rsqrt(jnp.sum(proj * proj, axis=-1, keepdims=True) + EPS)
        value = proj * scale
        unit[...] = value
        inv[...] = jnp.broadcast_to(scale, (B, 128))
        ref[6 + core] = value.astype(jnp.bfloat16)

    loads[0].wait()
    send(FEA + 1, fea(0), fea(1), z_mate(-side))
    send(FEA + 3, fea(0), fea(3), z_mate(side))
    loads[1].wait()
    project(lambda j: txtf[:, pl.ds(j * CH, CH)], txth, acc_t, 2, DT // CH)
    normalize(acc_t, unit_t, inv_t, texts)
    for half in (0, 1):
        row_send(TXT, texts, half)
    sib_send(TXT, texts, 0, 0)
    project(lambda j: feats[pl.ds(0, B), pl.ds(j * CH, CH)], imgh, acc_i, 10, DI // CH)
    normalize(acc_i, unit_i, inv_i, images)
    sib_send(IMG, images, 0, 0)

    temper = jnp.exp(jnp.full((1, 2 * B), ls_ref[0], jnp.float32))
    bias = lb_ref[0]
    rows = lax.broadcasted_iota(jnp.int32, (B, 2 * B), 0)
    cols = lax.broadcasted_iota(jnp.int32, (B, 2 * B), 1)
    acc_i[...] = jnp.zeros((B, E), jnp.float32)
    acc_t[...] = jnp.zeros((B, E), jnp.float32)
    totals = [jnp.zeros((1, 2 * B), jnp.float32) for _ in range(3)]

    def pair(base, own, ref, n, acc, stats):
        off = 0 if n == 0 else in_row(x, n) if n < 4 else crossed(x, n - 3)
        sib_wait(base, ref, n, off)
        block = ref[pl.ds(2 * (3 + off), 2)].reshape(2 * B, E)
        cosine = lax.dot_general(
            own[6 + core], block, (((1,), (1,)), ((), ())), preferred_element_type=jnp.float32
        )
        logits = temper * cosine + bias
        small = jnp.exp(-jnp.abs(logits))
        grad = jnp.where(logits >= 0.0, 1.0, small) / (1.0 + small)
        if n == 0:
            hit = cols == rows + core * B
            grad = grad - jnp.where(hit, 1.0, 0.0)
        else:
            apart = 2 * off - core + (cols >= B).astype(jnp.int32)
            valid = (apart >= -6) & (apart <= 6)
            grad = jnp.where(valid, grad, 0.0)
        if stats:
            signed = jnp.where(hit, -logits, logits) if n == 0 else logits
            loss = jnp.maximum(signed, 0.0) + jnp.log1p(small)
            if n > 0:
                loss = jnp.where(valid, loss, 0.0)
            for k, term in enumerate((loss, grad * cosine, grad)):
                totals[k] = totals[k] + jnp.sum(term, axis=0, keepdims=True)
        weights = (temper * grad).astype(jnp.bfloat16)
        acc[...] += jnp.dot(weights, block, preferred_element_type=jnp.float32)

    def text_pair(n):
        pair(TXT, images, texts, n, acc_i, True)

    def image_pair(n):
        pair(IMG, texts, images, n, acc_t, False)

    text_pair(0)
    for half in (0, 1):
        for q in (1, 3):
            row_wait(TXT, texts, q, half)
            cross_send(TXT, texts, q, half)
        opposite_send(TXT, texts, half)
    for q in (1, 3):
        sib_send(TXT, texts, q, in_row(x, q))
    arrived(FEA + 1, fea(1))
    send(FEA + 2, fea(1), fea(2), z_mate(-side))
    text_pair(1)
    for half in (0, 1):
        row_wait(TXT, texts, 2, half)
        cross_send(TXT, texts, 2, half)
        hand_on(TXT, texts, half)
    sib_send(TXT, texts, 2, in_row(x, 2))
    text_pair(3)
    row_send(IMG, images, None)
    text_pair(2)
    for q in (1, 3):
        for half in (0, 1):
            cross_wait_rest(TXT, texts, q, half)
        sib_send(TXT, texts, 3 + q, crossed(x, q))
    text_pair(4)
    text_pair(6)
    for half in (0, 1):
        cross_wait(TXT, texts, 2, half)
    sib_send(TXT, texts, 5, crossed(x, 2))
    text_pair(5)

    stat[...] = jnp.zeros((8, 2 * B), jnp.float32)
    stat[0:1, 0:B] = totals[0][:, :B] + totals[0][:, B:]
    stat[0:1, B : 2 * B] = totals[1][:, :B] + totals[1][:, B:]
    stat[1:2, 0:B] = totals[2][:, :B] + totals[2][:, B:]
    send(SIB + 1, stat, stats2, sib)
    unit = unit_i[...]
    dunit = acc_i[...]
    dproj = inv_i[:, 0:1] * (dunit - unit * jnp.sum(unit * dunit, axis=-1, keepdims=True))
    for j in range(4):
        dlow_t[j] = dproj[:, j * 256 : (j + 1) * 256].T.astype(jnp.bfloat16)

    def window(n):
        return dgat.at[:, pl.ds(n * B, B)]

    for n, off in ((1, -side), (2, -2 * side), (3, side)):
        send(DLO + n, dlow_t.at[quarter(off)], window(n), z_mate(off))
    dgat[:, 0:B] = dlow_t[quarter(0)]
    for q in (1, 3):
        row_wait(IMG, images, q, None)
        cross_send(IMG, images, q, None)
    opposite_send(IMG, images, None)
    for q in (1, 3):
        sib_send(IMG, images, q, in_row(x, q))
    for n in (0, 1, 3):
        image_pair(n)

    for n in (1, 2, 3):
        arrived(DLO + n, window(n))
    arrived(FEA + 2, fea(2))
    arrived(FEA + 3, fea(3))

    def product(half, ref):
        for n in range(3):
            res = jnp.dot(
                dgat[...], feats[:, pl.ds(pl.multiple_of(half * 768 + n * 256, 256), 256)],
                preferred_element_type=jnp.float32,
            ).T
            ref[pl.ds(n * 256, 256), :] = res

    product(1 - core, part_sib)
    send(SIB, part_sib, part_rcv, sib)
    product(core, part)
    arrived(SIB, part_rcv)
    arrived(SIB + 1, stats2)
    both = stat[...] + stats2[...]
    for t in range(16):
        pieces[t, 0:48, :] = part[t * 48 : (t + 1) * 48, :] + part_rcv[t * 48 : (t + 1) * 48, :]
        pieces[t, 48:56, :] = both
    for o in range(1, 16):
        send(PLN + o, pieces.at[lax.rem(spot + o, 16)], plane.at[spot], plane_mate(o))
    plane[spot] = pieces[spot]

    row_wait(IMG, images, 2, None)
    cross_send(IMG, images, 2, None)
    sib_send(IMG, images, 2, in_row(x, 2))
    hand_on(IMG, images, None)
    for q in (1, 3):
        cross_wait_rest(IMG, images, q, None)
        sib_send(IMG, images, 3 + q, crossed(x, q))
    image_pair(2)

    for o in range(1, 16):
        arrived(PLN + o, plane.at[lax.rem(spot + 16 - o, 16)])
    total = jnp.sum(plane[...], axis=0)
    for j in range(8):
        tails[j, 0:6, :] = total[6 * j : 6 * j + 6, :]
        tails[j, 6:8, :] = total[48:50, :]
    for j in range(8):
        @pl.when(first_owner + j != me)
        def _():
            pltpu.make_async_remote_copy(
                src_ref=tails.at[j], dst_ref=owned.at[z],
                send_sem=send_sem.at[OWN + j], recv_sem=recv_sem.at[OWN + z],
                device_id={"dp": first_owner + j}, device_id_type=pl.DeviceIdType.MESH,
            ).start()

        @pl.when(first_owner + j == me)
        def _():
            owned[z] = tails[j]

    image_pair(4)
    image_pair(6)
    cross_wait(IMG, images, 2, None)
    sib_send(IMG, images, 5, crossed(x, 2))
    image_pair(5)
    unit = unit_t[...]
    dunit = acc_t[...]
    tg_ref[...] = dunit - unit * jnp.sum(unit * dunit, axis=-1, keepdims=True)
    tinv_ref[...] = inv_t[...]

    for zz in range(8):
        @pl.when(source(zz) != me)
        def _():
            arrived(OWN + zz, owned.at[zz])
    for n in range(4):
        hg_ref[:, n * 256 : (n + 1) * 256] = owned[n, 0:6, :] + owned[n + 4, 0:6, :]
    st_ref[...] = jnp.sum(owned[...], axis=0)
    for j in range(8):
        @pl.when(first_owner + j != me)
        def _():
            copy(OWN + j, tails.at[j], owned.at[z], first_owner + j).wait_send()
    for c in sent:
        c.wait_send()
    for cond, c in sent_if:
        @pl.when(cond)
        def _():
            c.wait_send()


def finish(ls_ref, st_ref, hgs_ref, tgs_ref, tinv_ref, loss_ref, sg_ref, hg_ref, tg_ref):
    temper = jnp.exp(jnp.full((1, B), ls_ref[0], jnp.float32))
    loss_ref[0] = jnp.sum(st_ref[6:7, 0:B]) / PAIRS
    sg_ref[0] = jnp.sum(st_ref[6:7, B : 2 * B] * temper) / PAIRS
    sg_ref[1] = jnp.sum(st_ref[7:8, 0:B]) / PAIRS
    hg_ref[...] = hgs_ref[...] * (1.0 / B)
    tg_ref[...] = tgs_ref[...] * tinv_ref[:, 0:1]


def shards(img_feats, txt_feats, img_head, txt_head, log_scale, logit_bias):
    f32, bf16 = jnp.float32, jnp.bfloat16
    smem = pl.BlockSpec(memory_space=pltpu.SMEM)
    vmem = pl.BlockSpec(memory_space=pltpu.VMEM)
    hbm = pl.BlockSpec(memory_space=pl.ANY)
    sums = pl.pallas_call(
        kernel,
        out_shape=(
            jax.ShapeDtypeStruct((8, 2 * B), f32),
            jax.ShapeDtypeStruct((6, E), f32),
            jax.ShapeDtypeStruct((B, E), f32),
            jax.ShapeDtypeStruct((B, 128), f32),
        ),
        in_specs=[smem] * 2 + [hbm] * 4,
        out_specs=(vmem,) * 4,
        scratch_shapes=[
            pltpu.VMEM((B, DT), bf16),
            pltpu.VMEM((DI, E), bf16),
            pltpu.VMEM((DT, E), bf16),
            pltpu.VMEM((4 * B, DI), bf16),
            pltpu.VMEM((14, B, E), bf16),
            pltpu.VMEM((14, B, E), bf16),
            pltpu.VMEM((B, E), f32),
            pltpu.VMEM((B, E), f32),
            pltpu.VMEM((B, E), f32),
            pltpu.VMEM((B, E), f32),
            pltpu.VMEM((B, 128), f32),
            pltpu.VMEM((B, 128), f32),
            pltpu.VMEM((4, 256, B), bf16),
            pltpu.VMEM((256, 4 * B), bf16),
            pltpu.VMEM((8, 256), f32),
            pltpu.VMEM((8, 256), f32),
            pltpu.VMEM((8, 8, 256), f32),
            pltpu.VMEM((768, 256), f32),
            pltpu.VMEM((768, 256), f32),
            pltpu.VMEM((768, 256), f32),
            pltpu.VMEM((16, 56, 256), f32),
            pltpu.VMEM((8, 8, 256), f32),
            pltpu.VMEM((16, 56, 256), f32),
            pltpu.SemaphoreType.DMA((16,)),
            pltpu.SemaphoreType.DMA((IDS,)),
            pltpu.SemaphoreType.DMA((IDS,)),
        ],
        compiler_params=pltpu.CompilerParams(
            collective_id=0, has_side_effects=True, vmem_limit_bytes=62 * 2**20
        ),
        cost_estimate=pl.CostEstimate(flops=5 * 10**9, bytes_accessed=14 * 10**6, transcendentals=10**6),
        name="contrastive",
    )(log_scale, logit_bias, img_feats, txt_feats, img_head, txt_head)
    loss, scalar_grads, head_grad, text_grad = pl.pallas_call(
        finish,
        out_shape=(
            jax.ShapeDtypeStruct((1,), f32),
            jax.ShapeDtypeStruct((2,), f32),
            jax.ShapeDtypeStruct((6, E), f32),
            jax.ShapeDtypeStruct((B, E), f32),
        ),
        in_specs=[smem] + [vmem] * 4,
        out_specs=(smem, smem, vmem, vmem),
        name="finish",
    )(log_scale, *sums)
    return loss.reshape(()), scalar_grads, head_grad, text_grad


def solution(mesh):
    in_specs = (P("dp", None), P("dp", None), P(), P(), P(), P())
    out_specs = (P(), P(), P("dp", None), P("dp", None))
    return jax.shard_map(shards, mesh=mesh, in_specs=in_specs, out_specs=out_specs, check_vma=False)
```

```python
import jax
import jax.numpy as jnp
from jax import lax
from jax.experimental import pallas as pl
from jax.experimental.pallas import tpu as pltpu
from jax.sharding import PartitionSpec as P

EPS = 1e-06
B = 128
E = 1024
DI = 1536
DT = 4096
N = 256
PAIRS = 54525952
CH = 512

TXT = 0
IMG = 24
FEA = 48
DLO = 52
SIB = 56
PLN = 60
OWN = 76
IDS = 84


def kernel(
    ls_ref, lb_ref, imgf_ref, txtf_ref, imgh_ref, txth_ref,
    st_ref, hg_ref, tg_ref, tinv_ref,
    txtf, imgh, txth, feats, texts, images, unit_t, unit_i, acc_t, acc_i, inv_t, inv_i,
    dlow_t, dgat, stat, stats2, tails, part_sib, part_rcv, part, plane, owned, pieces,
    load_sem, send_sem, recv_sem,
):
    me = lax.axis_index("dp")
    core = lax.rem(me, 2)
    spot = lax.rem(me // 2, 16)
    z = me // 32
    x = lax.rem(spot, 4)
    row_first = me - 2 * x
    right_x = lax.rem(x + 1, 4)
    left_x = lax.rem(x + 3, 4)
    right = row_first + 2 * right_x
    left = row_first + 2 * left_x
    inner = (x == 1) | (x == 2)
    up = lax.rem(me + 8, N)
    down = lax.rem(me + N - 8, N)
    sib = me + 1 - 2 * core

    side = 1 - 2 * core

    def z_mate(off):
        return lax.rem(me + 32 * off + N, N)

    def quarter(off):
        return lax.rem(z + off + 8, 4)

    def plane_mate(off):
        return 32 * z + 2 * lax.rem(spot + off, 16) + core

    first_owner = 128 * core + 8 * spot
    my_row = me // 8
    src_core = my_row // 16
    src_spot = lax.rem(my_row, 16)

    def source(zz):
        return 32 * zz + 2 * src_spot + src_core

    barrier = pltpu.get_barrier_semaphore()

    def greet(dev):
        pl.semaphore_signal(barrier, inc=1, device_id={"dp": dev}, device_id_type=pl.DeviceIdType.MESH)

    for dev in [right, left, up, down, sib] + [z_mate(side), z_mate(2 * side), z_mate(-side)] + [plane_mate(o) for o in range(1, 16)]:
        greet(dev)
    for zz in range(8):
        @pl.when(source(zz) != me)
        def _():
            greet(source(zz))

    loads = {}

    def load(i, src, dst):
        loads[i] = pltpu.make_async_copy(src, dst, load_sem.at[i])
        loads[i].start()

    load(0, imgf_ref, feats.at[pl.ds(0, B)])
    load(1, txtf_ref, txtf)
    for j in range(DT // CH):
        load(2 + j, txth_ref.at[pl.ds(j * CH, CH)], txth.at[pl.ds(j * CH, CH)])
    for j in range(DI // CH):
        load(10 + j, imgh_ref.at[pl.ds(j * CH, CH)], imgh.at[pl.ds(j * CH, CH)])

    owner_is_me = (me >= first_owner) & (me < first_owner + 8)

    sent = []
    sent_if = []

    def copy(i, src, dst, dev):
        return pltpu.make_async_remote_copy(
            src_ref=src, dst_ref=dst, send_sem=send_sem.at[i], recv_sem=recv_sem.at[i],
            device_id={"dp": dev}, device_id_type=pl.DeviceIdType.MESH,
        )

    def send(i, src, dst, dev):
        c = copy(i, src, dst, dev)
        c.start()
        sent.append(c)

    def send_if(cond, i, src, dst, dev, landing=None):
        c = pltpu.make_async_remote_copy(
            src_ref=src, dst_ref=dst, send_sem=send_sem.at[i],
            recv_sem=recv_sem.at[i if landing is None else landing],
            device_id={"dp": dev}, device_id_type=pl.DeviceIdType.MESH,
        )

        @pl.when(cond)
        def _():
            c.start()

        sent_if.append((cond, c))

    def arrived(i, dst):
        copy(i, dst, dst, sib).wait_recv()

    def fea(n):
        return feats.at[pl.ds(n * B, B)]

    def in_row(at, q):
        return q - 4 * (at + q >= 4).astype(jnp.int32)

    def crossed(at, q):
        return q - 4 * (at + q < 4).astype(jnp.int32)

    def slot(ref, off, half=None):
        if half is None:
            return ref.at[2 * (3 + off) + core]
        return ref.at[2 * (3 + off) + core, pl.ds(half * (B // 2), B // 2)]

    def row_send(base, ref, half):
        send(base + 4 + (half or 0), slot(ref, 0, half), slot(ref, in_row(right_x, 3), half), right)
        send(base + (half or 0), slot(ref, 0, half), slot(ref, in_row(left_x, 1), half), left)

    def row_wait(base, ref, q, half):
        arrived(base + 2 * (q - 1) + (half or 0), slot(ref, in_row(x, q), half))

    def opposite_send(base, ref, half):
        at = lax.rem(x + side + 4, 4)
        send(
            base + 2 + (half or 0), slot(ref, in_row(x, 2 + side), half), slot(ref, in_row(at, 2), half),
            row_first + 2 * at,
        )

    def cross_send(base, ref, q, half):
        dev = jnp.where(x + q < 4, up, down)
        i = base + 6 + 2 * (q - 1) + (half or 0)
        src, dst = slot(ref, in_row(x, q), half), slot(ref, crossed(x, q), half)
        if q == 2:
            send_if(inner, i, src, dst, dev)
        else:
            send(i, src, dst, dev)

    def cross_wait(base, ref, q, half):
        arrived(base + 6 + 2 * (q - 1) + (half or 0), slot(ref, crossed(x, q), half))

    def cross_wait_rest(base, ref, q, half):
        @pl.when(x != (q + 1) // 2)
        def _():
            cross_wait(base, ref, q, half)

    def hand_on(base, ref, half):
        for at in (1, 2):
            @pl.when(x == at)
            def _():
                cross_wait(base, ref, 2 * at - 1, half)
        near = jnp.where(inner, x, 1)
        taken = crossed(near, 2 * near - 1)
        to = 3 * (near - 1)
        send_if(
            inner, base + 12 + (half or 0), slot(ref, taken, half), slot(ref, crossed(to, 2), half),
            row_first + 2 * to, base + 8 + (half or 0),
        )

    def sib_send(base, ref, n, off):
        send(base + 14 + n, slot(ref, off), slot(ref, off), sib)

    def sib_wait(base, ref, n, off):
        arrived(base + 14 + n, ref.at[2 * (3 + off) + 1 - core])

    def project(read, head, acc, first, count):
        acc[...] = jnp.zeros((B, E), jnp.float32)
        for j in range(count):
            loads[first + j].wait()
            acc[...] += jnp.dot(read(j), head[pl.ds(j * CH, CH), :], preferred_element_type=jnp.float32)

    def normalize(acc, unit, inv, ref):
        proj = acc[...]
        scale = lax.rsqrt(jnp.sum(proj * proj, axis=-1, keepdims=True) + EPS)
        value = proj * scale
        unit[...] = value
        inv[...] = jnp.broadcast_to(scale, (B, 128))
        ref[6 + core] = value.astype(jnp.bfloat16)

    loads[1].wait()
    project(lambda j: txtf[:, pl.ds(j * CH, CH)], txth, acc_t, 2, DT // CH)
    normalize(acc_t, unit_t, inv_t, texts)
    pl.semaphore_wait(barrier, 23 + 8 - owner_is_me.astype(jnp.int32))
    for half in (0, 1):
        row_send(TXT, texts, half)
    sib_send(TXT, texts, 0, 0)
    loads[0].wait()
    send(FEA + 1, fea(0), fea(1), z_mate(-side))
    send(FEA + 3, fea(0), fea(3), z_mate(side))
    project(lambda j: feats[pl.ds(0, B), pl.ds(j * CH, CH)], imgh, acc_i, 10, DI // CH)
    normalize(acc_i, unit_i, inv_i, images)
    sib_send(IMG, images, 0, 0)

    temper = jnp.exp(jnp.full((1, 2 * B), ls_ref[0], jnp.float32))
    bias = lb_ref[0]
    rows = lax.broadcasted_iota(jnp.int32, (B, 2 * B), 0)
    cols = lax.broadcasted_iota(jnp.int32, (B, 2 * B), 1)
    acc_i[...] = jnp.zeros((B, E), jnp.float32)
    acc_t[...] = jnp.zeros((B, E), jnp.float32)
    totals = [jnp.zeros((1, 2 * B), jnp.float32) for _ in range(3)]

    def pairs(base, own, ref, numbers, acc, stats):
        offs = [0 if n == 0 else in_row(x, n) if n < 4 else crossed(x, n - 3) for n in numbers]
        for n, off in zip(numbers, offs):
            sib_wait(base, ref, n, off)
        added = None
        for n, off in zip(numbers, offs):
            block = ref[pl.ds(2 * (3 + off), 2)].reshape(2 * B, E)
            cosine = lax.dot_general(
                own[6 + core], block, (((1,), (1,)), ((), ())), preferred_element_type=jnp.float32
            )
            logits = temper * cosine + bias
            small = jnp.exp(-jnp.abs(logits))
            grad = jnp.where(logits >= 0.0, 1.0, small) / (1.0 + small)
            if n == 0:
                hit = cols == rows + core * B
                grad = grad - jnp.where(hit, 1.0, 0.0)
            else:
                apart = 2 * off - core + (cols >= B).astype(jnp.int32)
                valid = (apart >= -6) & (apart <= 6)
                grad = jnp.where(valid, grad, 0.0)
            if stats:
                signed = jnp.where(hit, -logits, logits) if n == 0 else logits
                loss = jnp.maximum(signed, 0.0) + jnp.log1p(small)
                if n > 0:
                    loss = jnp.where(valid, loss, 0.0)
                for k, term in enumerate((loss, grad * cosine, grad)):
                    totals[k] = totals[k] + jnp.sum(term, axis=0, keepdims=True)
            weights = (temper * grad).astype(jnp.bfloat16)
            term = jnp.dot(weights, block, preferred_element_type=jnp.float32)
            added = term if added is None else added + term
        acc[...] += added

    def text_pairs(*numbers):
        pairs(TXT, images, texts, numbers, acc_i, True)

    def image_pairs(*numbers):
        pairs(IMG, texts, images, numbers, acc_t, False)

    text_pairs(0)
    for half in (0, 1):
        for q in (1, 3):
            row_wait(TXT, texts, q, half)
            cross_send(TXT, texts, q, half)
        opposite_send(TXT, texts, half)
    for q in (1, 3):
        sib_send(TXT, texts, q, in_row(x, q))
    for half in (0, 1):
        row_wait(TXT, texts, 2, half)
        cross_send(TXT, texts, 2, half)
        hand_on(TXT, texts, half)
    sib_send(TXT, texts, 2, in_row(x, 2))
    arrived(FEA + 1, fea(1))
    send(FEA + 2, fea(1), fea(2), z_mate(-side))
    text_pairs(1, 3)
    row_send(IMG, images, None)
    text_pairs(2)
    for q in (1, 3):
        for half in (0, 1):
            cross_wait_rest(TXT, texts, q, half)
        sib_send(TXT, texts, 3 + q, crossed(x, q))
    text_pairs(4, 6)
    for half in (0, 1):
        cross_wait(TXT, texts, 2, half)
    sib_send(TXT, texts, 5, crossed(x, 2))
    text_pairs(5)

    stat[...] = jnp.zeros((8, 2 * B), jnp.float32)
    stat[0:1, 0:B] = totals[0][:, :B] + totals[0][:, B:]
    stat[0:1, B : 2 * B] = totals[1][:, :B] + totals[1][:, B:]
    stat[1:2, 0:B] = totals[2][:, :B] + totals[2][:, B:]
    send(SIB + 2, stat, stats2, sib)
    unit = unit_i[...]
    dunit = acc_i[...]
    dproj = inv_i[:, 0:1] * (dunit - unit * jnp.sum(unit * dunit, axis=-1, keepdims=True))
    for j in range(4):
        dlow_t[j] = dproj[:, j * 256 : (j + 1) * 256].T.astype(jnp.bfloat16)

    def window(n):
        return dgat.at[:, pl.ds(n * B, B)]

    for n, off in ((1, -side), (2, -2 * side), (3, side)):
        send(DLO + n, dlow_t.at[quarter(off)], window(n), z_mate(off))
    dgat[:, 0:B] = dlow_t[quarter(0)]
    for q in (1, 3):
        row_wait(IMG, images, q, None)
        cross_send(IMG, images, q, None)
    opposite_send(IMG, images, None)
    for q in (1, 3):
        sib_send(IMG, images, q, in_row(x, q))
    image_pairs(0)
    image_pairs(1, 3)

    for n in (1, 2, 3):
        arrived(DLO + n, window(n))
    arrived(FEA + 2, fea(2))
    arrived(FEA + 3, fea(3))

    def part_rows(ref, n):
        return ref.at[pl.ds(pl.multiple_of(n * 384, 384), 384)]

    def product(half, n, ref):
        columns = pl.ds(pl.multiple_of(half * 768 + n * 384, 128), 384)
        part_rows(ref, n)[...] = jnp.dot(
            dgat[...], feats[:, columns], preferred_element_type=jnp.float32
        ).T

    for j, n in enumerate((1 - core, core)):
        product(1 - core, n, part_sib)
        send(SIB + j, part_rows(part_sib, n), part_rows(part_rcv, n), sib)
    for n in (core, 1 - core):
        product(core, n, part)
    arrived(SIB + 2, stats2)
    both = stat[...] + stats2[...]
    for j, n in enumerate((core, 1 - core)):
        arrived(SIB + j, part_rows(part_rcv, n))
        for i in range(8):
            span = pl.ds(pl.multiple_of(n * 384 + i * 48, 16), 48)
            pieces[8 * n + i, 0:48, :] = part[span, :] + part_rcv[span, :]
            pieces[8 * n + i, 48:56, :] = both
        for i in range(8):
            to = 8 * n + lax.rem(spot + i, 8)
            send_if(
                to != spot, PLN + lax.rem(to - spot + 16, 16), pieces.at[to], plane.at[spot],
                32 * z + 2 * to + core,
            )
    plane[spot] = pieces[spot]

    row_wait(IMG, images, 2, None)
    cross_send(IMG, images, 2, None)
    sib_send(IMG, images, 2, in_row(x, 2))
    hand_on(IMG, images, None)
    for q in (1, 3):
        cross_wait_rest(IMG, images, q, None)
        sib_send(IMG, images, 3 + q, crossed(x, q))
    image_pairs(2)
    image_pairs(4, 6)

    for o in range(1, 16):
        arrived(PLN + o, plane.at[lax.rem(spot + 16 - o, 16)])
    total = jnp.sum(plane[...], axis=0)
    for j in range(8):
        tails[j, 0:6, :] = total[6 * j : 6 * j + 6, :]
        tails[j, 6:8, :] = total[48:50, :]
    for j in range(8):
        @pl.when(first_owner + j != me)
        def _():
            pltpu.make_async_remote_copy(
                src_ref=tails.at[j], dst_ref=owned.at[z],
                send_sem=send_sem.at[OWN + j], recv_sem=recv_sem.at[OWN + z],
                device_id={"dp": first_owner + j}, device_id_type=pl.DeviceIdType.MESH,
            ).start()

        @pl.when(first_owner + j == me)
        def _():
            owned[z] = tails[j]

    cross_wait(IMG, images, 2, None)
    sib_send(IMG, images, 5, crossed(x, 2))
    image_pairs(5)
    unit = unit_t[...]
    dunit = acc_t[...]
    tg_ref[...] = dunit - unit * jnp.sum(unit * dunit, axis=-1, keepdims=True)
    tinv_ref[...] = inv_t[...]

    for zz in range(8):
        @pl.when(source(zz) != me)
        def _():
            arrived(OWN + zz, owned.at[zz])
    for n in range(4):
        hg_ref[:, n * 256 : (n + 1) * 256] = owned[n, 0:6, :] + owned[n + 4, 0:6, :]
    st_ref[...] = jnp.sum(owned[...], axis=0)
    for j in range(8):
        @pl.when(first_owner + j != me)
        def _():
            copy(OWN + j, tails.at[j], owned.at[z], first_owner + j).wait_send()
    for c in sent:
        c.wait_send()
    for cond, c in sent_if:
        @pl.when(cond)
        def _():
            c.wait_send()


def finish(ls_ref, st_ref, hgs_ref, tgs_ref, tinv_ref, loss_ref, sg_ref, hg_ref, tg_ref):
    temper = jnp.exp(jnp.full((1, B), ls_ref[0], jnp.float32))
    loss_ref[0] = jnp.sum(st_ref[6:7, 0:B]) / PAIRS
    sg_ref[0] = jnp.sum(st_ref[6:7, B : 2 * B] * temper) / PAIRS
    sg_ref[1] = jnp.sum(st_ref[7:8, 0:B]) / PAIRS
    hg_ref[...] = hgs_ref[...] * (1.0 / B)
    tg_ref[...] = tgs_ref[...] * tinv_ref[:, 0:1]


def shards(img_feats, txt_feats, img_head, txt_head, log_scale, logit_bias):
    f32, bf16 = jnp.float32, jnp.bfloat16
    smem = pl.BlockSpec(memory_space=pltpu.SMEM)
    vmem = pl.BlockSpec(memory_space=pltpu.VMEM)
    hbm = pl.BlockSpec(memory_space=pl.ANY)
    sums = pl.pallas_call(
        kernel,
        out_shape=(
            jax.ShapeDtypeStruct((8, 2 * B), f32),
            jax.ShapeDtypeStruct((6, E), f32),
            jax.ShapeDtypeStruct((B, E), f32),
            jax.ShapeDtypeStruct((B, 128), f32),
        ),
        in_specs=[smem] * 2 + [hbm] * 4,
        out_specs=(vmem,) * 4,
        scratch_shapes=[
            pltpu.VMEM((B, DT), bf16),
            pltpu.VMEM((DI, E), bf16),
            pltpu.VMEM((DT, E), bf16),
            pltpu.VMEM((4 * B, DI), bf16),
            pltpu.VMEM((14, B, E), bf16),
            pltpu.VMEM((14, B, E), bf16),
            pltpu.VMEM((B, E), f32),
            pltpu.VMEM((B, E), f32),
            pltpu.VMEM((B, E), f32),
            pltpu.VMEM((B, E), f32),
            pltpu.VMEM((B, 128), f32),
            pltpu.VMEM((B, 128), f32),
            pltpu.VMEM((4, 256, B), bf16),
            pltpu.VMEM((256, 4 * B), bf16),
            pltpu.VMEM((8, 256), f32),
            pltpu.VMEM((8, 256), f32),
            pltpu.VMEM((8, 8, 256), f32),
            pltpu.VMEM((768, 256), f32),
            pltpu.VMEM((768, 256), f32),
            pltpu.VMEM((768, 256), f32),
            pltpu.VMEM((16, 56, 256), f32),
            pltpu.VMEM((8, 8, 256), f32),
            pltpu.VMEM((16, 56, 256), f32),
            pltpu.SemaphoreType.DMA((16,)),
            pltpu.SemaphoreType.DMA((IDS,)),
            pltpu.SemaphoreType.DMA((IDS,)),
        ],
        compiler_params=pltpu.CompilerParams(
            collective_id=0, has_side_effects=True, vmem_limit_bytes=62 * 2**20
        ),
        cost_estimate=pl.CostEstimate(flops=5 * 10**9, bytes_accessed=14 * 10**6, transcendentals=10**6),
        name="contrastive",
    )(log_scale, logit_bias, img_feats, txt_feats, img_head, txt_head)
    loss, scalar_grads, head_grad, text_grad = pl.pallas_call(
        finish,
        out_shape=(
            jax.ShapeDtypeStruct((1,), f32),
            jax.ShapeDtypeStruct((2,), f32),
            jax.ShapeDtypeStruct((6, E), f32),
            jax.ShapeDtypeStruct((B, E), f32),
        ),
        in_specs=[smem] + [vmem] * 4,
        out_specs=(smem, smem, vmem, vmem),
        name="finish",
    )(log_scale, *sums)
    return loss.reshape(()), scalar_grads, head_grad, text_grad


def solution(mesh):
    in_specs = (P("dp", None), P("dp", None), P(), P(), P(), P())
    out_specs = (P(), P(), P("dp", None), P("dp", None))
    return jax.shard_map(shards, mesh=mesh, in_specs=in_specs, out_specs=out_specs, check_vma=False)
```

```python
import jax
import jax.numpy as jnp
from jax import lax
from jax.experimental import pallas as pl
from jax.experimental.pallas import tpu as pltpu
from jax.sharding import PartitionSpec as P

EPS = 1e-06
B = 128
E = 1024
DI = 1536
DT = 4096
N = 256
PAIRS = 54525952
CH = 512

TXT = 0
IMG = 24
FEA = 48
DLO = 52
SIB = 56
PLN = 60
OWN = 76
IDS = 84


def kernel(
    ls_ref, lb_ref, imgf_ref, txtf_ref, imgh_ref, txth_ref,
    st_ref, hg_ref, tg_ref, tinv_ref,
    txtf, imgh, txth, feats, texts, images, unit_t, unit_i, acc_t, acc_i, inv_t, inv_i,
    dlow_t, dgat, stat, stats2, tails, part_sib, part_rcv, part, plane, owned, pieces,
    load_sem, send_sem, recv_sem,
):
    me = lax.axis_index("dp")
    core = lax.rem(me, 2)
    spot = lax.rem(me // 2, 16)
    z = me // 32
    x = lax.rem(spot, 4)
    row_first = me - 2 * x
    right_x = lax.rem(x + 1, 4)
    left_x = lax.rem(x + 3, 4)
    right = row_first + 2 * right_x
    left = row_first + 2 * left_x
    inner = (x == 1) | (x == 2)
    up = lax.rem(me + 8, N)
    down = lax.rem(me + N - 8, N)
    sib = me + 1 - 2 * core

    side = 1 - 2 * core

    def z_mate(off):
        return lax.rem(me + 32 * off + N, N)

    def quarter(off):
        return lax.rem(z + off + 8, 4)

    def plane_mate(off):
        return 32 * z + 2 * lax.rem(spot + off, 16) + core

    first_owner = 128 * core + 8 * spot
    my_row = me // 8
    src_core = my_row // 16
    src_spot = lax.rem(my_row, 16)

    def source(zz):
        return 32 * zz + 2 * src_spot + src_core

    barrier = pltpu.get_barrier_semaphore()

    def greet(dev):
        pl.semaphore_signal(barrier, inc=1, device_id={"dp": dev}, device_id_type=pl.DeviceIdType.MESH)

    for dev in [right, left, up, down, sib] + [z_mate(side), z_mate(2 * side), z_mate(-side)] + [plane_mate(o) for o in range(1, 16)]:
        greet(dev)
    for zz in range(8):
        @pl.when(source(zz) != me)
        def _():
            greet(source(zz))

    loads = {}

    def load(i, src, dst):
        loads[i] = pltpu.make_async_copy(src, dst, load_sem.at[i])
        loads[i].start()

    load(0, imgf_ref, feats.at[pl.ds(0, B)])
    load(1, txtf_ref, txtf)
    for j in range(DT // CH):
        load(2 + j, txth_ref.at[pl.ds(j * CH, CH)], txth.at[pl.ds(j * CH, CH)])
    for j in range(DI // CH):
        load(10 + j, imgh_ref.at[pl.ds(j * CH, CH)], imgh.at[pl.ds(j * CH, CH)])

    owner_is_me = (me >= first_owner) & (me < first_owner + 8)

    sent = []
    sent_if = []

    def copy(i, src, dst, dev):
        return pltpu.make_async_remote_copy(
            src_ref=src, dst_ref=dst, send_sem=send_sem.at[i], recv_sem=recv_sem.at[i],
            device_id={"dp": dev}, device_id_type=pl.DeviceIdType.MESH,
        )

    def send(i, src, dst, dev):
        c = copy(i, src, dst, dev)
        c.start()
        sent.append(c)

    def send_if(cond, i, src, dst, dev, landing=None):
        c = pltpu.make_async_remote_copy(
            src_ref=src, dst_ref=dst, send_sem=send_sem.at[i],
            recv_sem=recv_sem.at[i if landing is None else landing],
            device_id={"dp": dev}, device_id_type=pl.DeviceIdType.MESH,
        )

        @pl.when(cond)
        def _():
            c.start()

        sent_if.append((cond, c))

    def drain(always, perhaps):
        for c in always:
            c.wait_send()
        for cond, c in perhaps:
            @pl.when(cond)
            def _():
                c.wait_send()

    def arrived(i, dst):
        copy(i, dst, dst, sib).wait_recv()

    def fea(n):
        return feats.at[pl.ds(n * B, B)]

    def in_row(at, q):
        return q - 4 * (at + q >= 4).astype(jnp.int32)

    def crossed(at, q):
        return q - 4 * (at + q < 4).astype(jnp.int32)

    def slot(ref, off, half=None):
        if half is None:
            return ref.at[2 * (3 + off) + core]
        return ref.at[2 * (3 + off) + core, pl.ds(half * (B // 2), B // 2)]

    def row_send(base, ref, half):
        send(base + 4 + (half or 0), slot(ref, 0, half), slot(ref, in_row(right_x, 3), half), right)
        send(base + (half or 0), slot(ref, 0, half), slot(ref, in_row(left_x, 1), half), left)

    def row_wait(base, ref, q, half):
        arrived(base + 2 * (q - 1) + (half or 0), slot(ref, in_row(x, q), half))

    def opposite_send(base, ref, half):
        at = lax.rem(x + side + 4, 4)
        send(
            base + 2 + (half or 0), slot(ref, in_row(x, 2 + side), half), slot(ref, in_row(at, 2), half),
            row_first + 2 * at,
        )

    def cross_send(base, ref, q, half):
        dev = jnp.where(x + q < 4, up, down)
        i = base + 6 + 2 * (q - 1) + (half or 0)
        src, dst = slot(ref, in_row(x, q), half), slot(ref, crossed(x, q), half)
        if q == 2:
            send_if(inner, i, src, dst, dev)
        else:
            send(i, src, dst, dev)

    def cross_wait(base, ref, q, half):
        arrived(base + 6 + 2 * (q - 1) + (half or 0), slot(ref, crossed(x, q), half))

    def cross_wait_rest(base, ref, q, half):
        @pl.when(x != (q + 1) // 2)
        def _():
            cross_wait(base, ref, q, half)

    def hand_on(base, ref, half):
        for at in (1, 2):
            @pl.when(x == at)
            def _():
                cross_wait(base, ref, 2 * at - 1, half)
        near = jnp.where(inner, x, 1)
        taken = crossed(near, 2 * near - 1)
        to = 3 * (near - 1)
        send_if(
            inner, base + 12 + (half or 0), slot(ref, taken, half), slot(ref, crossed(to, 2), half),
            row_first + 2 * to, base + 8 + (half or 0),
        )

    def sib_send(base, ref, n, off):
        send(base + 14 + n, slot(ref, off), slot(ref, off), sib)

    def sib_wait(base, ref, n, off):
        arrived(base + 14 + n, ref.at[2 * (3 + off) + 1 - core])

    def project(read, head, acc, first, count):
        acc[...] = jnp.zeros((B, E), jnp.float32)
        for j in range(count):
            loads[first + j].wait()
            acc[...] += jnp.dot(read(j), head[pl.ds(j * CH, CH), :], preferred_element_type=jnp.float32)

    def normalize(acc, unit, inv, ref):
        proj = acc[...]
        scale = lax.rsqrt(jnp.sum(proj * proj, axis=-1, keepdims=True) + EPS)
        value = proj * scale
        unit[...] = value
        inv[...] = jnp.broadcast_to(scale, (B, 128))
        ref[6 + core] = value.astype(jnp.bfloat16)

    loads[1].wait()
    project(lambda j: txtf[:, pl.ds(j * CH, CH)], txth, acc_t, 2, DT // CH)
    normalize(acc_t, unit_t, inv_t, texts)
    pl.semaphore_wait(barrier, 23 + 8 - owner_is_me.astype(jnp.int32))
    for half in (0, 1):
        row_send(TXT, texts, half)
    sib_send(TXT, texts, 0, 0)
    loads[0].wait()
    send(FEA + 1, fea(0), fea(1), z_mate(-side))
    send(FEA + 3, fea(0), fea(3), z_mate(side))
    project(lambda j: feats[pl.ds(0, B), pl.ds(j * CH, CH)], imgh, acc_i, 10, DI // CH)
    normalize(acc_i, unit_i, inv_i, images)
    sib_send(IMG, images, 0, 0)

    temper = jnp.exp(jnp.full((1, 2 * B), ls_ref[0], jnp.float32))
    bias = lb_ref[0]
    rows = lax.broadcasted_iota(jnp.int32, (B, 2 * B), 0)
    cols = lax.broadcasted_iota(jnp.int32, (B, 2 * B), 1)
    acc_i[...] = jnp.zeros((B, E), jnp.float32)
    acc_t[...] = jnp.zeros((B, E), jnp.float32)
    totals = [jnp.zeros((1, 2 * B), jnp.float32) for _ in range(3)]

    def pairs(base, own, ref, numbers, acc, stats):
        offs = [0 if n == 0 else in_row(x, n) if n < 4 else crossed(x, n - 3) for n in numbers]
        for n, off in zip(numbers, offs):
            sib_wait(base, ref, n, off)
        added = None
        for n, off in zip(numbers, offs):
            block = ref[pl.ds(2 * (3 + off), 2)].reshape(2 * B, E)
            cosine = lax.dot_general(
                own[6 + core], block, (((1,), (1,)), ((), ())), preferred_element_type=jnp.float32
            )
            logits = temper * cosine + bias
            small = jnp.exp(-jnp.abs(logits))
            grad = jnp.where(logits >= 0.0, 1.0, small) / (1.0 + small)
            if n == 0:
                hit = cols == rows + core * B
                grad = grad - jnp.where(hit, 1.0, 0.0)
            else:
                apart = 2 * off - core + (cols >= B).astype(jnp.int32)
                valid = (apart >= -6) & (apart <= 6)
                grad = jnp.where(valid, grad, 0.0)
            if stats:
                signed = jnp.where(hit, -logits, logits) if n == 0 else logits
                loss = jnp.maximum(signed, 0.0) + jnp.log1p(small)
                if n > 0:
                    loss = jnp.where(valid, loss, 0.0)
                for k, term in enumerate((loss, grad * cosine, grad)):
                    totals[k] = totals[k] + jnp.sum(term, axis=0, keepdims=True)
            weights = (temper * grad).astype(jnp.bfloat16)
            term = jnp.dot(weights, block, preferred_element_type=jnp.float32)
            added = term if added is None else added + term
        acc[...] += added

    def text_pairs(*numbers):
        pairs(TXT, images, texts, numbers, acc_i, True)

    def image_pairs(*numbers):
        pairs(IMG, texts, images, numbers, acc_t, False)

    text_pairs(0)
    for half in (0, 1):
        for q in (1, 3):
            row_wait(TXT, texts, q, half)
            cross_send(TXT, texts, q, half)
        opposite_send(TXT, texts, half)
    for q in (1, 3):
        sib_send(TXT, texts, q, in_row(x, q))
    for half in (0, 1):
        row_wait(TXT, texts, 2, half)
        cross_send(TXT, texts, 2, half)
        hand_on(TXT, texts, half)
    sib_send(TXT, texts, 2, in_row(x, 2))
    arrived(FEA + 1, fea(1))
    send(FEA + 2, fea(1), fea(2), z_mate(-side))
    for half in (0, 1):
        row_send(IMG, images, half)
    text_pairs(1, 3)
    text_pairs(2)
    for q in (1, 3):
        for half in (0, 1):
            cross_wait_rest(TXT, texts, q, half)
        sib_send(TXT, texts, 3 + q, crossed(x, q))

    def image_forward(half):
        for q in (1, 3):
            row_wait(IMG, images, q, half)
            cross_send(IMG, images, q, half)
        opposite_send(IMG, images, half)

    image_forward(0)
    text_pairs(4, 6)
    for half in (0, 1):
        cross_wait(TXT, texts, 2, half)
    sib_send(TXT, texts, 5, crossed(x, 2))
    text_pairs(5)

    stat[...] = jnp.zeros((8, 2 * B), jnp.float32)
    stat[0:1, 0:B] = totals[0][:, :B] + totals[0][:, B:]
    stat[0:1, B : 2 * B] = totals[1][:, :B] + totals[1][:, B:]
    stat[1:2, 0:B] = totals[2][:, :B] + totals[2][:, B:]
    send(SIB + 2, stat, stats2, sib)
    unit = unit_i[...]
    dunit = acc_i[...]
    dproj = inv_i[:, 0:1] * (dunit - unit * jnp.sum(unit * dunit, axis=-1, keepdims=True))
    for j in range(4):
        dlow_t[j] = dproj[:, j * 256 : (j + 1) * 256].T.astype(jnp.bfloat16)

    def window(n):
        return dgat.at[:, pl.ds(n * B, B)]

    for n, off in ((1, -side), (2, -2 * side), (3, side)):
        send(DLO + n, dlow_t.at[quarter(off)], window(n), z_mate(off))
    dgat[:, 0:B] = dlow_t[quarter(0)]
    image_forward(1)
    for q in (1, 3):
        sib_send(IMG, images, q, in_row(x, q))
    image_pairs(0)
    image_pairs(1, 3)
    for half in (0, 1):
        row_wait(IMG, images, 2, half)
        cross_send(IMG, images, 2, half)
    sib_send(IMG, images, 2, in_row(x, 2))

    for n in (1, 2, 3):
        arrived(DLO + n, window(n))
    arrived(FEA + 2, fea(2))
    arrived(FEA + 3, fea(3))

    def part_rows(ref, n):
        return ref.at[pl.ds(pl.multiple_of(n * 384, 384), 384)]

    def product(half, n, ref):
        columns = pl.ds(pl.multiple_of(half * 768 + n * 384, 128), 384)
        part_rows(ref, n)[...] = jnp.dot(
            dgat[...], feats[:, columns], preferred_element_type=jnp.float32
        ).T

    for j, n in enumerate((1 - core, core)):
        product(1 - core, n, part_sib)
        send(SIB + j, part_rows(part_sib, n), part_rows(part_rcv, n), sib)
    for n in (core, 1 - core):
        product(core, n, part)
    early, early_if = list(sent), list(sent_if)
    sent.clear()
    sent_if.clear()
    arrived(SIB + 2, stats2)
    both = stat[...] + stats2[...]
    for j, n in enumerate((core, 1 - core)):
        arrived(SIB + j, part_rows(part_rcv, n))
        for i in range(8):
            span = pl.ds(pl.multiple_of(n * 384 + i * 48, 16), 48)
            pieces[8 * n + i, 0:48, :] = part[span, :] + part_rcv[span, :]
            pieces[8 * n + i, 48:56, :] = both
        for i in range(8):
            to = 8 * n + lax.rem(spot + i, 8)
            send_if(
                to != spot, PLN + lax.rem(to - spot + 16, 16), pieces.at[to], plane.at[spot],
                32 * z + 2 * to + core,
            )
    plane[spot] = pieces[spot]

    for half in (0, 1):
        hand_on(IMG, images, half)
    image_pairs(2)
    drain(early, early_if)

    for o in range(1, 16):
        arrived(PLN + o, plane.at[lax.rem(spot + 16 - o, 16)])
    total = jnp.sum(plane[...], axis=0)
    for j in range(8):
        tails[j, 0:6, :] = total[6 * j : 6 * j + 6, :]
        tails[j, 6:8, :] = total[48:50, :]
    for j in range(8):
        @pl.when(first_owner + j != me)
        def _():
            pltpu.make_async_remote_copy(
                src_ref=tails.at[j], dst_ref=owned.at[z],
                send_sem=send_sem.at[OWN + j], recv_sem=recv_sem.at[OWN + z],
                device_id={"dp": first_owner + j}, device_id_type=pl.DeviceIdType.MESH,
            ).start()

        @pl.when(first_owner + j == me)
        def _():
            owned[z] = tails[j]

    for q in (1, 3):
        for half in (0, 1):
            cross_wait_rest(IMG, images, q, half)
        sib_send(IMG, images, 3 + q, crossed(x, q))
    image_pairs(4, 6)
    for half in (0, 1):
        cross_wait(IMG, images, 2, half)
    sib_send(IMG, images, 5, crossed(x, 2))
    image_pairs(5)
    unit = unit_t[...]
    dunit = acc_t[...]
    tg_ref[...] = dunit - unit * jnp.sum(unit * dunit, axis=-1, keepdims=True)
    tinv_ref[...] = inv_t[...]

    for zz in range(8):
        @pl.when(source(zz) != me)
        def _():
            arrived(OWN + zz, owned.at[zz])
    for n in range(4):
        hg_ref[:, n * 256 : (n + 1) * 256] = owned[n, 0:6, :] + owned[n + 4, 0:6, :]
    st_ref[...] = jnp.sum(owned[...], axis=0)
    for j in range(8):
        @pl.when(first_owner + j != me)
        def _():
            copy(OWN + j, tails.at[j], owned.at[z], first_owner + j).wait_send()
    drain(sent, sent_if)


def finish(ls_ref, st_ref, hgs_ref, tgs_ref, tinv_ref, loss_ref, sg_ref, hg_ref, tg_ref):
    temper = jnp.exp(jnp.full((1, B), ls_ref[0], jnp.float32))
    loss_ref[0] = jnp.sum(st_ref[6:7, 0:B]) / PAIRS
    sg_ref[0] = jnp.sum(st_ref[6:7, B : 2 * B] * temper) / PAIRS
    sg_ref[1] = jnp.sum(st_ref[7:8, 0:B]) / PAIRS
    hg_ref[...] = hgs_ref[...] * (1.0 / B)
    tg_ref[...] = tgs_ref[...] * tinv_ref[:, 0:1]


def shards(img_feats, txt_feats, img_head, txt_head, log_scale, logit_bias):
    f32, bf16 = jnp.float32, jnp.bfloat16
    smem = pl.BlockSpec(memory_space=pltpu.SMEM)
    vmem = pl.BlockSpec(memory_space=pltpu.VMEM)
    hbm = pl.BlockSpec(memory_space=pl.ANY)
    sums = pl.pallas_call(
        kernel,
        out_shape=(
            jax.ShapeDtypeStruct((8, 2 * B), f32),
            jax.ShapeDtypeStruct((6, E), f32),
            jax.ShapeDtypeStruct((B, E), f32),
            jax.ShapeDtypeStruct((B, 128), f32),
        ),
        in_specs=[smem] * 2 + [hbm] * 4,
        out_specs=(vmem,) * 4,
        scratch_shapes=[
            pltpu.VMEM((B, DT), bf16),
            pltpu.VMEM((DI, E), bf16),
            pltpu.VMEM((DT, E), bf16),
            pltpu.VMEM((4 * B, DI), bf16),
            pltpu.VMEM((14, B, E), bf16),
            pltpu.VMEM((14, B, E), bf16),
            pltpu.VMEM((B, E), f32),
            pltpu.VMEM((B, E), f32),
            pltpu.VMEM((B, E), f32),
            pltpu.VMEM((B, E), f32),
            pltpu.VMEM((B, 128), f32),
            pltpu.VMEM((B, 128), f32),
            pltpu.VMEM((4, 256, B), bf16),
            pltpu.VMEM((256, 4 * B), bf16),
            pltpu.VMEM((8, 256), f32),
            pltpu.VMEM((8, 256), f32),
            pltpu.VMEM((8, 8, 256), f32),
            pltpu.VMEM((768, 256), f32),
            pltpu.VMEM((768, 256), f32),
            pltpu.VMEM((768, 256), f32),
            pltpu.VMEM((16, 56, 256), f32),
            pltpu.VMEM((8, 8, 256), f32),
            pltpu.VMEM((16, 56, 256), f32),
            pltpu.SemaphoreType.DMA((16,)),
            pltpu.SemaphoreType.DMA((IDS,)),
            pltpu.SemaphoreType.DMA((IDS,)),
        ],
        compiler_params=pltpu.CompilerParams(
            collective_id=0, has_side_effects=True, vmem_limit_bytes=62 * 2**20
        ),
        cost_estimate=pl.CostEstimate(flops=5 * 10**9, bytes_accessed=14 * 10**6, transcendentals=10**6),
        name="contrastive",
    )(log_scale, logit_bias, img_feats, txt_feats, img_head, txt_head)
    loss, scalar_grads, head_grad, text_grad = pl.pallas_call(
        finish,
        out_shape=(
            jax.ShapeDtypeStruct((1,), f32),
            jax.ShapeDtypeStruct((2,), f32),
            jax.ShapeDtypeStruct((6, E), f32),
            jax.ShapeDtypeStruct((B, E), f32),
        ),
        in_specs=[smem] + [vmem] * 4,
        out_specs=(smem, smem, vmem, vmem),
        name="finish",
    )(log_scale, *sums)
    return loss.reshape(()), scalar_grads, head_grad, text_grad


def solution(mesh):
    in_specs = (P("dp", None), P("dp", None), P(), P(), P(), P())
    out_specs = (P(), P(), P("dp", None), P("dp", None))
    return jax.shard_map(shards, mesh=mesh, in_specs=in_specs, out_specs=out_specs, check_vma=False)
```

```python
import jax
import jax.numpy as jnp
from jax import lax
from jax.experimental import pallas as pl
from jax.experimental.pallas import tpu as pltpu
from jax.sharding import PartitionSpec as P

EPS = 1e-06
B = 128
E = 1024
DI = 1536
DT = 4096
N = 256
PAIRS = 54525952
CH = 512

TXT = 0
IMG = 24
FEA = 48
DLO = 52
SIB = 56
PLN = 60
OWN = 76
IDS = 84


def kernel(
    ls_ref, lb_ref, imgf_ref, txtf_ref, imgh_ref, txth_ref,
    st_ref, hg_ref, tg_ref, tinv_ref,
    txtf, imgh, txth, feats, texts, images, unit_t, unit_i, acc_t, acc_i, inv_t, inv_i,
    sum_t, sum_i, rcv_t, rcv_i, dlow_t, dgat, stat, stats2, tails, part_sib, part_rcv, part, plane, owned, pieces,
    load_sem, send_sem, recv_sem,
):
    me = lax.axis_index("dp")
    core = lax.rem(me, 2)
    spot = lax.rem(me // 2, 16)
    z = me // 32
    x = lax.rem(spot, 4)
    row_first = me - 2 * x
    right_x = lax.rem(x + 1, 4)
    left_x = lax.rem(x + 3, 4)
    right = row_first + 2 * right_x
    left = row_first + 2 * left_x
    inner = (x == 1) | (x == 2)
    up = lax.rem(me + 8, N)
    down = lax.rem(me + N - 8, N)
    sib = me + 1 - 2 * core

    side = 1 - 2 * core

    def z_mate(off):
        return lax.rem(me + 32 * off + N, N)

    def quarter(off):
        return lax.rem(z + off + 8, 4)

    def plane_mate(off):
        return 32 * z + 2 * lax.rem(spot + off, 16) + core

    first_owner = 128 * core + 8 * spot
    my_row = me // 8
    src_core = my_row // 16
    src_spot = lax.rem(my_row, 16)

    def source(zz):
        return 32 * zz + 2 * src_spot + src_core

    barrier = pltpu.get_barrier_semaphore()

    def greet(dev):
        pl.semaphore_signal(barrier, inc=1, device_id={"dp": dev}, device_id_type=pl.DeviceIdType.MESH)

    for dev in [right, left, up, down, sib] + [z_mate(side), z_mate(2 * side), z_mate(-side)] + [plane_mate(o) for o in range(1, 16)]:
        greet(dev)
    for zz in range(8):
        @pl.when(source(zz) != me)
        def _():
            greet(source(zz))

    loads = {}

    def load(i, src, dst):
        loads[i] = pltpu.make_async_copy(src, dst, load_sem.at[i])
        loads[i].start()

    load(0, imgf_ref, feats.at[pl.ds(0, B)])
    load(1, txtf_ref, txtf)
    for j in range(DT // CH):
        load(2 + j, txth_ref.at[pl.ds(j * CH, CH)], txth.at[pl.ds(j * CH, CH)])
    for j in range(DI // CH):
        load(10 + j, imgh_ref.at[pl.ds(j * CH, CH)], imgh.at[pl.ds(j * CH, CH)])

    owner_is_me = (me >= first_owner) & (me < first_owner + 8)

    sent = []
    sent_if = []

    def copy(i, src, dst, dev):
        return pltpu.make_async_remote_copy(
            src_ref=src, dst_ref=dst, send_sem=send_sem.at[i], recv_sem=recv_sem.at[i],
            device_id={"dp": dev}, device_id_type=pl.DeviceIdType.MESH,
        )

    def send(i, src, dst, dev):
        c = copy(i, src, dst, dev)
        c.start()
        sent.append(c)

    def send_if(cond, i, src, dst, dev, landing=None):
        c = pltpu.make_async_remote_copy(
            src_ref=src, dst_ref=dst, send_sem=send_sem.at[i],
            recv_sem=recv_sem.at[i if landing is None else landing],
            device_id={"dp": dev}, device_id_type=pl.DeviceIdType.MESH,
        )

        @pl.when(cond)
        def _():
            c.start()

        sent_if.append((cond, c))

    def drain(always, perhaps):
        for c in always:
            c.wait_send()
        for cond, c in perhaps:
            @pl.when(cond)
            def _():
                c.wait_send()

    def arrived(i, dst):
        copy(i, dst, dst, sib).wait_recv()

    def fea(n):
        return feats.at[pl.ds(n * B, B)]

    def in_row(at, q):
        return q - 4 * (at + q >= 4).astype(jnp.int32)

    def crossed(at, q):
        return q - 4 * (at + q < 4).astype(jnp.int32)

    def slot(ref, off, half=None):
        if half is None:
            return ref.at[2 * (3 + off) + core]
        return ref.at[2 * (3 + off) + core, pl.ds(half * (B // 2), B // 2)]

    def row_send(base, ref, half):
        send(base + 4 + (half or 0), slot(ref, 0, half), slot(ref, in_row(right_x, 3), half), right)
        send(base + (half or 0), slot(ref, 0, half), slot(ref, in_row(left_x, 1), half), left)

    def row_wait(base, ref, q, half):
        arrived(base + 2 * (q - 1) + (half or 0), slot(ref, in_row(x, q), half))

    right_on = (x == 3) | ((core == 0) & (x < 2))
    left_on = (x == 0) | ((core == 1) & (x >= 2))

    def opposite_send(base, ref, half):
        i = base + 2 + (half or 0)
        send_if(right_on, i, slot(ref, in_row(x, 3), half), slot(ref, in_row(right_x, 2), half), right)
        send_if(
            left_on, base + 21 + (half or 0), slot(ref, in_row(x, 1), half), slot(ref, in_row(left_x, 2), half),
            left, i,
        )

    def cross_send(base, ref, q, half):
        dev = jnp.where(x + q < 4, up, down)
        i = base + 6 + 2 * (q - 1) + (half or 0)
        src, dst = slot(ref, in_row(x, q), half), slot(ref, crossed(x, q), half)
        if q == 2:
            send_if(inner, i, src, dst, dev)
        else:
            send(i, src, dst, dev)

    def cross_wait(base, ref, q, half):
        arrived(base + 6 + 2 * (q - 1) + (half or 0), slot(ref, crossed(x, q), half))

    def cross_wait_rest(base, ref, q, half):
        @pl.when(x != (q + 1) // 2)
        def _():
            cross_wait(base, ref, q, half)

    def hand_on(base, ref, half):
        for at in (1, 2):
            @pl.when(x == at)
            def _():
                cross_wait(base, ref, 2 * at - 1, half)
        near = jnp.where(inner, x, 1)
        taken = crossed(near, 2 * near - 1)
        to = 3 * (near - 1)
        send_if(
            inner, base + 12 + (half or 0), slot(ref, taken, half), slot(ref, crossed(to, 2), half),
            row_first + 2 * to, base + 8 + (half or 0),
        )

    def own_rows(ref, of):
        return ref.at[pl.ds(pl.multiple_of(of * B, B), B)]

    def own_send(base, ref):
        send(base + 14, slot(ref, 0), slot(ref, 0), sib)

    def own_wait(base, ref):
        arrived(base + 14, ref.at[7 - core])

    def sums_send(base, acc, rcv):
        send(base + 15, own_rows(acc, 1 - core), rcv, sib)

    def sums(base, acc, rcv):
        arrived(base + 15, rcv)
        return own_rows(acc, core)[...] + rcv[...]

    def project(read, head, acc, first, count):
        acc[...] = jnp.zeros((B, E), jnp.float32)
        for j in range(count):
            loads[first + j].wait()
            acc[...] += jnp.dot(read(j), head[pl.ds(j * CH, CH), :], preferred_element_type=jnp.float32)

    def normalize(acc, unit, inv, ref):
        proj = acc[...]
        scale = lax.rsqrt(jnp.sum(proj * proj, axis=-1, keepdims=True) + EPS)
        value = proj * scale
        unit[...] = value
        inv[...] = jnp.broadcast_to(scale, (B, 128))
        ref[6 + core] = value.astype(jnp.bfloat16)

    loads[1].wait()
    project(lambda j: txtf[:, pl.ds(j * CH, CH)], txth, sum_t, 2, DT // CH)
    normalize(sum_t, unit_t, inv_t, texts)
    pl.semaphore_wait(barrier, 23 + 8 - owner_is_me.astype(jnp.int32))
    for half in (0, 1):
        row_send(TXT, texts, half)
    own_send(TXT, texts)
    loads[0].wait()
    send(FEA + 1, fea(0), fea(1), z_mate(-side))
    send(FEA + 3, fea(0), fea(3), z_mate(side))
    project(lambda j: feats[pl.ds(0, B), pl.ds(j * CH, CH)], imgh, sum_i, 10, DI // CH)
    normalize(sum_i, unit_i, inv_i, images)
    own_send(IMG, images)

    temper = jnp.exp(jnp.full((1, 2 * B), ls_ref[0], jnp.float32))
    bias = lb_ref[0]
    rows = lax.broadcasted_iota(jnp.int32, (2 * B, 1), 0)
    acc_i[...] = jnp.zeros((2 * B, E), jnp.float32)
    acc_t[...] = jnp.zeros((2 * B, E), jnp.float32)
    totals = [jnp.zeros((1, B), jnp.float32) for _ in range(3)]
    far_row = jnp.where((rows >= B) == (core == 0), 1.0, 0.0)

    def group(own, ref, numbers, acc, stats):
        offs = [0 if n == 0 else in_row(x, n) if n < 4 else crossed(x, n - 3) for n in numbers]
        wide = B * len(offs)
        block = jnp.concatenate([slot(ref, off)[...] for off in offs], axis=0)
        both = own[6:8].reshape(2 * B, E)
        cosine = lax.dot_general(
            both, block, (((1,), (1,)), ((), ())), preferred_element_type=jnp.float32
        )
        logits = temper[:, :wide] * cosine + bias
        small = jnp.exp(-jnp.abs(logits))
        grad = jnp.where(logits >= 0.0, 1.0, small) / (1.0 + small)
        if numbers == (0,):
            hit = lax.broadcasted_iota(jnp.int32, (2 * B, B), 1) + core * B == rows
            grad = grad - jnp.where(hit, 1.0, 0.0)
        else:
            far = jnp.concatenate(
                [jnp.full((1, B), (off == 6 * core - 3).astype(jnp.float32)) for off in offs], axis=1
            )
            live = 1.0 - far_row * far
            grad = grad * live
        if stats:
            signed = jnp.where(hit, -logits, logits) if numbers == (0,) else logits
            loss = jnp.maximum(signed, 0.0) + jnp.log1p(small)
            if numbers != (0,):
                loss = loss * live
            for k, term in enumerate((loss, grad * cosine, grad)):
                term = jnp.sum(term, axis=0, keepdims=True)
                for n in range(len(offs)):
                    totals[k] = totals[k] + term[:, n * B : (n + 1) * B]
        weights = (temper[:, :wide] * grad).astype(jnp.bfloat16)
        acc[...] += jnp.dot(weights, block, preferred_element_type=jnp.float32)

    def text_group(*numbers):
        group(images, texts, numbers, acc_i, True)

    def image_group(*numbers):
        group(texts, images, numbers, acc_t, False)

    own_wait(IMG, images)
    text_group(0)
    for half in (0, 1):
        for q in (1, 3):
            row_wait(TXT, texts, q, half)
            cross_send(TXT, texts, q, half)
        opposite_send(TXT, texts, half)
    for half in (0, 1):
        row_wait(TXT, texts, 2, half)
        cross_send(TXT, texts, 2, half)
        hand_on(TXT, texts, half)
    row_send(IMG, images, None)
    arrived(FEA + 1, fea(1))
    send(FEA + 2, fea(1), fea(2), z_mate(-side))
    text_group(1, 3)
    text_group(2)
    for q in (1, 3):
        for half in (0, 1):
            cross_wait_rest(TXT, texts, q, half)
    text_group(4, 6)
    for half in (0, 1):
        cross_wait(TXT, texts, 2, half)
    text_group(5)
    sums_send(TXT, acc_i, rcv_i)

    stat[...] = jnp.zeros((8, 2 * B), jnp.float32)
    stat[0:1, 0:B] = totals[0]
    stat[0:1, B : 2 * B] = totals[1]
    stat[1:2, 0:B] = totals[2]
    send(SIB + 2, stat, stats2, sib)
    unit = unit_i[...]
    dunit = sums(TXT, acc_i, rcv_i)
    dproj = inv_i[:, 0:1] * (dunit - unit * jnp.sum(unit * dunit, axis=-1, keepdims=True))
    for j in range(4):
        dlow_t[j] = dproj[:, j * 256 : (j + 1) * 256].T.astype(jnp.bfloat16)

    def window(n):
        return dgat.at[:, pl.ds(n * B, B)]

    for n, off in ((1, -side), (2, -2 * side), (3, side)):
        send(DLO + n, dlow_t.at[quarter(off)], window(n), z_mate(off))
    dgat[:, 0:B] = dlow_t[quarter(0)]
    for q in (1, 3):
        row_wait(IMG, images, q, None)
        cross_send(IMG, images, q, None)
    opposite_send(IMG, images, None)
    own_wait(TXT, texts)
    image_group(0)
    image_group(1, 3)
    row_wait(IMG, images, 2, None)
    cross_send(IMG, images, 2, None)

    for n in (1, 2, 3):
        arrived(DLO + n, window(n))
    arrived(FEA + 2, fea(2))
    arrived(FEA + 3, fea(3))

    def part_rows(ref, n):
        return ref.at[pl.ds(pl.multiple_of(n * 384, 384), 384)]

    def product(half, n, ref):
        columns = pl.ds(pl.multiple_of(half * 768 + n * 384, 128), 384)
        part_rows(ref, n)[...] = jnp.dot(
            dgat[...], feats[:, columns], preferred_element_type=jnp.float32
        ).T

    for j, n in enumerate((1 - core, core)):
        product(1 - core, n, part_sib)
        send(SIB + j, part_rows(part_sib, n), part_rows(part_rcv, n), sib)
    for n in (core, 1 - core):
        product(core, n, part)
    early, early_if = list(sent), list(sent_if)
    sent.clear()
    sent_if.clear()
    arrived(SIB + 2, stats2)
    both = stat[...] + stats2[...]
    for j, n in enumerate((core, 1 - core)):
        arrived(SIB + j, part_rows(part_rcv, n))
        for i in range(8):
            span = pl.ds(pl.multiple_of(n * 384 + i * 48, 16), 48)
            pieces[8 * n + i, 0:48, :] = part[span, :] + part_rcv[span, :]
            pieces[8 * n + i, 48:56, :] = both
        for i in range(8):
            to = 8 * n + lax.rem(spot + i, 8)
            send_if(
                to != spot, PLN + lax.rem(to - spot + 16, 16), pieces.at[to], plane.at[spot],
                32 * z + 2 * to + core,
            )
    plane[spot] = pieces[spot]

    hand_on(IMG, images, None)
    image_group(2)
    drain(early, early_if)

    for o in range(1, 16):
        arrived(PLN + o, plane.at[lax.rem(spot + 16 - o, 16)])
    total = jnp.sum(plane[...], axis=0)
    for j in range(8):
        tails[j, 0:6, :] = total[6 * j : 6 * j + 6, :]
        tails[j, 6:8, :] = total[48:50, :]
    for j in range(8):
        @pl.when(first_owner + j != me)
        def _():
            pltpu.make_async_remote_copy(
                src_ref=tails.at[j], dst_ref=owned.at[z],
                send_sem=send_sem.at[OWN + j], recv_sem=recv_sem.at[OWN + z],
                device_id={"dp": first_owner + j}, device_id_type=pl.DeviceIdType.MESH,
            ).start()

        @pl.when(first_owner + j == me)
        def _():
            owned[z] = tails[j]

    for q in (1, 3):
        cross_wait_rest(IMG, images, q, None)
    image_group(4, 6)
    cross_wait(IMG, images, 2, None)
    image_group(5)
    sums_send(IMG, acc_t, rcv_t)
    unit = unit_t[...]
    dunit = sums(IMG, acc_t, rcv_t)
    tg_ref[...] = dunit - unit * jnp.sum(unit * dunit, axis=-1, keepdims=True)
    tinv_ref[...] = inv_t[...]

    for zz in range(8):
        @pl.when(source(zz) != me)
        def _():
            arrived(OWN + zz, owned.at[zz])
    for n in range(4):
        hg_ref[:, n * 256 : (n + 1) * 256] = owned[n, 0:6, :] + owned[n + 4, 0:6, :]
    st_ref[...] = jnp.sum(owned[...], axis=0)
    for j in range(8):
        @pl.when(first_owner + j != me)
        def _():
            copy(OWN + j, tails.at[j], owned.at[z], first_owner + j).wait_send()
    drain(sent, sent_if)


def finish(ls_ref, st_ref, hgs_ref, tgs_ref, tinv_ref, loss_ref, sg_ref, hg_ref, tg_ref):
    temper = jnp.exp(jnp.full((1, B), ls_ref[0], jnp.float32))
    loss_ref[0] = jnp.sum(st_ref[6:7, 0:B]) / PAIRS
    sg_ref[0] = jnp.sum(st_ref[6:7, B : 2 * B] * temper) / PAIRS
    sg_ref[1] = jnp.sum(st_ref[7:8, 0:B]) / PAIRS
    hg_ref[...] = hgs_ref[...] * (1.0 / B)
    tg_ref[...] = tgs_ref[...] * tinv_ref[:, 0:1]


def shards(img_feats, txt_feats, img_head, txt_head, log_scale, logit_bias):
    f32, bf16 = jnp.float32, jnp.bfloat16
    smem = pl.BlockSpec(memory_space=pltpu.SMEM)
    vmem = pl.BlockSpec(memory_space=pltpu.VMEM)
    hbm = pl.BlockSpec(memory_space=pl.ANY)
    sums = pl.pallas_call(
        kernel,
        out_shape=(
            jax.ShapeDtypeStruct((8, 2 * B), f32),
            jax.ShapeDtypeStruct((6, E), f32),
            jax.ShapeDtypeStruct((B, E), f32),
            jax.ShapeDtypeStruct((B, 128), f32),
        ),
        in_specs=[smem] * 2 + [hbm] * 4,
        out_specs=(vmem,) * 4,
        scratch_shapes=[
            pltpu.VMEM((B, DT), bf16),
            pltpu.VMEM((DI, E), bf16),
            pltpu.VMEM((DT, E), bf16),
            pltpu.VMEM((4 * B, DI), bf16),
            pltpu.VMEM((14, B, E), bf16),
            pltpu.VMEM((14, B, E), bf16),
            pltpu.VMEM((B, E), f32),
            pltpu.VMEM((B, E), f32),
            pltpu.VMEM((2 * B, E), f32),
            pltpu.VMEM((2 * B, E), f32),
            pltpu.VMEM((B, 128), f32),
            pltpu.VMEM((B, 128), f32),
            pltpu.VMEM((B, E), f32),
            pltpu.VMEM((B, E), f32),
            pltpu.VMEM((B, E), f32),
            pltpu.VMEM((B, E), f32),
            pltpu.VMEM((4, 256, B), bf16),
            pltpu.VMEM((256, 4 * B), bf16),
            pltpu.VMEM((8, 256), f32),
            pltpu.VMEM((8, 256), f32),
            pltpu.VMEM((8, 8, 256), f32),
            pltpu.VMEM((768, 256), f32),
            pltpu.VMEM((768, 256), f32),
            pltpu.VMEM((768, 256), f32),
            pltpu.VMEM((16, 56, 256), f32),
            pltpu.VMEM((8, 8, 256), f32),
            pltpu.VMEM((16, 56, 256), f32),
            pltpu.SemaphoreType.DMA((16,)),
            pltpu.SemaphoreType.DMA((IDS,)),
            pltpu.SemaphoreType.DMA((IDS,)),
        ],
        compiler_params=pltpu.CompilerParams(
            collective_id=0, has_side_effects=True, vmem_limit_bytes=62 * 2**20
        ),
        cost_estimate=pl.CostEstimate(flops=5 * 10**9, bytes_accessed=14 * 10**6, transcendentals=10**6),
        name="contrastive",
    )(log_scale, logit_bias, img_feats, txt_feats, img_head, txt_head)
    loss, scalar_grads, head_grad, text_grad = pl.pallas_call(
        finish,
        out_shape=(
            jax.ShapeDtypeStruct((1,), f32),
            jax.ShapeDtypeStruct((2,), f32),
            jax.ShapeDtypeStruct((6, E), f32),
            jax.ShapeDtypeStruct((B, E), f32),
        ),
        in_specs=[smem] + [vmem] * 4,
        out_specs=(smem, smem, vmem, vmem),
        name="finish",
    )(log_scale, *sums)
    return loss.reshape(()), scalar_grads, head_grad, text_grad


def solution(mesh):
    in_specs = (P("dp", None), P("dp", None), P(), P(), P(), P())
    out_specs = (P(), P(), P("dp", None), P("dp", None))
    return jax.shard_map(shards, mesh=mesh, in_specs=in_specs, out_specs=out_specs, check_vma=False)
```

```python
import jax
import jax.numpy as jnp
from jax import lax
from jax.experimental import pallas as pl
from jax.experimental.pallas import tpu as pltpu
from jax.sharding import PartitionSpec as P

EPS = 1e-06
B = 128
E = 1024
DI = 1536
DT = 4096
N = 256
PAIRS = 54525952
CH = 512

TXT = 0
IMG = 24
FEA = 48
DLO = 52
SIB = 56
PLN = 60
OWN = 76
IDS = 84


def kernel(
    ls_ref, lb_ref, imgf_ref, txtf_ref, imgh_ref, txth_ref,
    st_ref, hg_ref, tg_ref, tinv_ref,
    txtf, imgh, txth, feats, texts, images, unit_t, unit_i, acc_t, acc_i, inv_t, inv_i,
    sum_t, sum_i, rcv_t, rcv_i, dlow_t, dgat, stat, stats2, tails, part_sib, part_rcv, part, plane, owned, pieces,
    load_sem, send_sem, recv_sem,
):
    me = lax.axis_index("dp")
    core = lax.rem(me, 2)
    spot = lax.rem(me // 2, 16)
    z = me // 32
    x = lax.rem(spot, 4)
    row_first = me - 2 * x
    right_x = lax.rem(x + 1, 4)
    left_x = lax.rem(x + 3, 4)
    right = row_first + 2 * right_x
    left = row_first + 2 * left_x
    inner = (x == 1) | (x == 2)
    up = lax.rem(me + 8, N)
    down = lax.rem(me + N - 8, N)
    sib = me + 1 - 2 * core

    side = 1 - 2 * core

    def z_mate(off):
        return lax.rem(me + 32 * off + N, N)

    def quarter(off):
        return lax.rem(z + off + 8, 4)

    def plane_mate(off):
        return 32 * z + 2 * lax.rem(spot + off, 16) + core

    first_owner = 128 * core + 8 * spot
    my_row = me // 8
    src_core = my_row // 16
    src_spot = lax.rem(my_row, 16)

    def source(zz):
        return 32 * zz + 2 * src_spot + src_core

    barrier = pltpu.get_barrier_semaphore()

    def greet(dev):
        pl.semaphore_signal(barrier, inc=1, device_id={"dp": dev}, device_id_type=pl.DeviceIdType.MESH)

    for dev in [right, left, up, down, sib] + [z_mate(side), z_mate(2 * side), z_mate(-side)] + [plane_mate(o) for o in range(1, 16)]:
        greet(dev)
    for zz in range(8):
        @pl.when(source(zz) != me)
        def _():
            greet(source(zz))

    loads = {}

    def load(i, src, dst):
        loads[i] = pltpu.make_async_copy(src, dst, load_sem.at[i])
        loads[i].start()

    load(0, imgf_ref, feats.at[pl.ds(0, B)])
    load(1, txtf_ref, txtf)
    for j in range(DT // CH):
        load(2 + j, txth_ref.at[pl.ds(j * CH, CH)], txth.at[pl.ds(j * CH, CH)])
    for j in range(DI // CH):
        load(10 + j, imgh_ref.at[pl.ds(j * CH, CH)], imgh.at[pl.ds(j * CH, CH)])

    owner_is_me = (me >= first_owner) & (me < first_owner + 8)

    sent = []
    sent_if = []

    def copy(i, src, dst, dev):
        return pltpu.make_async_remote_copy(
            src_ref=src, dst_ref=dst, send_sem=send_sem.at[i], recv_sem=recv_sem.at[i],
            device_id={"dp": dev}, device_id_type=pl.DeviceIdType.MESH,
        )

    def send(i, src, dst, dev):
        c = copy(i, src, dst, dev)
        c.start()
        sent.append(c)

    def send_if(cond, i, src, dst, dev, landing=None):
        c = pltpu.make_async_remote_copy(
            src_ref=src, dst_ref=dst, send_sem=send_sem.at[i],
            recv_sem=recv_sem.at[i if landing is None else landing],
            device_id={"dp": dev}, device_id_type=pl.DeviceIdType.MESH,
        )

        @pl.when(cond)
        def _():
            c.start()

        sent_if.append((cond, c))

    def drain(always, perhaps):
        for c in always:
            c.wait_send()
        for cond, c in perhaps:
            @pl.when(cond)
            def _():
                c.wait_send()

    def arrived(i, dst):
        copy(i, dst, dst, sib).wait_recv()

    def fea(n):
        return feats.at[pl.ds(n * B, B)]

    def in_row(at, q):
        return q - 4 * (at + q >= 4).astype(jnp.int32)

    def crossed(at, q):
        return q - 4 * (at + q < 4).astype(jnp.int32)

    def slot(ref, off, half=None):
        if half is None:
            return ref.at[2 * (3 + off) + core]
        return ref.at[2 * (3 + off) + core, pl.ds(half * (B // 2), B // 2)]

    def row_send(base, ref, half):
        send(base + 4 + (half or 0), slot(ref, 0, half), slot(ref, in_row(right_x, 3), half), right)
        send(base + (half or 0), slot(ref, 0, half), slot(ref, in_row(left_x, 1), half), left)

    def row_wait(base, ref, q, half):
        arrived(base + 2 * (q - 1) + (half or 0), slot(ref, in_row(x, q), half))

    right_on = (x == 3) | ((core == 0) & (x < 2))
    left_on = (x == 0) | ((core == 1) & (x >= 2))

    def opposite_send(base, ref, half):
        i = base + 2 + (half or 0)
        send_if(right_on, i, slot(ref, in_row(x, 3), half), slot(ref, in_row(right_x, 2), half), right)
        send_if(
            left_on, base + 21 + (half or 0), slot(ref, in_row(x, 1), half), slot(ref, in_row(left_x, 2), half),
            left, i,
        )

    def cross_send(base, ref, q, half):
        dev = jnp.where(x + q < 4, up, down)
        i = base + 6 + 2 * (q - 1) + (half or 0)
        src, dst = slot(ref, in_row(x, q), half), slot(ref, crossed(x, q), half)
        if q == 2:
            send_if(inner, i, src, dst, dev)
        else:
            send(i, src, dst, dev)

    def cross_wait(base, ref, q, half):
        arrived(base + 6 + 2 * (q - 1) + (half or 0), slot(ref, crossed(x, q), half))

    def cross_wait_rest(base, ref, q, half):
        @pl.when(x != (q + 1) // 2)
        def _():
            cross_wait(base, ref, q, half)

    def hand_on(base, ref, half):
        for at in (1, 2):
            @pl.when(x == at)
            def _():
                cross_wait(base, ref, 2 * at - 1, half)
        near = jnp.where(inner, x, 1)
        taken = crossed(near, 2 * near - 1)
        to = 3 * (near - 1)
        send_if(
            inner, base + 12 + (half or 0), slot(ref, taken, half), slot(ref, crossed(to, 2), half),
            row_first + 2 * to, base + 8 + (half or 0),
        )

    def own_rows(ref, of):
        return ref.at[pl.ds(pl.multiple_of(of * B, B), B)]

    def own_send(base, ref):
        send(base + 14, slot(ref, 0), slot(ref, 0), sib)

    def own_wait(base, ref):
        arrived(base + 14, ref.at[7 - core])

    def sums_send(base, acc, rcv):
        send(base + 15, own_rows(acc, 1 - core), rcv, sib)

    def sums(base, acc, rcv):
        arrived(base + 15, rcv)
        return own_rows(acc, core)[...] + rcv[...]

    def project(read, head, acc, first, count):
        acc[...] = jnp.zeros((B, E), jnp.float32)
        for j in range(count):
            loads[first + j].wait()
            acc[...] += jnp.dot(read(j), head[pl.ds(j * CH, CH), :], preferred_element_type=jnp.float32)

    def normalize(acc, unit, inv, ref):
        proj = acc[...]
        scale = lax.rsqrt(jnp.sum(proj * proj, axis=-1, keepdims=True) + EPS)
        value = proj * scale
        unit[...] = value
        inv[...] = jnp.broadcast_to(scale, (B, 128))
        ref[6 + core] = value.astype(jnp.bfloat16)

    loads[1].wait()
    project(lambda j: txtf[:, pl.ds(j * CH, CH)], txth, sum_t, 2, DT // CH)
    normalize(sum_t, unit_t, inv_t, texts)
    pl.semaphore_wait(barrier, 23 + 8 - owner_is_me.astype(jnp.int32))
    for half in (0, 1):
        row_send(TXT, texts, half)
    own_send(TXT, texts)
    loads[0].wait()
    send(FEA + 1, fea(0), fea(1), z_mate(-side))
    send(FEA + 3, fea(0), fea(3), z_mate(side))
    project(lambda j: feats[pl.ds(0, B), pl.ds(j * CH, CH)], imgh, sum_i, 10, DI // CH)
    normalize(sum_i, unit_i, inv_i, images)
    own_send(IMG, images)

    temper = jnp.exp(jnp.full((1, 2 * B), ls_ref[0], jnp.float32))
    bias = lb_ref[0]
    rows = lax.broadcasted_iota(jnp.int32, (2 * B, 1), 0)
    acc_i[...] = jnp.zeros((2 * B, E), jnp.float32)
    acc_t[...] = jnp.zeros((2 * B, E), jnp.float32)
    totals = [jnp.zeros((1, B), jnp.float32) for _ in range(3)]
    far_row = jnp.where((rows >= B) == (core == 0), 1.0, 0.0)

    def group(own, ref, numbers, acc, stats):
        offs = [0 if n == 0 else in_row(x, n) if n < 4 else crossed(x, n - 3) for n in numbers]
        wide = B * len(offs)
        block = jnp.concatenate([slot(ref, off)[...] for off in offs], axis=0)
        both = own[6:8].reshape(2 * B, E)
        cosine = lax.dot_general(
            both, block, (((1,), (1,)), ((), ())), preferred_element_type=jnp.float32
        )
        logits = temper[:, :wide] * cosine + bias
        small = jnp.exp(-jnp.abs(logits))
        grad = jnp.where(logits >= 0.0, 1.0, small) / (1.0 + small)
        if numbers == (0,):
            hit = lax.broadcasted_iota(jnp.int32, (2 * B, B), 1) + core * B == rows
            grad = grad - jnp.where(hit, 1.0, 0.0)
        else:
            far = jnp.concatenate(
                [jnp.full((1, B), (off == 6 * core - 3).astype(jnp.float32)) for off in offs], axis=1
            )
            live = 1.0 - far_row * far
            grad = grad * live
        if stats:
            signed = jnp.where(hit, -logits, logits) if numbers == (0,) else logits
            loss = jnp.maximum(signed, 0.0) + jnp.log1p(small)
            if numbers != (0,):
                loss = loss * live
            for k, term in enumerate((loss, grad * cosine, grad)):
                term = jnp.sum(term, axis=0, keepdims=True)
                for n in range(len(offs)):
                    totals[k] = totals[k] + term[:, n * B : (n + 1) * B]
        weights = (temper[:, :wide] * grad).astype(jnp.bfloat16)
        acc[...] += jnp.dot(weights, block, preferred_element_type=jnp.float32)

    def text_group(*numbers):
        group(images, texts, numbers, acc_i, True)

    def image_group(*numbers):
        group(texts, images, numbers, acc_t, False)

    own_wait(IMG, images)
    text_group(0)
    for half in (0, 1):
        for q in (1, 3):
            row_wait(TXT, texts, q, half)
            cross_send(TXT, texts, q, half)
        opposite_send(TXT, texts, half)
    for half in (0, 1):
        row_wait(TXT, texts, 2, half)
        cross_send(TXT, texts, 2, half)
        hand_on(TXT, texts, half)
    for half in (0, 1):
        row_send(IMG, images, half)
    arrived(FEA + 1, fea(1))
    send(FEA + 2, fea(1), fea(2), z_mate(-side))
    text_group(1, 3)
    text_group(2)
    for q in (1, 3):
        for half in (0, 1):
            cross_wait_rest(TXT, texts, q, half)
    early, early_if = list(sent), list(sent_if)
    sent.clear()
    sent_if.clear()

    def image_forward(half):
        for q in (1, 3):
            row_wait(IMG, images, q, half)
            cross_send(IMG, images, q, half)
        opposite_send(IMG, images, half)

    image_forward(0)
    text_group(4, 6)
    for half in (0, 1):
        cross_wait(TXT, texts, 2, half)
    text_group(5)
    sums_send(TXT, acc_i, rcv_i)
    image_forward(1)

    stat[...] = jnp.zeros((8, 2 * B), jnp.float32)
    stat[0:1, 0:B] = totals[0]
    stat[0:1, B : 2 * B] = totals[1]
    stat[1:2, 0:B] = totals[2]
    send(SIB + 2, stat, stats2, sib)
    unit = unit_i[...]
    dunit = sums(TXT, acc_i, rcv_i)
    dproj = inv_i[:, 0:1] * (dunit - unit * jnp.sum(unit * dunit, axis=-1, keepdims=True))
    for j in range(4):
        dlow_t[j] = dproj[:, j * 256 : (j + 1) * 256].T.astype(jnp.bfloat16)

    def window(n):
        return dgat.at[:, pl.ds(n * B, B)]

    for n, off in ((1, -side), (2, -2 * side), (3, side)):
        send(DLO + n, dlow_t.at[quarter(off)], window(n), z_mate(off))
    dgat[:, 0:B] = dlow_t[quarter(0)]
    own_wait(TXT, texts)
    image_group(0)
    image_group(1, 3)
    for half in (0, 1):
        row_wait(IMG, images, 2, half)
        cross_send(IMG, images, 2, half)

    for n in (1, 2, 3):
        arrived(DLO + n, window(n))
    arrived(FEA + 2, fea(2))
    arrived(FEA + 3, fea(3))

    def part_rows(ref, n):
        return ref.at[pl.ds(pl.multiple_of(n * 384, 384), 384)]

    def product(half, n, ref):
        columns = pl.ds(pl.multiple_of(half * 768 + n * 384, 128), 384)
        part_rows(ref, n)[...] = jnp.dot(
            dgat[...], feats[:, columns], preferred_element_type=jnp.float32
        ).T

    for j, n in enumerate((1 - core, core)):
        product(1 - core, n, part_sib)
        send(SIB + j, part_rows(part_sib, n), part_rows(part_rcv, n), sib)
    for n in (core, 1 - core):
        product(core, n, part)
    arrived(SIB + 2, stats2)
    both = stat[...] + stats2[...]
    for j, n in enumerate((core, 1 - core)):
        arrived(SIB + j, part_rows(part_rcv, n))
        for i in range(8):
            span = pl.ds(pl.multiple_of(n * 384 + i * 48, 16), 48)
            pieces[8 * n + i, 0:48, :] = part[span, :] + part_rcv[span, :]
            pieces[8 * n + i, 48:56, :] = both
        for i in range(8):
            to = 8 * n + lax.rem(spot + i, 8)
            send_if(
                to != spot, PLN + lax.rem(to - spot + 16, 16), pieces.at[to], plane.at[spot],
                32 * z + 2 * to + core,
            )
    plane[spot] = pieces[spot]

    for half in (0, 1):
        hand_on(IMG, images, half)
    image_group(2)
    drain(early, early_if)

    for o in range(1, 16):
        arrived(PLN + o, plane.at[lax.rem(spot + 16 - o, 16)])
    total = jnp.sum(plane[...], axis=0)
    for j in range(8):
        tails[j, 0:6, :] = total[6 * j : 6 * j + 6, :]
        tails[j, 6:8, :] = total[48:50, :]
    for j in range(8):
        @pl.when(first_owner + j != me)
        def _():
            pltpu.make_async_remote_copy(
                src_ref=tails.at[j], dst_ref=owned.at[z],
                send_sem=send_sem.at[OWN + j], recv_sem=recv_sem.at[OWN + z],
                device_id={"dp": first_owner + j}, device_id_type=pl.DeviceIdType.MESH,
            ).start()

        @pl.when(first_owner + j == me)
        def _():
            owned[z] = tails[j]

    for q in (1, 3):
        for half in (0, 1):
            cross_wait_rest(IMG, images, q, half)
    image_group(4, 6)
    for half in (0, 1):
        cross_wait(IMG, images, 2, half)
    image_group(5)
    sums_send(IMG, acc_t, rcv_t)
    unit = unit_t[...]
    dunit = sums(IMG, acc_t, rcv_t)
    tg_ref[...] = dunit - unit * jnp.sum(unit * dunit, axis=-1, keepdims=True)
    tinv_ref[...] = inv_t[...]

    for zz in range(8):
        @pl.when(source(zz) != me)
        def _():
            arrived(OWN + zz, owned.at[zz])
    for n in range(4):
        hg_ref[:, n * 256 : (n + 1) * 256] = owned[n, 0:6, :] + owned[n + 4, 0:6, :]
    st_ref[...] = jnp.sum(owned[...], axis=0)
    for j in range(8):
        @pl.when(first_owner + j != me)
        def _():
            copy(OWN + j, tails.at[j], owned.at[z], first_owner + j).wait_send()
    drain(sent, sent_if)


def finish(ls_ref, st_ref, hgs_ref, tgs_ref, tinv_ref, loss_ref, sg_ref, hg_ref, tg_ref):
    temper = jnp.exp(jnp.full((1, B), ls_ref[0], jnp.float32))
    loss_ref[0] = jnp.sum(st_ref[6:7, 0:B]) / PAIRS
    sg_ref[0] = jnp.sum(st_ref[6:7, B : 2 * B] * temper) / PAIRS
    sg_ref[1] = jnp.sum(st_ref[7:8, 0:B]) / PAIRS
    hg_ref[...] = hgs_ref[...] * (1.0 / B)
    tg_ref[...] = tgs_ref[...] * tinv_ref[:, 0:1]


def shards(img_feats, txt_feats, img_head, txt_head, log_scale, logit_bias):
    f32, bf16 = jnp.float32, jnp.bfloat16
    smem = pl.BlockSpec(memory_space=pltpu.SMEM)
    vmem = pl.BlockSpec(memory_space=pltpu.VMEM)
    hbm = pl.BlockSpec(memory_space=pl.ANY)
    sums = pl.pallas_call(
        kernel,
        out_shape=(
            jax.ShapeDtypeStruct((8, 2 * B), f32),
            jax.ShapeDtypeStruct((6, E), f32),
            jax.ShapeDtypeStruct((B, E), f32),
            jax.ShapeDtypeStruct((B, 128), f32),
        ),
        in_specs=[smem] * 2 + [hbm] * 4,
        out_specs=(vmem,) * 4,
        scratch_shapes=[
            pltpu.VMEM((B, DT), bf16),
            pltpu.VMEM((DI, E), bf16),
            pltpu.VMEM((DT, E), bf16),
            pltpu.VMEM((4 * B, DI), bf16),
            pltpu.VMEM((14, B, E), bf16),
            pltpu.VMEM((14, B, E), bf16),
            pltpu.VMEM((B, E), f32),
            pltpu.VMEM((B, E), f32),
            pltpu.VMEM((2 * B, E), f32),
            pltpu.VMEM((2 * B, E), f32),
            pltpu.VMEM((B, 128), f32),
            pltpu.VMEM((B, 128), f32),
            pltpu.VMEM((B, E), f32),
            pltpu.VMEM((B, E), f32),
            pltpu.VMEM((B, E), f32),
            pltpu.VMEM((B, E), f32),
            pltpu.VMEM((4, 256, B), bf16),
            pltpu.VMEM((256, 4 * B), bf16),
            pltpu.VMEM((8, 256), f32),
            pltpu.VMEM((8, 256), f32),
            pltpu.VMEM((8, 8, 256), f32),
            pltpu.VMEM((768, 256), f32),
            pltpu.VMEM((768, 256), f32),
            pltpu.VMEM((768, 256), f32),
            pltpu.VMEM((16, 56, 256), f32),
            pltpu.VMEM((8, 8, 256), f32),
            pltpu.VMEM((16, 56, 256), f32),
            pltpu.SemaphoreType.DMA((16,)),
            pltpu.SemaphoreType.DMA((IDS,)),
            pltpu.SemaphoreType.DMA((IDS,)),
        ],
        compiler_params=pltpu.CompilerParams(
            collective_id=0, has_side_effects=True, vmem_limit_bytes=62 * 2**20
        ),
        cost_estimate=pl.CostEstimate(flops=5 * 10**9, bytes_accessed=14 * 10**6, transcendentals=10**6),
        name="contrastive",
    )(log_scale, logit_bias, img_feats, txt_feats, img_head, txt_head)
    loss, scalar_grads, head_grad, text_grad = pl.pallas_call(
        finish,
        out_shape=(
            jax.ShapeDtypeStruct((1,), f32),
            jax.ShapeDtypeStruct((2,), f32),
            jax.ShapeDtypeStruct((6, E), f32),
            jax.ShapeDtypeStruct((B, E), f32),
        ),
        in_specs=[smem] + [vmem] * 4,
        out_specs=(smem, smem, vmem, vmem),
        name="finish",
    )(log_scale, *sums)
    return loss.reshape(()), scalar_grads, head_grad, text_grad


def solution(mesh):
    in_specs = (P("dp", None), P("dp", None), P(), P(), P(), P())
    out_specs = (P(), P(), P("dp", None), P("dp", None))
    return jax.shard_map(shards, mesh=mesh, in_specs=in_specs, out_specs=out_specs, check_vma=False)
```

```python
import jax
import jax.numpy as jnp
from jax import lax
from jax.experimental import pallas as pl
from jax.experimental.pallas import tpu as pltpu
from jax.sharding import PartitionSpec as P

EPS = 1e-06
B = 128
E = 1024
DI = 1536
DT = 4096
N = 256
PAIRS = 54525952
CH = 512

TXT = 0
IMG = 24
FEA = 48
DLO = 52
SIB = 56
PLA = 60
PLB = 68
OWN = 76
IDS = 84


def kernel(
    ls_ref, lb_ref, imgf_ref, txtf_ref, imgh_ref, txth_ref,
    st_ref, hg_ref, tg_ref, tinv_ref,
    txtf, imgh, txth, feats, texts, images, unit_t, unit_i, acc_t, acc_i, inv_t, inv_i,
    sum_t, sum_i, rcv_t, rcv_i, dlow_t, dgat, stat, stats2, tails, part_sib, part_rcv, part, owned,
    out_a, in_a, out_b, in_b, out_a2, in_a2, out_b2, in_b2,
    load_sem, send_sem, recv_sem,
):
    me = lax.axis_index("dp")
    core = lax.rem(me, 2)
    spot = lax.rem(me // 2, 16)
    z = me // 32
    x = lax.rem(spot, 4)
    row_first = me - 2 * x
    right_x = lax.rem(x + 1, 4)
    left_x = lax.rem(x + 3, 4)
    right = row_first + 2 * right_x
    left = row_first + 2 * left_x
    inner = (x == 1) | (x == 2)
    up = lax.rem(me + 8, N)
    down = lax.rem(me + N - 8, N)
    sib = me + 1 - 2 * core

    side = 1 - 2 * core

    def z_mate(off):
        return lax.rem(me + 32 * off + N, N)

    def quarter(off):
        return lax.rem(z + off + 8, 4)

    y = spot // 4

    def x_mate(off):
        return row_first + 2 * lax.rem(x + off, 4)

    def y_mate(off):
        return 32 * z + 8 * lax.rem(y + off, 4) + 2 * x + core

    first_owner = 128 * core + 8 * spot
    my_row = me // 8
    src_core = my_row // 16
    src_spot = lax.rem(my_row, 16)

    def source(zz):
        return 32 * zz + 2 * src_spot + src_core

    barrier = pltpu.get_barrier_semaphore()

    def greet(dev):
        pl.semaphore_signal(barrier, inc=1, device_id={"dp": dev}, device_id_type=pl.DeviceIdType.MESH)

    for dev in [right, left, up, down, sib, x_mate(2)] + [z_mate(side), z_mate(2 * side), z_mate(-side)] + [y_mate(o) for o in range(1, 4)]:
        greet(dev)
    for zz in range(8):
        @pl.when(source(zz) != me)
        def _():
            greet(source(zz))

    loads = {}

    def load(i, src, dst):
        loads[i] = pltpu.make_async_copy(src, dst, load_sem.at[i])
        loads[i].start()

    load(0, imgf_ref, feats.at[pl.ds(0, B)])
    load(1, txtf_ref, txtf)
    for j in range(DT // CH):
        load(2 + j, txth_ref.at[pl.ds(j * CH, CH)], txth.at[pl.ds(j * CH, CH)])
    for j in range(DI // CH):
        load(10 + j, imgh_ref.at[pl.ds(j * CH, CH)], imgh.at[pl.ds(j * CH, CH)])

    owner_is_me = (me >= first_owner) & (me < first_owner + 8)

    sent = []
    sent_if = []

    def copy(i, src, dst, dev):
        return pltpu.make_async_remote_copy(
            src_ref=src, dst_ref=dst, send_sem=send_sem.at[i], recv_sem=recv_sem.at[i],
            device_id={"dp": dev}, device_id_type=pl.DeviceIdType.MESH,
        )

    def send(i, src, dst, dev):
        c = copy(i, src, dst, dev)
        c.start()
        sent.append(c)

    def send_if(cond, i, src, dst, dev, landing=None):
        c = pltpu.make_async_remote_copy(
            src_ref=src, dst_ref=dst, send_sem=send_sem.at[i],
            recv_sem=recv_sem.at[i if landing is None else landing],
            device_id={"dp": dev}, device_id_type=pl.DeviceIdType.MESH,
        )

        @pl.when(cond)
        def _():
            c.start()

        sent_if.append((cond, c))

    def drain(always, perhaps):
        for c in always:
            c.wait_send()
        for cond, c in perhaps:
            @pl.when(cond)
            def _():
                c.wait_send()

    def arrived(i, dst):
        copy(i, dst, dst, sib).wait_recv()

    def fea(n):
        return feats.at[pl.ds(n * B, B)]

    def in_row(at, q):
        return q - 4 * (at + q >= 4).astype(jnp.int32)

    def crossed(at, q):
        return q - 4 * (at + q < 4).astype(jnp.int32)

    def slot(ref, off, half=None):
        if half is None:
            return ref.at[2 * (3 + off) + core]
        return ref.at[2 * (3 + off) + core, pl.ds(half * (B // 2), B // 2)]

    def row_send(base, ref, half):
        send(base + 4 + (half or 0), slot(ref, 0, half), slot(ref, in_row(right_x, 3), half), right)
        send(base + (half or 0), slot(ref, 0, half), slot(ref, in_row(left_x, 1), half), left)

    def row_wait(base, ref, q, half):
        arrived(base + 2 * (q - 1) + (half or 0), slot(ref, in_row(x, q), half))

    right_on = (x == 3) | ((core == 0) & (x < 2))
    left_on = (x == 0) | ((core == 1) & (x >= 2))

    def opposite_send(base, ref, half):
        i = base + 2 + (half or 0)
        send_if(right_on, i, slot(ref, in_row(x, 3), half), slot(ref, in_row(right_x, 2), half), right)
        send_if(
            left_on, base + 21 + (half or 0), slot(ref, in_row(x, 1), half), slot(ref, in_row(left_x, 2), half),
            left, i,
        )

    def cross_send(base, ref, q, half):
        dev = jnp.where(x + q < 4, up, down)
        i = base + 6 + 2 * (q - 1) + (half or 0)
        src, dst = slot(ref, in_row(x, q), half), slot(ref, crossed(x, q), half)
        if q == 2:
            send_if(inner, i, src, dst, dev)
        else:
            send(i, src, dst, dev)

    def cross_wait(base, ref, q, half):
        arrived(base + 6 + 2 * (q - 1) + (half or 0), slot(ref, crossed(x, q), half))

    def cross_wait_rest(base, ref, q, half):
        @pl.when(x != (q + 1) // 2)
        def _():
            cross_wait(base, ref, q, half)

    def hand_on(base, ref, half):
        for at in (1, 2):
            @pl.when(x == at)
            def _():
                cross_wait(base, ref, 2 * at - 1, half)
        near = jnp.where(inner, x, 1)
        taken = crossed(near, 2 * near - 1)
        to = 3 * (near - 1)
        send_if(
            inner, base + 12 + (half or 0), slot(ref, taken, half), slot(ref, crossed(to, 2), half),
            row_first + 2 * to, base + 8 + (half or 0),
        )

    def own_rows(ref, of):
        return ref.at[pl.ds(pl.multiple_of(of * B, B), B)]

    def own_send(base, ref):
        send(base + 14, slot(ref, 0), slot(ref, 0), sib)

    def own_wait(base, ref):
        arrived(base + 14, ref.at[7 - core])

    def sums_send(base, acc, rcv):
        send(base + 15, own_rows(acc, 1 - core), rcv, sib)

    def sums(base, acc, rcv):
        arrived(base + 15, rcv)
        return own_rows(acc, core)[...] + rcv[...]

    def project(read, head, acc, first, count):
        acc[...] = jnp.zeros((B, E), jnp.float32)
        for j in range(count):
            loads[first + j].wait()
            acc[...] += jnp.dot(read(j), head[pl.ds(j * CH, CH), :], preferred_element_type=jnp.float32)

    def normalize(acc, unit, inv, ref):
        proj = acc[...]
        scale = lax.rsqrt(jnp.sum(proj * proj, axis=-1, keepdims=True) + EPS)
        value = proj * scale
        unit[...] = value
        inv[...] = jnp.broadcast_to(scale, (B, 128))
        ref[6 + core] = value.astype(jnp.bfloat16)

    loads[1].wait()
    project(lambda j: txtf[:, pl.ds(j * CH, CH)], txth, sum_t, 2, DT // CH)
    normalize(sum_t, unit_t, inv_t, texts)
    pl.semaphore_wait(barrier, 12 + 8 - owner_is_me.astype(jnp.int32))
    for half in (0, 1):
        row_send(TXT, texts, half)
    own_send(TXT, texts)
    loads[0].wait()
    send(FEA + 1, fea(0), fea(1), z_mate(-side))
    send(FEA + 3, fea(0), fea(3), z_mate(side))
    project(lambda j: feats[pl.ds(0, B), pl.ds(j * CH, CH)], imgh, sum_i, 10, DI // CH)
    normalize(sum_i, unit_i, inv_i, images)
    own_send(IMG, images)

    temper = jnp.exp(jnp.full((1, 2 * B), ls_ref[0], jnp.float32))
    bias = lb_ref[0]
    rows = lax.broadcasted_iota(jnp.int32, (2 * B, 1), 0)
    acc_i[...] = jnp.zeros((2 * B, E), jnp.float32)
    acc_t[...] = jnp.zeros((2 * B, E), jnp.float32)
    totals = [jnp.zeros((1, B), jnp.float32) for _ in range(3)]
    far_row = jnp.where((rows >= B) == (core == 0), 1.0, 0.0)

    def group(own, ref, numbers, acc, stats):
        offs = [0 if n == 0 else in_row(x, n) if n < 4 else crossed(x, n - 3) for n in numbers]
        wide = B * len(offs)
        block = jnp.concatenate([slot(ref, off)[...] for off in offs], axis=0)
        both = own[6:8].reshape(2 * B, E)
        cosine = lax.dot_general(
            both, block, (((1,), (1,)), ((), ())), preferred_element_type=jnp.float32
        )
        logits = temper[:, :wide] * cosine + bias
        small = jnp.exp(-jnp.abs(logits))
        grad = jnp.where(logits >= 0.0, 1.0, small) / (1.0 + small)
        if numbers == (0,):
            hit = lax.broadcasted_iota(jnp.int32, (2 * B, B), 1) + core * B == rows
            grad = grad - jnp.where(hit, 1.0, 0.0)
        else:
            far = jnp.concatenate(
                [jnp.full((1, B), (off == 6 * core - 3).astype(jnp.float32)) for off in offs], axis=1
            )
            live = 1.0 - far_row * far
            grad = grad * live
        if stats:
            signed = jnp.where(hit, -logits, logits) if numbers == (0,) else logits
            loss = jnp.maximum(signed, 0.0) + jnp.log1p(small)
            if numbers != (0,):
                loss = loss * live
            for k, term in enumerate((loss, grad * cosine, grad)):
                term = jnp.sum(term, axis=0, keepdims=True)
                for n in range(len(offs)):
                    totals[k] = totals[k] + term[:, n * B : (n + 1) * B]
        weights = (temper[:, :wide] * grad).astype(jnp.bfloat16)
        acc[...] += jnp.dot(weights, block, preferred_element_type=jnp.float32)

    def text_group(*numbers):
        group(images, texts, numbers, acc_i, True)

    def image_group(*numbers):
        group(texts, images, numbers, acc_t, False)

    own_wait(IMG, images)
    text_group(0)
    for half in (0, 1):
        for q in (1, 3):
            row_wait(TXT, texts, q, half)
            cross_send(TXT, texts, q, half)
        opposite_send(TXT, texts, half)
    for half in (0, 1):
        row_wait(TXT, texts, 2, half)
        cross_send(TXT, texts, 2, half)
        hand_on(TXT, texts, half)
    row_send(IMG, images, None)
    arrived(FEA + 1, fea(1))
    send(FEA + 2, fea(1), fea(2), z_mate(-side))
    text_group(1, 3)
    text_group(2)
    for q in (1, 3):
        for half in (0, 1):
            cross_wait_rest(TXT, texts, q, half)
    text_group(4, 6)
    for half in (0, 1):
        cross_wait(TXT, texts, 2, half)
    text_group(5)
    sums_send(TXT, acc_i, rcv_i)

    for n in range(3):
        stat[n : n + 1, :] = totals[n]
    stat[3:8, :] = jnp.zeros((5, B), jnp.float32)
    send(SIB + 2, stat, stats2, sib)
    unit = unit_i[...]
    dunit = sums(TXT, acc_i, rcv_i)
    dproj = inv_i[:, 0:1] * (dunit - unit * jnp.sum(unit * dunit, axis=-1, keepdims=True))
    for j in range(4):
        dlow_t[j] = dproj[:, j * 256 : (j + 1) * 256].T.astype(jnp.bfloat16)

    def window(n):
        return dgat.at[:, pl.ds(n * B, B)]

    for n, off in ((1, -side), (2, -2 * side), (3, side)):
        send(DLO + n, dlow_t.at[quarter(off)], window(n), z_mate(off))
    dgat[:, 0:B] = dlow_t[quarter(0)]
    early, early_if = list(sent), list(sent_if)
    sent.clear()
    sent_if.clear()
    for q in (1, 3):
        row_wait(IMG, images, q, None)
        cross_send(IMG, images, q, None)
    opposite_send(IMG, images, None)
    own_wait(TXT, texts)
    image_group(0)
    image_group(1, 3)
    row_wait(IMG, images, 2, None)
    cross_send(IMG, images, 2, None)

    for n in (1, 2, 3):
        arrived(DLO + n, window(n))
    arrived(FEA + 2, fea(2))
    arrived(FEA + 3, fea(3))

    def part_rows(ref, n):
        return ref.at[pl.ds(pl.multiple_of(n * 384, 384), 384)]

    def product(half, n, ref):
        columns = pl.ds(pl.multiple_of(half * 768 + n * 384, 128), 384)
        part_rows(ref, n)[...] = jnp.dot(
            dgat[...], feats[:, columns], preferred_element_type=jnp.float32
        ).T

    for j, n in enumerate((1 - core, core)):
        product(1 - core, n, part_sib)
        send(SIB + j, part_rows(part_sib, n), part_rows(part_rcv, n), sib)
    for n in (core, 1 - core):
        product(core, n, part)
    arrived(SIB + 2, stats2)
    both = stat[...] + stats2[...]
    for j, n in enumerate((core, 1 - core)):
        arrived(SIB + j, part_rows(part_rcv, n))
        for i in range(8):
            span = pl.ds(pl.multiple_of(n * 384 + i * 48, 16), 48)
            value = part[span, :] + part_rcv[span, :]
            to_y, to_x = 2 * n + i // 4, i % 4
            out_a[to_x, pl.ds(pl.multiple_of(to_y * 48, 16), 48), :] = value[:, :B]
            out_b[to_y, 48 * to_x : 48 * to_x + 48, :] = value[:, B:]
        for i in range(2):
            to_y = 2 * n + i
            o = lax.rem(to_y - y + 4, 4)
            send_if(to_y != y, PLB + o, out_b.at[to_y], in_b.at[o], y_mate(o))
    for n in range(4):
        out_a[n, 192:200, :] = both
    for o in (1, 2, 3):
        send(PLA + o, out_a.at[lax.rem(x + o, 4)], in_a.at[o], x_mate(o))

    hand_on(IMG, images, None)
    image_group(2)
    drain(early, early_if)

    def summed(base, out, at, got):
        for o in (1, 2, 3):
            arrived(base + o, got.at[o])
        return out[at] + got[1] + got[2] + got[3]

    total = summed(PLB, out_b, y, in_b)
    for n in range(4):
        out_b2[n] = total[48 * n : 48 * n + 48, :]
    for o in (1, 2, 3):
        send(PLB + 4 + o, out_b2.at[lax.rem(x + o, 4)], in_b2.at[o], x_mate(o))
    total = summed(PLA, out_a, x, in_a)
    for n in range(4):
        out_a2[n, 0:48, :] = total[48 * n : 48 * n + 48, :]
        out_a2[n, 48:56, :] = total[192:200, :]
    for o in (1, 2, 3):
        send(PLA + 4 + o, out_a2.at[lax.rem(y + o, 4)], in_a2.at[o], y_mate(o))
    total_b = summed(PLB + 4, out_b2, x, in_b2)
    total_a = summed(PLA + 4, out_a2, y, in_a2)
    for j in range(8):
        tails[j, 0:6, 0:B] = total_a[6 * j : 6 * j + 6, :]
        tails[j, 0:6, B : 2 * B] = total_b[6 * j : 6 * j + 6, :]
        tails[j, 6:7, 0:B] = total_a[48:49, :]
        tails[j, 6:7, B : 2 * B] = total_a[49:50, :]
        tails[j, 7:8, 0:B] = total_a[50:51, :]
        tails[j, 7:8, B : 2 * B] = jnp.zeros((1, B), jnp.float32)
    for j in range(8):
        @pl.when(first_owner + j != me)
        def _():
            pltpu.make_async_remote_copy(
                src_ref=tails.at[j], dst_ref=owned.at[z],
                send_sem=send_sem.at[OWN + j], recv_sem=recv_sem.at[OWN + z],
                device_id={"dp": first_owner + j}, device_id_type=pl.DeviceIdType.MESH,
            ).start()

        @pl.when(first_owner + j == me)
        def _():
            owned[z] = tails[j]

    for q in (1, 3):
        cross_wait_rest(IMG, images, q, None)
    image_group(4, 6)
    cross_wait(IMG, images, 2, None)
    image_group(5)
    sums_send(IMG, acc_t, rcv_t)
    unit = unit_t[...]
    dunit = sums(IMG, acc_t, rcv_t)
    tg_ref[...] = dunit - unit * jnp.sum(unit * dunit, axis=-1, keepdims=True)
    tinv_ref[...] = inv_t[...]

    for zz in range(8):
        @pl.when(source(zz) != me)
        def _():
            arrived(OWN + zz, owned.at[zz])
    for n in range(4):
        hg_ref[:, n * 256 : (n + 1) * 256] = owned[n, 0:6, :] + owned[n + 4, 0:6, :]
    st_ref[...] = jnp.sum(owned[...], axis=0)
    for j in range(8):
        @pl.when(first_owner + j != me)
        def _():
            copy(OWN + j, tails.at[j], owned.at[z], first_owner + j).wait_send()
    drain(sent, sent_if)


def finish(ls_ref, st_ref, hgs_ref, tgs_ref, tinv_ref, loss_ref, sg_ref, hg_ref, tg_ref):
    temper = jnp.exp(jnp.full((1, B), ls_ref[0], jnp.float32))
    loss_ref[0] = jnp.sum(st_ref[6:7, 0:B]) / PAIRS
    sg_ref[0] = jnp.sum(st_ref[6:7, B : 2 * B] * temper) / PAIRS
    sg_ref[1] = jnp.sum(st_ref[7:8, 0:B]) / PAIRS
    hg_ref[...] = hgs_ref[...] * (1.0 / B)
    tg_ref[...] = tgs_ref[...] * tinv_ref[:, 0:1]


def shards(img_feats, txt_feats, img_head, txt_head, log_scale, logit_bias):
    f32, bf16 = jnp.float32, jnp.bfloat16
    smem = pl.BlockSpec(memory_space=pltpu.SMEM)
    vmem = pl.BlockSpec(memory_space=pltpu.VMEM)
    hbm = pl.BlockSpec(memory_space=pl.ANY)
    sums = pl.pallas_call(
        kernel,
        out_shape=(
            jax.ShapeDtypeStruct((8, 2 * B), f32),
            jax.ShapeDtypeStruct((6, E), f32),
            jax.ShapeDtypeStruct((B, E), f32),
            jax.ShapeDtypeStruct((B, 128), f32),
        ),
        in_specs=[smem] * 2 + [hbm] * 4,
        out_specs=(vmem,) * 4,
        scratch_shapes=[
            pltpu.VMEM((B, DT), bf16),
            pltpu.VMEM((DI, E), bf16),
            pltpu.VMEM((DT, E), bf16),
            pltpu.VMEM((4 * B, DI), bf16),
            pltpu.VMEM((14, B, E), bf16),
            pltpu.VMEM((14, B, E), bf16),
            pltpu.VMEM((B, E), f32),
            pltpu.VMEM((B, E), f32),
            pltpu.VMEM((2 * B, E), f32),
            pltpu.VMEM((2 * B, E), f32),
            pltpu.VMEM((B, 128), f32),
            pltpu.VMEM((B, 128), f32),
            pltpu.VMEM((B, E), f32),
            pltpu.VMEM((B, E), f32),
            pltpu.VMEM((B, E), f32),
            pltpu.VMEM((B, E), f32),
            pltpu.VMEM((4, 256, B), bf16),
            pltpu.VMEM((256, 4 * B), bf16),
            pltpu.VMEM((8, 128), f32),
            pltpu.VMEM((8, 128), f32),
            pltpu.VMEM((8, 8, 256), f32),
            pltpu.VMEM((768, 256), f32),
            pltpu.VMEM((768, 256), f32),
            pltpu.VMEM((768, 256), f32),
            pltpu.VMEM((8, 8, 256), f32),
            pltpu.VMEM((4, 200, 128), f32),
            pltpu.VMEM((4, 200, 128), f32),
            pltpu.VMEM((4, 192, 128), f32),
            pltpu.VMEM((4, 192, 128), f32),
            pltpu.VMEM((4, 56, 128), f32),
            pltpu.VMEM((4, 56, 128), f32),
            pltpu.VMEM((4, 48, 128), f32),
            pltpu.VMEM((4, 48, 128), f32),
            pltpu.SemaphoreType.DMA((16,)),
            pltpu.SemaphoreType.DMA((IDS,)),
            pltpu.SemaphoreType.DMA((IDS,)),
        ],
        compiler_params=pltpu.CompilerParams(
            collective_id=0, has_side_effects=True, vmem_limit_bytes=62 * 2**20
        ),
        cost_estimate=pl.CostEstimate(flops=5 * 10**9, bytes_accessed=14 * 10**6, transcendentals=10**6),
        name="contrastive",
    )(log_scale, logit_bias, img_feats, txt_feats, img_head, txt_head)
    loss, scalar_grads, head_grad, text_grad = pl.pallas_call(
        finish,
        out_shape=(
            jax.ShapeDtypeStruct((1,), f32),
            jax.ShapeDtypeStruct((2,), f32),
            jax.ShapeDtypeStruct((6, E), f32),
            jax.ShapeDtypeStruct((B, E), f32),
        ),
        in_specs=[smem] + [vmem] * 4,
        out_specs=(smem, smem, vmem, vmem),
        name="finish",
    )(log_scale, *sums)
    return loss.reshape(()), scalar_grads, head_grad, text_grad


def solution(mesh):
    in_specs = (P("dp", None), P("dp", None), P(), P(), P(), P())
    out_specs = (P(), P(), P("dp", None), P("dp", None))
    return jax.shard_map(shards, mesh=mesh, in_specs=in_specs, out_specs=out_specs, check_vma=False)
```

```python
import jax
import jax.numpy as jnp
from jax import lax
from jax.experimental import pallas as pl
from jax.experimental.pallas import tpu as pltpu
from jax.sharding import PartitionSpec as P

EPS = 1e-06
B = 128
E = 1024
DI = 1536
DT = 4096
N = 256
PAIRS = 54525952
CH = 512

TXT = 0
IMG = 24
FEA = 48
DLO = 52
SIB = 56
PLA = 60
PLB = 68
OWN = 76
IDS = 84


def kernel(
    ls_ref, lb_ref, imgf_ref, txtf_ref, imgh_ref, txth_ref,
    st_ref, hg_ref, tg_ref, tinv_ref,
    txtf, imgh, txth, feats, texts, images, unit_t, unit_i, acc_t, acc_i, inv_t, inv_i,
    sum_t, sum_i, rcv_t, rcv_i, dlow, dlow_t, dgat, stat, stats2, tails, part_sib, part_rcv, part, owned,
    out_a, in_a, out_b, in_b, out_a2, in_a2, out_b2, in_b2,
    load_sem, send_sem, recv_sem,
):
    me = lax.axis_index("dp")
    core = lax.rem(me, 2)
    spot = lax.rem(me // 2, 16)
    z = me // 32
    x = lax.rem(spot, 4)
    row_first = me - 2 * x
    right_x = lax.rem(x + 1, 4)
    left_x = lax.rem(x + 3, 4)
    right = row_first + 2 * right_x
    left = row_first + 2 * left_x
    inner = (x == 1) | (x == 2)
    up = lax.rem(me + 8, N)
    down = lax.rem(me + N - 8, N)
    sib = me + 1 - 2 * core

    side = 1 - 2 * core

    def z_mate(off):
        return lax.rem(me + 32 * off + N, N)

    def quarter(off):
        return lax.rem(z + off + 8, 4)

    y = spot // 4

    def x_mate(off):
        return row_first + 2 * lax.rem(x + off, 4)

    def y_mate(off):
        return 32 * z + 8 * lax.rem(y + off, 4) + 2 * x + core

    first_owner = 128 * core + 8 * spot
    my_row = me // 8
    src_core = my_row // 16
    src_spot = lax.rem(my_row, 16)

    def source(zz):
        return 32 * zz + 2 * src_spot + src_core

    loads = {}

    def load(i, src, dst):
        loads[i] = pltpu.make_async_copy(src, dst, load_sem.at[i])
        loads[i].start()

    load(0, imgf_ref, feats.at[pl.ds(0, B)])
    load(1, txtf_ref, txtf)
    for j in range(DT // CH):
        load(2 + j, txth_ref.at[pl.ds(j * CH, CH)], txth.at[pl.ds(j * CH, CH)])
    for j in range(DI // CH):
        load(10 + j, imgh_ref.at[pl.ds(j * CH, CH)], imgh.at[pl.ds(j * CH, CH)])

    barrier = pltpu.get_barrier_semaphore()

    def greet(dev):
        pl.semaphore_signal(barrier, inc=1, device_id={"dp": dev}, device_id_type=pl.DeviceIdType.MESH)

    for dev in [right, left, up, down, sib, x_mate(2)] + [z_mate(side), z_mate(2 * side), z_mate(-side)] + [y_mate(o) for o in range(1, 4)]:
        greet(dev)
    for zz in range(8):
        @pl.when(source(zz) != me)
        def _():
            greet(source(zz))

    owner_is_me = (me >= first_owner) & (me < first_owner + 8)

    sent = []
    sent_if = []

    def copy(i, src, dst, dev):
        return pltpu.make_async_remote_copy(
            src_ref=src, dst_ref=dst, send_sem=send_sem.at[i], recv_sem=recv_sem.at[i],
            device_id={"dp": dev}, device_id_type=pl.DeviceIdType.MESH,
        )

    def send(i, src, dst, dev):
        c = copy(i, src, dst, dev)
        c.start()
        sent.append(c)

    def send_if(cond, i, src, dst, dev, landing=None):
        c = pltpu.make_async_remote_copy(
            src_ref=src, dst_ref=dst, send_sem=send_sem.at[i],
            recv_sem=recv_sem.at[i if landing is None else landing],
            device_id={"dp": dev}, device_id_type=pl.DeviceIdType.MESH,
        )

        @pl.when(cond)
        def _():
            c.start()

        sent_if.append((cond, c))

    def drain(always, perhaps):
        for c in always:
            c.wait_send()
        for cond, c in perhaps:
            @pl.when(cond)
            def _():
                c.wait_send()

    def arrived(i, dst):
        copy(i, dst, dst, sib).wait_recv()

    def fea(n):
        return feats.at[pl.ds(n * B, B)]

    def in_row(at, q):
        return q - 4 * (at + q >= 4).astype(jnp.int32)

    def crossed(at, q):
        return q - 4 * (at + q < 4).astype(jnp.int32)

    def slot(ref, off, half=None):
        if half is None:
            return ref.at[2 * (3 + off) + core]
        return ref.at[2 * (3 + off) + core, pl.ds(half * (B // 2), B // 2)]

    def row_send(base, ref, half):
        send(base + 4 + (half or 0), slot(ref, 0, half), slot(ref, in_row(right_x, 3), half), right)
        send(base + (half or 0), slot(ref, 0, half), slot(ref, in_row(left_x, 1), half), left)

    def row_wait(base, ref, q, half):
        arrived(base + 2 * (q - 1) + (half or 0), slot(ref, in_row(x, q), half))

    right_on = (x == 3) | ((core == 0) & (x < 2))
    left_on = (x == 0) | ((core == 1) & (x >= 2))

    def opposite_send(base, ref, half):
        i = base + 2 + (half or 0)
        send_if(right_on, i, slot(ref, in_row(x, 3), half), slot(ref, in_row(right_x, 2), half), right)
        send_if(
            left_on, base + 21 + (half or 0), slot(ref, in_row(x, 1), half), slot(ref, in_row(left_x, 2), half),
            left, i,
        )

    def cross_send(base, ref, q, half):
        dev = jnp.where(x + q < 4, up, down)
        i = base + 6 + 2 * (q - 1) + (half or 0)
        src, dst = slot(ref, in_row(x, q), half), slot(ref, crossed(x, q), half)
        if q == 2:
            send_if(inner, i, src, dst, dev)
        else:
            send(i, src, dst, dev)

    def cross_wait(base, ref, q, half):
        arrived(base + 6 + 2 * (q - 1) + (half or 0), slot(ref, crossed(x, q), half))

    def cross_wait_rest(base, ref, q, half):
        @pl.when(x != (q + 1) // 2)
        def _():
            cross_wait(base, ref, q, half)

    def hand_on(base, ref, half):
        for at in (1, 2):
            @pl.when(x == at)
            def _():
                cross_wait(base, ref, 2 * at - 1, half)
        near = jnp.where(inner, x, 1)
        taken = crossed(near, 2 * near - 1)
        to = 3 * (near - 1)
        send_if(
            inner, base + 12 + (half or 0), slot(ref, taken, half), slot(ref, crossed(to, 2), half),
            row_first + 2 * to, base + 8 + (half or 0),
        )

    def own_rows(ref, of):
        return ref.at[pl.ds(pl.multiple_of(of * B, B), B)]

    def own_send(base, ref):
        send(base + 14, slot(ref, 0), slot(ref, 0), sib)

    def own_wait(base, ref):
        arrived(base + 14, ref.at[7 - core])

    def sums_send(base, acc, rcv):
        send(base + 15, own_rows(acc, 1 - core), rcv, sib)

    def sums(base, acc, rcv):
        arrived(base + 15, rcv)
        return own_rows(acc, core)[...] + rcv[...]

    def project(read, head, acc, first, count):
        acc[...] = jnp.zeros((B, E), jnp.float32)
        for j in range(count):
            loads[first + j].wait()
            acc[...] += jnp.dot(read(j), head[pl.ds(j * CH, CH), :], preferred_element_type=jnp.float32)

    def normalize(acc, unit, inv, ref):
        proj = acc[...]
        scale = lax.rsqrt(jnp.sum(proj * proj, axis=-1, keepdims=True) + EPS)
        value = proj * scale
        unit[...] = value
        inv[...] = jnp.broadcast_to(scale, (B, 128))
        ref[6 + core] = value.astype(jnp.bfloat16)

    loads[1].wait()
    project(lambda j: txtf[:, pl.ds(j * CH, CH)], txth, sum_t, 2, DT // CH)
    normalize(sum_t, unit_t, inv_t, texts)
    pl.semaphore_wait(barrier, 12 + 8 - owner_is_me.astype(jnp.int32))
    for half in (0, 1):
        row_send(TXT, texts, half)
    own_send(TXT, texts)
    loads[0].wait()
    send(FEA + 1, fea(0), fea(1), z_mate(-side))
    send(FEA + 3, fea(0), fea(3), z_mate(side))
    project(lambda j: feats[pl.ds(0, B), pl.ds(j * CH, CH)], imgh, sum_i, 10, DI // CH)
    normalize(sum_i, unit_i, inv_i, images)
    own_send(IMG, images)

    temper = jnp.exp(jnp.full((1, 2 * B), ls_ref[0], jnp.float32))
    bias = lb_ref[0]
    rows = lax.broadcasted_iota(jnp.int32, (2 * B, 1), 0)
    acc_i[...] = jnp.zeros((2 * B, E), jnp.float32)
    acc_t[...] = jnp.zeros((2 * B, E), jnp.float32)
    totals = [jnp.zeros((1, B), jnp.float32) for _ in range(3)]
    far_row = jnp.where((rows >= B) == (core == 0), 1.0, 0.0)

    def group(own, ref, numbers, acc, stats):
        offs = [0 if n == 0 else in_row(x, n) if n < 4 else crossed(x, n - 3) for n in numbers]
        wide = B * len(offs)
        block = jnp.concatenate([slot(ref, off)[...] for off in offs], axis=0)
        both = own[6:8].reshape(2 * B, E)
        cosine = lax.dot_general(
            both, block, (((1,), (1,)), ((), ())), preferred_element_type=jnp.float32
        )
        logits = temper[:, :wide] * cosine + bias
        small = jnp.exp(-jnp.abs(logits))
        grad = jnp.where(logits >= 0.0, 1.0, small) / (1.0 + small)
        if numbers == (0,):
            hit = lax.broadcasted_iota(jnp.int32, (2 * B, B), 1) + core * B == rows
            grad = grad - jnp.where(hit, 1.0, 0.0)
        else:
            far = jnp.concatenate(
                [jnp.full((1, B), (off == 6 * core - 3).astype(jnp.float32)) for off in offs], axis=1
            )
            live = 1.0 - far_row * far
            grad = grad * live
        if stats:
            signed = jnp.where(hit, -logits, logits) if numbers == (0,) else logits
            loss = jnp.maximum(signed, 0.0) + jnp.log1p(small)
            if numbers != (0,):
                loss = loss * live
            for k, term in enumerate((loss, grad * cosine, grad)):
                term = jnp.sum(term, axis=0, keepdims=True)
                for n in range(len(offs)):
                    totals[k] = totals[k] + term[:, n * B : (n + 1) * B]
        weights = (temper[:, :wide] * grad).astype(jnp.bfloat16)
        acc[...] += jnp.dot(weights, block, preferred_element_type=jnp.float32)

    def text_group(*numbers):
        group(images, texts, numbers, acc_i, True)

    def image_group(*numbers):
        group(texts, images, numbers, acc_t, False)

    own_wait(IMG, images)
    text_group(0)
    for half in (0, 1):
        for q in (1, 3):
            row_wait(TXT, texts, q, half)
            cross_send(TXT, texts, q, half)
        opposite_send(TXT, texts, half)
    for half in (0, 1):
        row_wait(TXT, texts, 2, half)
        cross_send(TXT, texts, 2, half)
        hand_on(TXT, texts, half)
    row_send(IMG, images, None)
    arrived(FEA + 1, fea(1))
    send(FEA + 2, fea(1), fea(2), z_mate(-side))
    text_group(1, 3)
    text_group(2)
    for q in (1, 3):
        for half in (0, 1):
            cross_wait_rest(TXT, texts, q, half)
    text_group(4, 6)
    for half in (0, 1):
        cross_wait(TXT, texts, 2, half)
    text_group(5)
    sums_send(TXT, acc_i, rcv_i)

    for n in range(3):
        stat[n : n + 1, :] = totals[n]
    stat[3:8, :] = jnp.zeros((5, B), jnp.float32)
    send(SIB + 2, stat, stats2, sib)
    unit = unit_i[...]
    dunit = sums(TXT, acc_i, rcv_i)
    dproj = inv_i[:, 0:1] * (dunit - unit * jnp.sum(unit * dunit, axis=-1, keepdims=True))
    dlow[...] = dproj

    def window(n):
        return dgat.at[:, pl.ds(n * B, B)]

    for n, off in ((2, -2 * side), (1, -side), (3, side), (0, 0)):
        j = quarter(off)
        turned = dlow[:, pl.ds(pl.multiple_of(j * 256, 256), 256)].T.astype(jnp.bfloat16)
        if n == 0:
            dgat[:, 0:B] = turned
        else:
            dlow_t[n] = turned
            send(DLO + n, dlow_t.at[n], window(n), z_mate(off))
    early, early_if = list(sent), list(sent_if)
    sent.clear()
    sent_if.clear()
    for q in (1, 3):
        row_wait(IMG, images, q, None)
        cross_send(IMG, images, q, None)
    opposite_send(IMG, images, None)
    own_wait(TXT, texts)
    image_group(0)
    image_group(1, 3)

    for n in (1, 2, 3):
        arrived(DLO + n, window(n))
    arrived(FEA + 2, fea(2))
    arrived(FEA + 3, fea(3))

    def part_rows(ref, n):
        return ref.at[pl.ds(pl.multiple_of(n * 384, 384), 384)]

    def product(half, n, ref):
        columns = pl.ds(pl.multiple_of(half * 768 + n * 384, 128), 384)
        part_rows(ref, n)[...] = jnp.dot(
            dgat[...], feats[:, columns], preferred_element_type=jnp.float32
        ).T

    for j, n in enumerate((1 - core, core)):
        product(1 - core, n, part_sib)
        send(SIB + j, part_rows(part_sib, n), part_rows(part_rcv, n), sib)
    for n in (core, 1 - core):
        product(core, n, part)
    arrived(SIB + 2, stats2)
    both = stat[...] + stats2[...]
    for j, n in enumerate((core, 1 - core)):
        arrived(SIB + j, part_rows(part_rcv, n))
        for i in range(8):
            span = pl.ds(pl.multiple_of(n * 384 + i * 48, 16), 48)
            value = part[span, :] + part_rcv[span, :]
            to_y, to_x = 2 * n + i // 4, i % 4
            out_a[to_x, pl.ds(pl.multiple_of(to_y * 48, 16), 48), :] = value[:, :B]
            out_b[to_y, 48 * to_x : 48 * to_x + 48, :] = value[:, B:]
        for i in range(2):
            to_y = 2 * n + i
            o = lax.rem(to_y - y + 4, 4)
            send_if(to_y != y, PLB + o, out_b.at[to_y], in_b.at[o], y_mate(o))
    for n in range(4):
        out_a[n, 192:200, :] = both
    for o in (1, 2, 3):
        send(PLA + o, out_a.at[lax.rem(x + o, 4)], in_a.at[o], x_mate(o))

    row_wait(IMG, images, 2, None)
    cross_send(IMG, images, 2, None)
    hand_on(IMG, images, None)
    image_group(2)
    drain(early, early_if)

    def summed(base, out, at, got):
        for o in (1, 2, 3):
            arrived(base + o, got.at[o])
        return out[at] + got[1] + got[2] + got[3]

    total = summed(PLB, out_b, y, in_b)
    for n in range(4):
        out_b2[n] = total[48 * n : 48 * n + 48, :]
    for o in (1, 2, 3):
        send(PLB + 4 + o, out_b2.at[lax.rem(x + o, 4)], in_b2.at[o], x_mate(o))
    total = summed(PLA, out_a, x, in_a)
    for n in range(4):
        out_a2[n, 0:48, :] = total[48 * n : 48 * n + 48, :]
        out_a2[n, 48:56, :] = total[192:200, :]
    for o in (1, 2, 3):
        send(PLA + 4 + o, out_a2.at[lax.rem(y + o, 4)], in_a2.at[o], y_mate(o))
    total_b = summed(PLB + 4, out_b2, x, in_b2)
    total_a = summed(PLA + 4, out_a2, y, in_a2)
    for j in range(8):
        tails[j, 0:6, 0:B] = total_a[6 * j : 6 * j + 6, :]
        tails[j, 0:6, B : 2 * B] = total_b[6 * j : 6 * j + 6, :]
        tails[j, 6:7, 0:B] = total_a[48:49, :]
        tails[j, 6:7, B : 2 * B] = total_a[49:50, :]
        tails[j, 7:8, 0:B] = total_a[50:51, :]
        tails[j, 7:8, B : 2 * B] = jnp.zeros((1, B), jnp.float32)
    for j in range(8):
        @pl.when(first_owner + j != me)
        def _():
            pltpu.make_async_remote_copy(
                src_ref=tails.at[j], dst_ref=owned.at[z],
                send_sem=send_sem.at[OWN + j], recv_sem=recv_sem.at[OWN + z],
                device_id={"dp": first_owner + j}, device_id_type=pl.DeviceIdType.MESH,
            ).start()

        @pl.when(first_owner + j == me)
        def _():
            owned[z] = tails[j]

    for q in (1, 3):
        cross_wait_rest(IMG, images, q, None)
    image_group(4, 6)
    cross_wait(IMG, images, 2, None)
    image_group(5)
    sums_send(IMG, acc_t, rcv_t)
    unit = unit_t[...]
    dunit = sums(IMG, acc_t, rcv_t)
    tg_ref[...] = dunit - unit * jnp.sum(unit * dunit, axis=-1, keepdims=True)
    tinv_ref[...] = inv_t[...]

    for zz in range(8):
        @pl.when(source(zz) != me)
        def _():
            arrived(OWN + zz, owned.at[zz])
    for n in range(4):
        hg_ref[:, n * 256 : (n + 1) * 256] = owned[n, 0:6, :] + owned[n + 4, 0:6, :]
    st_ref[...] = jnp.sum(owned[...], axis=0)
    for j in range(8):
        @pl.when(first_owner + j != me)
        def _():
            copy(OWN + j, tails.at[j], owned.at[z], first_owner + j).wait_send()
    drain(sent, sent_if)


def finish(ls_ref, st_ref, hgs_ref, tgs_ref, tinv_ref, loss_ref, sg_ref, hg_ref, tg_ref):
    temper = jnp.exp(jnp.full((1, B), ls_ref[0], jnp.float32))
    loss_ref[0] = jnp.sum(st_ref[6:7, 0:B]) / PAIRS
    sg_ref[0] = jnp.sum(st_ref[6:7, B : 2 * B] * temper) / PAIRS
    sg_ref[1] = jnp.sum(st_ref[7:8, 0:B]) / PAIRS
    hg_ref[...] = hgs_ref[...] * (1.0 / B)
    tg_ref[...] = tgs_ref[...] * tinv_ref[:, 0:1]


def shards(img_feats, txt_feats, img_head, txt_head, log_scale, logit_bias):
    f32, bf16 = jnp.float32, jnp.bfloat16
    smem = pl.BlockSpec(memory_space=pltpu.SMEM)
    vmem = pl.BlockSpec(memory_space=pltpu.VMEM)
    hbm = pl.BlockSpec(memory_space=pl.ANY)
    sums = pl.pallas_call(
        kernel,
        out_shape=(
            jax.ShapeDtypeStruct((8, 2 * B), f32),
            jax.ShapeDtypeStruct((6, E), f32),
            jax.ShapeDtypeStruct((B, E), f32),
            jax.ShapeDtypeStruct((B, 128), f32),
        ),
        in_specs=[smem] * 2 + [hbm] * 4,
        out_specs=(vmem,) * 4,
        scratch_shapes=[
            pltpu.VMEM((B, DT), bf16),
            pltpu.VMEM((DI, E), bf16),
            pltpu.VMEM((DT, E), bf16),
            pltpu.VMEM((4 * B, DI), bf16),
            pltpu.VMEM((14, B, E), bf16),
            pltpu.VMEM((14, B, E), bf16),
            pltpu.VMEM((B, E), f32),
            pltpu.VMEM((B, E), f32),
            pltpu.VMEM((2 * B, E), f32),
            pltpu.VMEM((2 * B, E), f32),
            pltpu.VMEM((B, 128), f32),
            pltpu.VMEM((B, 128), f32),
            pltpu.VMEM((B, E), f32),
            pltpu.VMEM((B, E), f32),
            pltpu.VMEM((B, E), f32),
            pltpu.VMEM((B, E), f32),
            pltpu.VMEM((B, E), f32),
            pltpu.VMEM((4, 256, B), bf16),
            pltpu.VMEM((256, 4 * B), bf16),
            pltpu.VMEM((8, 128), f32),
            pltpu.VMEM((8, 128), f32),
            pltpu.VMEM((8, 8, 256), f32),
            pltpu.VMEM((768, 256), f32),
            pltpu.VMEM((768, 256), f32),
            pltpu.VMEM((768, 256), f32),
            pltpu.VMEM((8, 8, 256), f32),
            pltpu.VMEM((4, 200, 128), f32),
            pltpu.VMEM((4, 200, 128), f32),
            pltpu.VMEM((4, 192, 128), f32),
            pltpu.VMEM((4, 192, 128), f32),
            pltpu.VMEM((4, 56, 128), f32),
            pltpu.VMEM((4, 56, 128), f32),
            pltpu.VMEM((4, 48, 128), f32),
            pltpu.VMEM((4, 48, 128), f32),
            pltpu.SemaphoreType.DMA((16,)),
            pltpu.SemaphoreType.DMA((IDS,)),
            pltpu.SemaphoreType.DMA((IDS,)),
        ],
        compiler_params=pltpu.CompilerParams(
            collective_id=0, has_side_effects=True, vmem_limit_bytes=62 * 2**20
        ),
        cost_estimate=pl.CostEstimate(flops=5 * 10**9, bytes_accessed=14 * 10**6, transcendentals=10**6),
        name="contrastive",
    )(log_scale, logit_bias, img_feats, txt_feats, img_head, txt_head)
    loss, scalar_grads, head_grad, text_grad = pl.pallas_call(
        finish,
        out_shape=(
            jax.ShapeDtypeStruct((1,), f32),
            jax.ShapeDtypeStruct((2,), f32),
            jax.ShapeDtypeStruct((6, E), f32),
            jax.ShapeDtypeStruct((B, E), f32),
        ),
        in_specs=[smem] + [vmem] * 4,
        out_specs=(smem, smem, vmem, vmem),
        name="finish",
    )(log_scale, *sums)
    return loss.reshape(()), scalar_grads, head_grad, text_grad


def solution(mesh):
    in_specs = (P("dp", None), P("dp", None), P(), P(), P(), P())
    out_specs = (P(), P(), P("dp", None), P("dp", None))
    return jax.shard_map(shards, mesh=mesh, in_specs=in_specs, out_specs=out_specs, check_vma=False)
```

```python
import jax
import jax.numpy as jnp
from jax import lax
from jax.experimental import pallas as pl
from jax.experimental.pallas import tpu as pltpu
from jax.sharding import PartitionSpec as P

EPS = 1e-06
B = 128
E = 1024
DI = 1536
DT = 4096
N = 256
PAIRS = 54525952
CH = 512

TXT = 0
IMG = 24
FEA = 48
DLO = 52
SIB = 56
PLA = 60
PLB = 68
OWN = 76
IDS = 84


def kernel(
    ls_ref, lb_ref, imgf_ref, txtf_ref, imgh_ref, txth_ref,
    st_ref, hg_ref, tg_ref, tinv_ref,
    txtf, imgh, txth, feats, texts, images, unit_t, unit_i, acc_t, acc_i, inv_t, inv_i,
    sum_t, sum_i, rcv_t, rcv_i, dlow, dlow_t, dgat, stat, stats2, tails, part_sib, part_rcv, part, owned,
    out_a, in_a, out_b, in_b, out_a2, in_a2, out_b2, in_b2,
    load_sem, send_sem, recv_sem,
):
    me = lax.axis_index("dp")
    core = lax.rem(me, 2)
    spot = lax.rem(me // 2, 16)
    z = me // 32
    x = lax.rem(spot, 4)
    row_first = me - 2 * x
    right_x = lax.rem(x + 1, 4)
    left_x = lax.rem(x + 3, 4)
    right = row_first + 2 * right_x
    left = row_first + 2 * left_x
    inner = (x == 1) | (x == 2)
    up = lax.rem(me + 8, N)
    down = lax.rem(me + N - 8, N)
    sib = me + 1 - 2 * core

    side = 1 - 2 * core

    def z_mate(off):
        return lax.rem(me + 32 * off + N, N)

    def quarter(off):
        return lax.rem(z + off + 8, 4)

    y = spot // 4

    def x_mate(off):
        return row_first + 2 * lax.rem(x + off, 4)

    def y_mate(off):
        return 32 * z + 8 * lax.rem(y + off, 4) + 2 * x + core

    first_owner = 128 * core + 8 * spot
    my_row = me // 8
    src_core = my_row // 16
    src_spot = lax.rem(my_row, 16)

    def source(zz):
        return 32 * zz + 2 * src_spot + src_core

    loads = {}

    def load(i, src, dst):
        loads[i] = pltpu.make_async_copy(src, dst, load_sem.at[i])
        loads[i].start()

    load(0, imgf_ref, feats.at[pl.ds(0, B)])
    load(1, txtf_ref, txtf)
    for j in range(DT // CH):
        load(2 + j, txth_ref.at[pl.ds(j * CH, CH)], txth.at[pl.ds(j * CH, CH)])
    for j in range(DI // CH):
        load(10 + j, imgh_ref.at[pl.ds(j * CH, CH)], imgh.at[pl.ds(j * CH, CH)])

    barrier = pltpu.get_barrier_semaphore()

    def greet(dev):
        pl.semaphore_signal(barrier, inc=1, device_id={"dp": dev}, device_id_type=pl.DeviceIdType.MESH)

    for dev in [right, left, up, down, sib, x_mate(2)] + [z_mate(side), z_mate(2 * side), z_mate(-side)] + [y_mate(o) for o in range(1, 4)]:
        greet(dev)
    for zz in range(8):
        @pl.when(source(zz) != me)
        def _():
            greet(source(zz))

    owner_is_me = (me >= first_owner) & (me < first_owner + 8)

    sent = []
    sent_if = []

    def copy(i, src, dst, dev):
        return pltpu.make_async_remote_copy(
            src_ref=src, dst_ref=dst, send_sem=send_sem.at[i], recv_sem=recv_sem.at[i],
            device_id={"dp": dev}, device_id_type=pl.DeviceIdType.MESH,
        )

    def send(i, src, dst, dev):
        c = copy(i, src, dst, dev)
        c.start()
        sent.append(c)

    def send_if(cond, i, src, dst, dev, landing=None):
        c = pltpu.make_async_remote_copy(
            src_ref=src, dst_ref=dst, send_sem=send_sem.at[i],
            recv_sem=recv_sem.at[i if landing is None else landing],
            device_id={"dp": dev}, device_id_type=pl.DeviceIdType.MESH,
        )

        @pl.when(cond)
        def _():
            c.start()

        sent_if.append((cond, c))

    def drain(always, perhaps):
        for c in always:
            c.wait_send()
        for cond, c in perhaps:
            @pl.when(cond)
            def _():
                c.wait_send()

    def arrived(i, dst):
        copy(i, dst, dst, sib).wait_recv()

    def fea(n):
        return feats.at[pl.ds(n * B, B)]

    def in_row(at, q):
        return q - 4 * (at + q >= 4).astype(jnp.int32)

    def crossed(at, q):
        return q - 4 * (at + q < 4).astype(jnp.int32)

    def slot(ref, off, half=None):
        if half is None:
            return ref.at[2 * (3 + off) + core]
        return ref.at[2 * (3 + off) + core, pl.ds(half * (B // 2), B // 2)]

    def row_send(base, ref, half):
        send(base + 4 + (half or 0), slot(ref, 0, half), slot(ref, in_row(right_x, 3), half), right)
        send(base + (half or 0), slot(ref, 0, half), slot(ref, in_row(left_x, 1), half), left)

    def row_wait(base, ref, q, half):
        arrived(base + 2 * (q - 1) + (half or 0), slot(ref, in_row(x, q), half))

    right_on = (x == 3) | ((core == 0) & (x < 2))
    left_on = (x == 0) | ((core == 1) & (x >= 2))

    def opposite_send(base, ref, half):
        i = base + 2 + (half or 0)
        send_if(right_on, i, slot(ref, in_row(x, 3), half), slot(ref, in_row(right_x, 2), half), right)
        send_if(
            left_on, base + 21 + (half or 0), slot(ref, in_row(x, 1), half), slot(ref, in_row(left_x, 2), half),
            left, i,
        )

    def cross_send(base, ref, q, half):
        dev = jnp.where(x + q < 4, up, down)
        i = base + 6 + 2 * (q - 1) + (half or 0)
        src, dst = slot(ref, in_row(x, q), half), slot(ref, crossed(x, q), half)
        if q == 2:
            send_if(inner, i, src, dst, dev)
        else:
            send(i, src, dst, dev)

    def cross_wait(base, ref, q, half):
        arrived(base + 6 + 2 * (q - 1) + (half or 0), slot(ref, crossed(x, q), half))

    def cross_wait_rest(base, ref, q, half):
        @pl.when(x != (q + 1) // 2)
        def _():
            cross_wait(base, ref, q, half)

    def hand_on(base, ref, half):
        for at in (1, 2):
            @pl.when(x == at)
            def _():
                cross_wait(base, ref, 2 * at - 1, half)
        near = jnp.where(inner, x, 1)
        taken = crossed(near, 2 * near - 1)
        to = 3 * (near - 1)
        send_if(
            inner, base + 12 + (half or 0), slot(ref, taken, half), slot(ref, crossed(to, 2), half),
            row_first + 2 * to, base + 8 + (half or 0),
        )

    def own_rows(ref, of):
        return ref.at[pl.ds(pl.multiple_of(of * B, B), B)]

    def own_send(base, ref):
        send(base + 14, slot(ref, 0), slot(ref, 0), sib)

    def own_wait(base, ref):
        arrived(base + 14, ref.at[7 - core])

    def sums_send(base, acc, rcv):
        send(base + 15, own_rows(acc, 1 - core), rcv, sib)

    def sums(base, acc, rcv):
        arrived(base + 15, rcv)
        return own_rows(acc, core)[...] + rcv[...]

    def project(read, head, acc, first, count):
        acc[...] = jnp.zeros((B, E), jnp.float32)
        for j in range(count):
            loads[first + j].wait()
            acc[...] += jnp.dot(read(j), head[pl.ds(j * CH, CH), :], preferred_element_type=jnp.float32)

    def normalize(acc, unit, inv, ref):
        proj = acc[...]
        scale = lax.rsqrt(jnp.sum(proj * proj, axis=-1, keepdims=True) + EPS)
        value = proj * scale
        unit[...] = value
        inv[...] = jnp.broadcast_to(scale, (B, 128))
        ref[6 + core] = value.astype(jnp.bfloat16)

    loads[1].wait()
    project(lambda j: txtf[:, pl.ds(j * CH, CH)], txth, sum_t, 2, DT // CH)
    normalize(sum_t, unit_t, inv_t, texts)
    pl.semaphore_wait(barrier, 12 + 8 - owner_is_me.astype(jnp.int32))
    for half in (0, 1):
        row_send(TXT, texts, half)
    own_send(TXT, texts)
    loads[0].wait()
    send(FEA + 1, fea(0), fea(1), z_mate(-side))
    send(FEA + 3, fea(0), fea(3), z_mate(side))
    project(lambda j: feats[pl.ds(0, B), pl.ds(j * CH, CH)], imgh, sum_i, 10, DI // CH)
    normalize(sum_i, unit_i, inv_i, images)
    own_send(IMG, images)

    temper = jnp.exp(jnp.full((1, 2 * B), ls_ref[0], jnp.float32))
    bias = lb_ref[0]
    rows = lax.broadcasted_iota(jnp.int32, (2 * B, 1), 0)
    acc_i[...] = jnp.zeros((2 * B, E), jnp.float32)
    acc_t[...] = jnp.zeros((2 * B, E), jnp.float32)
    totals = [jnp.zeros((1, B), jnp.float32) for _ in range(3)]
    far_row = jnp.where((rows >= B) == (core == 0), 1.0, 0.0)

    def group(own, ref, numbers, acc, stats):
        offs = [0 if n == 0 else in_row(x, n) if n < 4 else crossed(x, n - 3) for n in numbers]
        wide = B * len(offs)
        block = jnp.concatenate([slot(ref, off)[...] for off in offs], axis=0)
        both = own[6:8].reshape(2 * B, E)
        cosine = lax.dot_general(
            both, block, (((1,), (1,)), ((), ())), preferred_element_type=jnp.float32
        )
        logits = temper[:, :wide] * cosine + bias
        small = jnp.exp(-jnp.abs(logits))
        grad = jnp.where(logits >= 0.0, 1.0, small) / (1.0 + small)
        if numbers == (0,):
            hit = lax.broadcasted_iota(jnp.int32, (2 * B, B), 1) + core * B == rows
            grad = grad - jnp.where(hit, 1.0, 0.0)
        else:
            far = jnp.concatenate(
                [jnp.full((1, B), (off == 6 * core - 3).astype(jnp.float32)) for off in offs], axis=1
            )
            live = 1.0 - far_row * far
            grad = grad * live
        if stats:
            signed = jnp.where(hit, -logits, logits) if numbers == (0,) else logits
            loss = jnp.maximum(signed, 0.0) + jnp.log1p(small)
            if numbers != (0,):
                loss = loss * live
            for k, term in enumerate((loss, grad * cosine, grad)):
                term = jnp.sum(term, axis=0, keepdims=True)
                for n in range(len(offs)):
                    totals[k] = totals[k] + term[:, n * B : (n + 1) * B]
        weights = (temper[:, :wide] * grad).astype(jnp.bfloat16)
        acc[...] += jnp.dot(weights, block, preferred_element_type=jnp.float32)

    def text_group(*numbers):
        group(images, texts, numbers, acc_i, True)

    def image_group(*numbers):
        group(texts, images, numbers, acc_t, False)

    own_wait(IMG, images)
    text_group(0)
    for half in (0, 1):
        for q in (1, 3):
            row_wait(TXT, texts, q, half)
            cross_send(TXT, texts, q, half)
        opposite_send(TXT, texts, half)
    for half in (0, 1):
        row_wait(TXT, texts, 2, half)
        cross_send(TXT, texts, 2, half)
        hand_on(TXT, texts, half)
    row_send(IMG, images, None)
    arrived(FEA + 1, fea(1))
    send(FEA + 2, fea(1), fea(2), z_mate(-side))
    text_group(1, 3)
    text_group(2)
    for q in (1, 3):
        for half in (0, 1):
            cross_wait_rest(TXT, texts, q, half)
    text_group(4, 6)
    for half in (0, 1):
        cross_wait(TXT, texts, 2, half)
    text_group(5)
    sums_send(TXT, acc_i, rcv_i)

    stat[...] = jnp.zeros((8, 2 * B), jnp.float32)
    stat[0:1, 0:B] = totals[0]
    stat[0:1, B : 2 * B] = totals[1]
    stat[1:2, 0:B] = totals[2]
    send(SIB + 2, stat, stats2, sib)
    unit = unit_i[...]
    dunit = sums(TXT, acc_i, rcv_i)
    dproj = inv_i[:, 0:1] * (dunit - unit * jnp.sum(unit * dunit, axis=-1, keepdims=True))
    dlow[...] = dproj

    def window(n):
        return dgat.at[:, pl.ds(n * B, B)]

    for n, off in ((2, -2 * side), (1, -side), (3, side), (0, 0)):
        j = quarter(off)
        turned = dlow[:, pl.ds(pl.multiple_of(j * 256, 256), 256)].T.astype(jnp.bfloat16)
        if n == 0:
            dgat[:, 0:B] = turned
        else:
            dlow_t[n] = turned
            send(DLO + n, dlow_t.at[n], window(n), z_mate(off))
    early, early_if = list(sent), list(sent_if)
    sent.clear()
    sent_if.clear()
    for q in (1, 3):
        row_wait(IMG, images, q, None)
        cross_send(IMG, images, q, None)
    opposite_send(IMG, images, None)
    own_wait(TXT, texts)
    image_group(0)
    image_group(1, 3)

    for n in (1, 2, 3):
        arrived(DLO + n, window(n))
    arrived(FEA + 2, fea(2))
    arrived(FEA + 3, fea(3))

    def part_rows(ref, n):
        return ref.at[pl.ds(pl.multiple_of(n * 384, 384), 384)]

    def product(half, n, ref):
        columns = pl.ds(pl.multiple_of(half * 768 + n * 384, 128), 384)
        part_rows(ref, n)[...] = jnp.dot(
            dgat[...], feats[:, columns], preferred_element_type=jnp.float32
        ).T

    for j, n in enumerate((1 - core, core)):
        product(1 - core, n, part_sib)
        send(SIB + j, part_rows(part_sib, n), part_rows(part_rcv, n), sib)
    for n in (core, 1 - core):
        product(core, n, part)
    arrived(SIB + 2, stats2)
    both = stat[...] + stats2[...]
    for j, n in enumerate((core, 1 - core)):
        arrived(SIB + j, part_rows(part_rcv, n))
        for i in range(8):
            span = pl.ds(pl.multiple_of(n * 384 + i * 48, 16), 48)
            value = part[span, :] + part_rcv[span, :]
            to_y, to_x = 2 * n + i // 4, i % 4
            out_a[to_x, pl.ds(pl.multiple_of(to_y * 32, 32), 32), :] = value[:32, :]
            out_b[to_y, 16 * to_x : 16 * to_x + 16, :] = value[32:, :]
        for i in range(2):
            to_y = 2 * n + i
            o = lax.rem(to_y - y + 4, 4)
            send_if(to_y != y, PLB + o, out_b.at[to_y], in_b.at[o], y_mate(o))
    for n in range(4):
        out_a[n, 128:136, :] = both
    for o in (1, 2, 3):
        send(PLA + o, out_a.at[lax.rem(x + o, 4)], in_a.at[o], x_mate(o))

    row_wait(IMG, images, 2, None)
    cross_send(IMG, images, 2, None)
    hand_on(IMG, images, None)
    image_group(2)
    drain(early, early_if)

    def summed(base, out, at, got):
        for o in (1, 2, 3):
            arrived(base + o, got.at[o])
        return out[at] + got[1] + got[2] + got[3]

    total = summed(PLB, out_b, y, in_b)
    for n in range(4):
        out_b2[n] = total[16 * n : 16 * n + 16, :]
    for o in (1, 2, 3):
        send(PLB + 4 + o, out_b2.at[lax.rem(x + o, 4)], in_b2.at[o], x_mate(o))
    total = summed(PLA, out_a, x, in_a)
    for n in range(4):
        out_a2[n, 0:32, :] = total[32 * n : 32 * n + 32, :]
        out_a2[n, 32:40, :] = total[128:136, :]
    for o in (1, 2, 3):
        send(PLA + 4 + o, out_a2.at[lax.rem(y + o, 4)], in_a2.at[o], y_mate(o))
    total_b = summed(PLB + 4, out_b2, x, in_b2)
    total_a = summed(PLA + 4, out_a2, y, in_a2)
    total = jnp.concatenate([total_a[:32, :], total_b], axis=0)
    for j in range(8):
        tails[j, 0:6, :] = total[6 * j : 6 * j + 6, :]
        tails[j, 6:8, :] = total_a[32:34, :]
    for j in range(8):
        @pl.when(first_owner + j != me)
        def _():
            pltpu.make_async_remote_copy(
                src_ref=tails.at[j], dst_ref=owned.at[z],
                send_sem=send_sem.at[OWN + j], recv_sem=recv_sem.at[OWN + z],
                device_id={"dp": first_owner + j}, device_id_type=pl.DeviceIdType.MESH,
            ).start()

        @pl.when(first_owner + j == me)
        def _():
            owned[z] = tails[j]

    for q in (1, 3):
        cross_wait_rest(IMG, images, q, None)
    image_group(4, 6)
    cross_wait(IMG, images, 2, None)
    image_group(5)
    sums_send(IMG, acc_t, rcv_t)
    unit = unit_t[...]
    dunit = sums(IMG, acc_t, rcv_t)
    tg_ref[...] = dunit - unit * jnp.sum(unit * dunit, axis=-1, keepdims=True)
    tinv_ref[...] = inv_t[...]

    for zz in range(8):
        @pl.when(source(zz) != me)
        def _():
            arrived(OWN + zz, owned.at[zz])
    for n in range(4):
        hg_ref[:, n * 256 : (n + 1) * 256] = owned[n, 0:6, :] + owned[n + 4, 0:6, :]
    st_ref[...] = jnp.sum(owned[...], axis=0)
    for j in range(8):
        @pl.when(first_owner + j != me)
        def _():
            copy(OWN + j, tails.at[j], owned.at[z], first_owner + j).wait_send()
    drain(sent, sent_if)


def finish(ls_ref, st_ref, hgs_ref, tgs_ref, tinv_ref, loss_ref, sg_ref, hg_ref, tg_ref):
    temper = jnp.exp(jnp.full((1, B), ls_ref[0], jnp.float32))
    loss_ref[0] = jnp.sum(st_ref[6:7, 0:B]) / PAIRS
    sg_ref[0] = jnp.sum(st_ref[6:7, B : 2 * B] * temper) / PAIRS
    sg_ref[1] = jnp.sum(st_ref[7:8, 0:B]) / PAIRS
    hg_ref[...] = hgs_ref[...] * (1.0 / B)
    tg_ref[...] = tgs_ref[...] * tinv_ref[:, 0:1]


def shards(img_feats, txt_feats, img_head, txt_head, log_scale, logit_bias):
    f32, bf16 = jnp.float32, jnp.bfloat16
    smem = pl.BlockSpec(memory_space=pltpu.SMEM)
    vmem = pl.BlockSpec(memory_space=pltpu.VMEM)
    hbm = pl.BlockSpec(memory_space=pl.ANY)
    sums = pl.pallas_call(
        kernel,
        out_shape=(
            jax.ShapeDtypeStruct((8, 2 * B), f32),
            jax.ShapeDtypeStruct((6, E), f32),
            jax.ShapeDtypeStruct((B, E), f32),
            jax.ShapeDtypeStruct((B, 128), f32),
        ),
        in_specs=[smem] * 2 + [hbm] * 4,
        out_specs=(vmem,) * 4,
        scratch_shapes=[
            pltpu.VMEM((B, DT), bf16),
            pltpu.VMEM((DI, E), bf16),
            pltpu.VMEM((DT, E), bf16),
            pltpu.VMEM((4 * B, DI), bf16),
            pltpu.VMEM((14, B, E), bf16),
            pltpu.VMEM((14, B, E), bf16),
            pltpu.VMEM((B, E), f32),
            pltpu.VMEM((B, E), f32),
            pltpu.VMEM((2 * B, E), f32),
            pltpu.VMEM((2 * B, E), f32),
            pltpu.VMEM((B, 128), f32),
            pltpu.VMEM((B, 128), f32),
            pltpu.VMEM((B, E), f32),
            pltpu.VMEM((B, E), f32),
            pltpu.VMEM((B, E), f32),
            pltpu.VMEM((B, E), f32),
            pltpu.VMEM((B, E), f32),
            pltpu.VMEM((4, 256, B), bf16),
            pltpu.VMEM((256, 4 * B), bf16),
            pltpu.VMEM((8, 256), f32),
            pltpu.VMEM((8, 256), f32),
            pltpu.VMEM((8, 8, 256), f32),
            pltpu.VMEM((768, 256), f32),
            pltpu.VMEM((768, 256), f32),
            pltpu.VMEM((768, 256), f32),
            pltpu.VMEM((8, 8, 256), f32),
            pltpu.VMEM((4, 136, 256), f32),
            pltpu.VMEM((4, 136, 256), f32),
            pltpu.VMEM((4, 64, 256), f32),
            pltpu.VMEM((4, 64, 256), f32),
            pltpu.VMEM((4, 40, 256), f32),
            pltpu.VMEM((4, 40, 256), f32),
            pltpu.VMEM((4, 16, 256), f32),
            pltpu.VMEM((4, 16, 256), f32),
            pltpu.SemaphoreType.DMA((16,)),
            pltpu.SemaphoreType.DMA((IDS,)),
            pltpu.SemaphoreType.DMA((IDS,)),
        ],
        compiler_params=pltpu.CompilerParams(
            collective_id=0, has_side_effects=True, vmem_limit_bytes=62 * 2**20
        ),
        cost_estimate=pl.CostEstimate(flops=5 * 10**9, bytes_accessed=14 * 10**6, transcendentals=10**6),
        name="contrastive",
    )(log_scale, logit_bias, img_feats, txt_feats, img_head, txt_head)
    loss, scalar_grads, head_grad, text_grad = pl.pallas_call(
        finish,
        out_shape=(
            jax.ShapeDtypeStruct((1,), f32),
            jax.ShapeDtypeStruct((2,), f32),
            jax.ShapeDtypeStruct((6, E), f32),
            jax.ShapeDtypeStruct((B, E), f32),
        ),
        in_specs=[smem] + [vmem] * 4,
        out_specs=(smem, smem, vmem, vmem),
        name="finish",
    )(log_scale, *sums)
    return loss.reshape(()), scalar_grads, head_grad, text_grad


def solution(mesh):
    in_specs = (P("dp", None), P("dp", None), P(), P(), P(), P())
    out_specs = (P(), P(), P("dp", None), P("dp", None))
    return jax.shard_map(shards, mesh=mesh, in_specs=in_specs, out_specs=out_specs, check_vma=False)
```

```python
import jax
import jax.numpy as jnp
from jax import lax
from jax.experimental import pallas as pl
from jax.experimental.pallas import tpu as pltpu
from jax.sharding import PartitionSpec as P

EPS = 1e-06
B = 128
E = 1024
DI = 1536
DT = 4096
N = 256
PAIRS = 54525952
CH = 512

TXT = 0
IMG = 26
FEA = 52
DLO = 56
SIB = 100
PLA = 60
PLB = 68
OWN = 76
IDS = 104
PIECES = ((0, 32), (32, 48), (80, 48))


def kernel(
    ls_ref, lb_ref, imgf_ref, txtf_ref, imgh_ref, txth_ref,
    st_ref, hg_ref, tg_ref, tinv_ref,
    txtf, imgh, txth, feats, texts, images, unit_t, unit_i, acc_t, acc_i, inv_t, inv_i,
    sum_t, sum_i, rcv_t, rcv_i, dlow, dlow_t, dgat, stat, stats2, tails, part_sib, part_rcv, part, owned,
    out_a, in_a, out_b, in_b, out_a2, in_a2, out_b2, in_b2,
    load_sem, send_sem, recv_sem,
):
    me = lax.axis_index("dp")
    core = lax.rem(me, 2)
    spot = lax.rem(me // 2, 16)
    z = me // 32
    x = lax.rem(spot, 4)
    row_first = me - 2 * x
    right_x = lax.rem(x + 1, 4)
    left_x = lax.rem(x + 3, 4)
    right = row_first + 2 * right_x
    left = row_first + 2 * left_x
    inner = (x == 1) | (x == 2)
    up = lax.rem(me + 8, N)
    down = lax.rem(me + N - 8, N)
    sib = me + 1 - 2 * core

    side = 1 - 2 * core

    def z_mate(off):
        return lax.rem(me + 32 * off + N, N)

    def quarter(off):
        return lax.rem(z + off + 8, 4)

    y = spot // 4

    def x_mate(off):
        return row_first + 2 * lax.rem(x + off, 4)

    def y_mate(off):
        return 32 * z + 8 * lax.rem(y + off, 4) + 2 * x + core

    first_owner = 128 * core + 8 * spot
    my_row = me // 8
    src_core = my_row // 16
    src_spot = lax.rem(my_row, 16)

    def source(zz):
        return 32 * zz + 2 * src_spot + src_core

    loads = {}

    def load(i, src, dst):
        loads[i] = pltpu.make_async_copy(src, dst, load_sem.at[i])
        loads[i].start()

    load(0, imgf_ref, feats.at[pl.ds(0, B)])
    load(1, txtf_ref, txtf)
    for j in range(DT // CH):
        load(2 + j, txth_ref.at[pl.ds(j * CH, CH)], txth.at[pl.ds(j * CH, CH)])
    for j in range(DI // CH):
        load(10 + j, imgh_ref.at[pl.ds(j * CH, CH)], imgh.at[pl.ds(j * CH, CH)])

    barrier = pltpu.get_barrier_semaphore()

    def greet(dev):
        pl.semaphore_signal(barrier, inc=1, device_id={"dp": dev}, device_id_type=pl.DeviceIdType.MESH)

    for dev in [right, left, up, down, sib, x_mate(2)] + [z_mate(side), z_mate(2 * side), z_mate(-side)] + [y_mate(o) for o in range(1, 4)]:
        greet(dev)
    for zz in range(8):
        @pl.when(source(zz) != me)
        def _():
            greet(source(zz))

    owner_is_me = (me >= first_owner) & (me < first_owner + 8)

    sent = []
    sent_if = []

    def copy(i, src, dst, dev):
        return pltpu.make_async_remote_copy(
            src_ref=src, dst_ref=dst, send_sem=send_sem.at[i], recv_sem=recv_sem.at[i],
            device_id={"dp": dev}, device_id_type=pl.DeviceIdType.MESH,
        )

    def send(i, src, dst, dev):
        c = copy(i, src, dst, dev)
        c.start()
        sent.append(c)

    def send_if(cond, i, src, dst, dev, landing=None):
        c = pltpu.make_async_remote_copy(
            src_ref=src, dst_ref=dst, send_sem=send_sem.at[i],
            recv_sem=recv_sem.at[i if landing is None else landing],
            device_id={"dp": dev}, device_id_type=pl.DeviceIdType.MESH,
        )

        @pl.when(cond)
        def _():
            c.start()

        sent_if.append((cond, c))

    def drain(always, perhaps):
        for c in always:
            c.wait_send()
        for cond, c in perhaps:
            @pl.when(cond)
            def _():
                c.wait_send()

    def arrived(i, dst):
        copy(i, dst, dst, sib).wait_recv()

    def fea(n):
        return feats.at[pl.ds(n * B, B)]

    def in_row(at, q):
        return q - 4 * (at + q >= 4).astype(jnp.int32)

    def crossed(at, q):
        return q - 4 * (at + q < 4).astype(jnp.int32)

    def slot(ref, off, piece=None):
        if piece is None:
            return ref.at[2 * (3 + off) + core]
        return ref.at[2 * (3 + off) + core, pl.ds(*PIECES[piece])]

    def row_send(base, ref, piece):
        send(base + 6 + (piece or 0), slot(ref, 0, piece), slot(ref, in_row(right_x, 3), piece), right)
        send(base + (piece or 0), slot(ref, 0, piece), slot(ref, in_row(left_x, 1), piece), left)

    def row_wait(base, ref, q, piece):
        arrived(base + 3 * (q - 1) + (piece or 0), slot(ref, in_row(x, q), piece))

    right_on = (x == 3) | ((core == 0) & (x < 2))
    left_on = (x == 0) | ((core == 1) & (x >= 2))

    def opposite_send(base, ref, piece):
        i = base + 3 + (piece or 0)
        send_if(right_on, i, slot(ref, in_row(x, 3), piece), slot(ref, in_row(right_x, 2), piece), right)
        send_if(
            left_on, base + 21 + (piece or 0), slot(ref, in_row(x, 1), piece), slot(ref, in_row(left_x, 2), piece),
            left, i,
        )

    def cross_send(base, ref, q, piece):
        dev = jnp.where(x + q < 4, up, down)
        i = base + 9 + 3 * (q - 1) + (piece or 0)
        src, dst = slot(ref, in_row(x, q), piece), slot(ref, crossed(x, q), piece)
        if q == 2:
            send_if(inner, i, src, dst, dev)
        else:
            send(i, src, dst, dev)

    def cross_wait(base, ref, q, piece):
        arrived(base + 9 + 3 * (q - 1) + (piece or 0), slot(ref, crossed(x, q), piece))

    def cross_wait_rest(base, ref, q, piece):
        @pl.when(x != (q + 1) // 2)
        def _():
            cross_wait(base, ref, q, piece)

    def hand_on(base, ref, piece):
        for at in (1, 2):
            @pl.when(x == at)
            def _():
                cross_wait(base, ref, 2 * at - 1, piece)
        near = jnp.where(inner, x, 1)
        taken = crossed(near, 2 * near - 1)
        to = 3 * (near - 1)
        send_if(
            inner, base + 18 + (piece or 0), slot(ref, taken, piece), slot(ref, crossed(to, 2), piece),
            row_first + 2 * to, base + 12 + (piece or 0),
        )

    def own_rows(ref, of):
        return ref.at[pl.ds(pl.multiple_of(of * B, B), B)]

    def own_send(base, ref):
        send(base + 24, slot(ref, 0), slot(ref, 0), sib)

    def own_wait(base, ref):
        arrived(base + 24, ref.at[7 - core])

    def sums_send(base, acc, rcv):
        send(base + 25, own_rows(acc, 1 - core), rcv, sib)

    def sums(base, acc, rcv):
        arrived(base + 25, rcv)
        return own_rows(acc, core)[...] + rcv[...]

    def project(read, head, acc, first, count):
        acc[...] = jnp.zeros((B, E), jnp.float32)
        for j in range(count):
            loads[first + j].wait()
            acc[...] += jnp.dot(read(j), head[pl.ds(j * CH, CH), :], preferred_element_type=jnp.float32)

    def normalize(acc, unit, inv, ref):
        proj = acc[...]
        scale = lax.rsqrt(jnp.sum(proj * proj, axis=-1, keepdims=True) + EPS)
        value = proj * scale
        unit[...] = value
        inv[...] = jnp.broadcast_to(scale, (B, 128))
        ref[6 + core] = value.astype(jnp.bfloat16)

    loads[1].wait()
    project(lambda j: txtf[:, pl.ds(j * CH, CH)], txth, sum_t, 2, DT // CH)
    normalize(sum_t, unit_t, inv_t, texts)
    pl.semaphore_wait(barrier, 12 + 8 - owner_is_me.astype(jnp.int32))
    for piece in range(len(PIECES)):
        row_send(TXT, texts, piece)
    own_send(TXT, texts)
    loads[0].wait()
    send(FEA + 1, fea(0), fea(1), z_mate(-side))
    send(FEA + 3, fea(0), fea(3), z_mate(side))
    project(lambda j: feats[pl.ds(0, B), pl.ds(j * CH, CH)], imgh, sum_i, 10, DI // CH)
    normalize(sum_i, unit_i, inv_i, images)
    own_send(IMG, images)

    temper = jnp.exp(jnp.full((1, 2 * B), ls_ref[0], jnp.float32))
    bias = lb_ref[0]
    rows = lax.broadcasted_iota(jnp.int32, (2 * B, 1), 0)
    acc_i[...] = jnp.zeros((2 * B, E), jnp.float32)
    acc_t[...] = jnp.zeros((2 * B, E), jnp.float32)
    totals = [jnp.zeros((1, B), jnp.float32) for _ in range(3)]
    far_row = jnp.where((rows >= B) == (core == 0), 1.0, 0.0)

    def group(own, ref, numbers, acc, stats):
        offs = [0 if n == 0 else in_row(x, n) if n < 4 else crossed(x, n - 3) for n in numbers]
        wide = B * len(offs)
        block = jnp.concatenate([slot(ref, off)[...] for off in offs], axis=0)
        both = own[6:8].reshape(2 * B, E)
        cosine = lax.dot_general(
            both, block, (((1,), (1,)), ((), ())), preferred_element_type=jnp.float32
        )
        logits = temper[:, :wide] * cosine + bias
        small = jnp.exp(-jnp.abs(logits))
        grad = jnp.where(logits >= 0.0, 1.0, small) / (1.0 + small)
        if numbers == (0,):
            hit = lax.broadcasted_iota(jnp.int32, (2 * B, B), 1) + core * B == rows
            grad = grad - jnp.where(hit, 1.0, 0.0)
        else:
            far = jnp.concatenate(
                [jnp.full((1, B), (off == 6 * core - 3).astype(jnp.float32)) for off in offs], axis=1
            )
            live = 1.0 - far_row * far
            grad = grad * live
        if stats:
            signed = jnp.where(hit, -logits, logits) if numbers == (0,) else logits
            loss = jnp.maximum(signed, 0.0) + jnp.log1p(small)
            if numbers != (0,):
                loss = loss * live
            for k, term in enumerate((loss, grad * cosine, grad)):
                term = jnp.sum(term, axis=0, keepdims=True)
                for n in range(len(offs)):
                    totals[k] = totals[k] + term[:, n * B : (n + 1) * B]
        weights = (temper[:, :wide] * grad).astype(jnp.bfloat16)
        acc[...] += jnp.dot(weights, block, preferred_element_type=jnp.float32)

    def text_group(*numbers):
        group(images, texts, numbers, acc_i, True)

    def image_group(*numbers):
        group(texts, images, numbers, acc_t, False)

    own_wait(IMG, images)
    text_group(0)
    for piece in range(len(PIECES)):
        for q in (1, 3):
            row_wait(TXT, texts, q, piece)
            cross_send(TXT, texts, q, piece)
        opposite_send(TXT, texts, piece)
    for piece in range(len(PIECES)):
        row_wait(TXT, texts, 2, piece)
        cross_send(TXT, texts, 2, piece)
        hand_on(TXT, texts, piece)
    row_send(IMG, images, None)
    arrived(FEA + 1, fea(1))
    send(FEA + 2, fea(1), fea(2), z_mate(-side))
    text_group(1, 3)
    text_group(2)
    for q in (1, 3):
        for piece in range(len(PIECES)):
            cross_wait_rest(TXT, texts, q, piece)
    text_group(4, 6)
    for piece in range(len(PIECES)):
        cross_wait(TXT, texts, 2, piece)
    text_group(5)
    sums_send(TXT, acc_i, rcv_i)

    stat[...] = jnp.zeros((8, 2 * B), jnp.float32)
    stat[0:1, 0:B] = totals[0]
    stat[0:1, B : 2 * B] = totals[1]
    stat[1:2, 0:B] = totals[2]
    send(SIB + 2, stat, stats2, sib)
    unit = unit_i[...]
    dunit = sums(TXT, acc_i, rcv_i)
    dproj = inv_i[:, 0:1] * (dunit - unit * jnp.sum(unit * dunit, axis=-1, keepdims=True))
    dlow[...] = dproj

    def window(n):
        return dgat.at[:, pl.ds(n * B, B)]

    for n, off in ((2, -2 * side), (1, -side), (3, side), (0, 0)):
        j = quarter(off)
        turned = dlow[:, pl.ds(pl.multiple_of(j * 256, 256), 256)].T.astype(jnp.bfloat16)
        if n == 0:
            dgat[:, 0:B] = turned
        else:
            dlow_t[n] = turned
            send(DLO + n, dlow_t.at[n], window(n), z_mate(off))
    early, early_if = list(sent), list(sent_if)
    sent.clear()
    sent_if.clear()
    for q in (1, 3):
        row_wait(IMG, images, q, None)
        cross_send(IMG, images, q, None)
    opposite_send(IMG, images, None)
    own_wait(TXT, texts)
    image_group(0)
    image_group(1, 3)

    for n in (1, 2, 3):
        arrived(DLO + n, window(n))
    arrived(FEA + 2, fea(2))
    arrived(FEA + 3, fea(3))

    def part_rows(ref, n):
        return ref.at[pl.ds(pl.multiple_of(n * 384, 384), 384)]

    def product(piece, n, ref):
        columns = pl.ds(pl.multiple_of(piece * 768 + n * 384, 128), 384)
        part_rows(ref, n)[...] = jnp.dot(
            dgat[...], feats[:, columns], preferred_element_type=jnp.float32
        ).T

    for j, n in enumerate((1 - core, core)):
        product(1 - core, n, part_sib)
        send(SIB + j, part_rows(part_sib, n), part_rows(part_rcv, n), sib)
    for n in (core, 1 - core):
        product(core, n, part)
    arrived(SIB + 2, stats2)
    both = stat[...] + stats2[...]
    for j, n in enumerate((core, 1 - core)):
        arrived(SIB + j, part_rows(part_rcv, n))
        for i in range(8):
            span = pl.ds(pl.multiple_of(n * 384 + i * 48, 16), 48)
            value = part[span, :] + part_rcv[span, :]
            to_y, to_x = 2 * n + i // 4, i % 4
            out_a[to_x, pl.ds(pl.multiple_of(to_y * 32, 32), 32), :] = value[:32, :]
            out_b[to_y, 16 * to_x : 16 * to_x + 16, :] = value[32:, :]
        for i in range(2):
            to_y = 2 * n + i
            o = lax.rem(to_y - y + 4, 4)
            send_if(to_y != y, PLB + o, out_b.at[to_y], in_b.at[o], y_mate(o))
    for n in range(4):
        out_a[n, 128:136, :] = both
    for o in (1, 2, 3):
        send(PLA + o, out_a.at[lax.rem(x + o, 4)], in_a.at[o], x_mate(o))

    row_wait(IMG, images, 2, None)
    cross_send(IMG, images, 2, None)
    hand_on(IMG, images, None)
    image_group(2)
    drain(early, early_if)

    def summed(base, out, at, got):
        for o in (1, 2, 3):
            arrived(base + o, got.at[o])
        return out[at] + got[1] + got[2] + got[3]

    total = summed(PLB, out_b, y, in_b)
    for n in range(4):
        out_b2[n] = total[16 * n : 16 * n + 16, :]
    for o in (1, 2, 3):
        send(PLB + 4 + o, out_b2.at[lax.rem(x + o, 4)], in_b2.at[o], x_mate(o))
    total = summed(PLA, out_a, x, in_a)
    for n in range(4):
        out_a2[n, 0:32, :] = total[32 * n : 32 * n + 32, :]
        out_a2[n, 32:40, :] = total[128:136, :]
    for o in (1, 2, 3):
        send(PLA + 4 + o, out_a2.at[lax.rem(y + o, 4)], in_a2.at[o], y_mate(o))
    total_b = summed(PLB + 4, out_b2, x, in_b2)
    total_a = summed(PLA + 4, out_a2, y, in_a2)
    total = jnp.concatenate([total_a[:32, :], total_b], axis=0)
    for j in range(8):
        tails[j, 0:6, :] = total[6 * j : 6 * j + 6, :]
        tails[j, 6:8, :] = total_a[32:34, :]
    for j in range(8):
        @pl.when(first_owner + j != me)
        def _():
            pltpu.make_async_remote_copy(
                src_ref=tails.at[j], dst_ref=owned.at[z],
                send_sem=send_sem.at[OWN + j], recv_sem=recv_sem.at[OWN + z],
                device_id={"dp": first_owner + j}, device_id_type=pl.DeviceIdType.MESH,
            ).start()

        @pl.when(first_owner + j == me)
        def _():
            owned[z] = tails[j]

    for q in (1, 3):
        cross_wait_rest(IMG, images, q, None)
    image_group(4, 6)
    cross_wait(IMG, images, 2, None)
    image_group(5)
    sums_send(IMG, acc_t, rcv_t)
    unit = unit_t[...]
    dunit = sums(IMG, acc_t, rcv_t)
    tg_ref[...] = dunit - unit * jnp.sum(unit * dunit, axis=-1, keepdims=True)
    tinv_ref[...] = inv_t[...]

    for zz in range(8):
        @pl.when(source(zz) != me)
        def _():
            arrived(OWN + zz, owned.at[zz])
    for n in range(4):
        hg_ref[:, n * 256 : (n + 1) * 256] = owned[n, 0:6, :] + owned[n + 4, 0:6, :]
    st_ref[...] = jnp.sum(owned[...], axis=0)
    for j in range(8):
        @pl.when(first_owner + j != me)
        def _():
            copy(OWN + j, tails.at[j], owned.at[z], first_owner + j).wait_send()
    drain(sent, sent_if)


def finish(ls_ref, st_ref, hgs_ref, tgs_ref, tinv_ref, loss_ref, sg_ref, hg_ref, tg_ref):
    temper = jnp.exp(jnp.full((1, B), ls_ref[0], jnp.float32))
    loss_ref[0] = jnp.sum(st_ref[6:7, 0:B]) / PAIRS
    sg_ref[0] = jnp.sum(st_ref[6:7, B : 2 * B] * temper) / PAIRS
    sg_ref[1] = jnp.sum(st_ref[7:8, 0:B]) / PAIRS
    hg_ref[...] = hgs_ref[...] * (1.0 / B)
    tg_ref[...] = tgs_ref[...] * tinv_ref[:, 0:1]


def shards(img_feats, txt_feats, img_head, txt_head, log_scale, logit_bias):
    f32, bf16 = jnp.float32, jnp.bfloat16
    smem = pl.BlockSpec(memory_space=pltpu.SMEM)
    vmem = pl.BlockSpec(memory_space=pltpu.VMEM)
    hbm = pl.BlockSpec(memory_space=pl.ANY)
    sums = pl.pallas_call(
        kernel,
        out_shape=(
            jax.ShapeDtypeStruct((8, 2 * B), f32),
            jax.ShapeDtypeStruct((6, E), f32),
            jax.ShapeDtypeStruct((B, E), f32),
            jax.ShapeDtypeStruct((B, 128), f32),
        ),
        in_specs=[smem] * 2 + [hbm] * 4,
        out_specs=(vmem,) * 4,
        scratch_shapes=[
            pltpu.VMEM((B, DT), bf16),
            pltpu.VMEM((DI, E), bf16),
            pltpu.VMEM((DT, E), bf16),
            pltpu.VMEM((4 * B, DI), bf16),
            pltpu.VMEM((14, B, E), bf16),
            pltpu.VMEM((14, B, E), bf16),
            pltpu.VMEM((B, E), f32),
            pltpu.VMEM((B, E), f32),
            pltpu.VMEM((2 * B, E), f32),
            pltpu.VMEM((2 * B, E), f32),
            pltpu.VMEM((B, 128), f32),
            pltpu.VMEM((B, 128), f32),
            pltpu.VMEM((B, E), f32),
            pltpu.VMEM((B, E), f32),
            pltpu.VMEM((B, E), f32),
            pltpu.VMEM((B, E), f32),
            pltpu.VMEM((B, E), f32),
            pltpu.VMEM((4, 256, B), bf16),
            pltpu.VMEM((256, 4 * B), bf16),
            pltpu.VMEM((8, 256), f32),
            pltpu.VMEM((8, 256), f32),
            pltpu.VMEM((8, 8, 256), f32),
            pltpu.VMEM((768, 256), f32),
            pltpu.VMEM((768, 256), f32),
            pltpu.VMEM((768, 256), f32),
            pltpu.VMEM((8, 8, 256), f32),
            pltpu.VMEM((4, 136, 256), f32),
            pltpu.VMEM((4, 136, 256), f32),
            pltpu.VMEM((4, 64, 256), f32),
            pltpu.VMEM((4, 64, 256), f32),
            pltpu.VMEM((4, 40, 256), f32),
            pltpu.VMEM((4, 40, 256), f32),
            pltpu.VMEM((4, 16, 256), f32),
            pltpu.VMEM((4, 16, 256), f32),
            pltpu.SemaphoreType.DMA((16,)),
            pltpu.SemaphoreType.DMA((IDS,)),
            pltpu.SemaphoreType.DMA((IDS,)),
        ],
        compiler_params=pltpu.CompilerParams(
            collective_id=0, has_side_effects=True, vmem_limit_bytes=62 * 2**20
        ),
        cost_estimate=pl.CostEstimate(flops=5 * 10**9, bytes_accessed=14 * 10**6, transcendentals=10**6),
        name="contrastive",
    )(log_scale, logit_bias, img_feats, txt_feats, img_head, txt_head)
    loss, scalar_grads, head_grad, text_grad = pl.pallas_call(
        finish,
        out_shape=(
            jax.ShapeDtypeStruct((1,), f32),
            jax.ShapeDtypeStruct((2,), f32),
            jax.ShapeDtypeStruct((6, E), f32),
            jax.ShapeDtypeStruct((B, E), f32),
        ),
        in_specs=[smem] + [vmem] * 4,
        out_specs=(smem, smem, vmem, vmem),
        name="finish",
    )(log_scale, *sums)
    return loss.reshape(()), scalar_grads, head_grad, text_grad


def solution(mesh):
    in_specs = (P("dp", None), P("dp", None), P(), P(), P(), P())
    out_specs = (P(), P(), P("dp", None), P("dp", None))
    return jax.shard_map(shards, mesh=mesh, in_specs=in_specs, out_specs=out_specs, check_vma=False)
```

```python
import jax
import jax.numpy as jnp
from jax import lax
from jax.experimental import pallas as pl
from jax.experimental.pallas import tpu as pltpu
from jax.sharding import PartitionSpec as P

EPS = 1e-06
B = 128
E = 1024
DI = 1536
DT = 4096
N = 256
PAIRS = 54525952
CH = 512

TXT = 0
IMG = 24
FEA = 48
DLO = 52
SIB = 56
PLA = 60
PLB = 68
OWN = 76
IDS = 84


def kernel(
    ls_ref, lb_ref, imgf_ref, txtf_ref, imgh_ref, txth_ref,
    st_ref, hg_ref, tg_ref, tinv_ref,
    txtf, imgh, txth, feats, texts, images, unit_t, unit_i, acc_t, acc_i, inv_t, inv_i,
    sum_t, sum_i, rcv_t, rcv_i, dlow, dlow_t, dgat, stat, stats2, tails, part_sib, part_rcv, part, owned,
    out_a, in_a, out_b, in_b, out_a2, in_a2, out_b2, in_b2,
    load_sem, send_sem, recv_sem,
):
    me = lax.axis_index("dp")
    core = lax.rem(me, 2)
    spot = lax.rem(me // 2, 16)
    z = me // 32
    x = lax.rem(spot, 4)
    row_first = me - 2 * x
    right_x = lax.rem(x + 1, 4)
    left_x = lax.rem(x + 3, 4)
    right = row_first + 2 * right_x
    left = row_first + 2 * left_x
    inner = (x == 1) | (x == 2)
    up = lax.rem(me + 8, N)
    down = lax.rem(me + N - 8, N)
    sib = me + 1 - 2 * core

    side = 1 - 2 * core

    def z_mate(off):
        return lax.rem(me + 32 * off + N, N)

    def quarter(off):
        return lax.rem(z + off + 8, 4)

    y = spot // 4

    def x_mate(off):
        return row_first + 2 * lax.rem(x + off, 4)

    def y_mate(off):
        return 32 * z + 8 * lax.rem(y + off, 4) + 2 * x + core

    first_owner = 128 * core + 8 * spot
    my_row = me // 8
    src_core = my_row // 16
    src_spot = lax.rem(my_row, 16)

    def source(zz):
        return 32 * zz + 2 * src_spot + src_core

    loads = {}

    def load(i, src, dst):
        loads[i] = pltpu.make_async_copy(src, dst, load_sem.at[i])
        loads[i].start()

    load(0, imgf_ref, feats.at[pl.ds(0, B)])
    load(1, txtf_ref, txtf)
    for j in range(DT // CH):
        load(2 + j, txth_ref.at[pl.ds(j * CH, CH)], txth.at[pl.ds(j * CH, CH)])
    for j in range(DI // CH):
        load(10 + j, imgh_ref.at[pl.ds(j * CH, CH)], imgh.at[pl.ds(j * CH, CH)])

    barrier = pltpu.get_barrier_semaphore()

    def greet(dev):
        pl.semaphore_signal(barrier, inc=1, device_id={"dp": dev}, device_id_type=pl.DeviceIdType.MESH)

    for dev in [right, left, up, down, sib, x_mate(2)] + [z_mate(side), z_mate(2 * side), z_mate(-side)] + [y_mate(o) for o in range(1, 4)]:
        greet(dev)
    for zz in range(8):
        @pl.when(source(zz) != me)
        def _():
            greet(source(zz))

    owner_is_me = (me >= first_owner) & (me < first_owner + 8)

    sent = []
    sent_if = []

    def copy(i, src, dst, dev):
        return pltpu.make_async_remote_copy(
            src_ref=src, dst_ref=dst, send_sem=send_sem.at[i], recv_sem=recv_sem.at[i],
            device_id={"dp": dev}, device_id_type=pl.DeviceIdType.MESH,
        )

    def send(i, src, dst, dev):
        c = copy(i, src, dst, dev)
        c.start()
        sent.append(c)

    def send_if(cond, i, src, dst, dev, landing=None):
        c = pltpu.make_async_remote_copy(
            src_ref=src, dst_ref=dst, send_sem=send_sem.at[i],
            recv_sem=recv_sem.at[i if landing is None else landing],
            device_id={"dp": dev}, device_id_type=pl.DeviceIdType.MESH,
        )

        @pl.when(cond)
        def _():
            c.start()

        sent_if.append((cond, c))

    def drain(always, perhaps):
        for c in always:
            c.wait_send()
        for cond, c in perhaps:
            @pl.when(cond)
            def _():
                c.wait_send()

    def arrived(i, dst):
        copy(i, dst, dst, sib).wait_recv()

    def fea(n):
        return feats.at[pl.ds(n * B, B)]

    def in_row(at, q):
        return q - 4 * (at + q >= 4).astype(jnp.int32)

    def crossed(at, q):
        return q - 4 * (at + q < 4).astype(jnp.int32)

    def slot(ref, off, half=None):
        if half is None:
            return ref.at[2 * (3 + off) + core]
        return ref.at[2 * (3 + off) + core, pl.ds(half * (B // 2), B // 2)]

    def row_send(base, ref, half):
        send(base + 4 + (half or 0), slot(ref, 0, half), slot(ref, in_row(right_x, 3), half), right)
        send(base + (half or 0), slot(ref, 0, half), slot(ref, in_row(left_x, 1), half), left)

    def row_wait(base, ref, q, half):
        arrived(base + 2 * (q - 1) + (half or 0), slot(ref, in_row(x, q), half))

    right_on = (x == 3) | ((core == 0) & (x < 2))
    left_on = (x == 0) | ((core == 1) & (x >= 2))

    def opposite_send(base, ref, half):
        i = base + 2 + (half or 0)
        send_if(right_on, i, slot(ref, in_row(x, 3), half), slot(ref, in_row(right_x, 2), half), right)
        send_if(
            left_on, base + 21 + (half or 0), slot(ref, in_row(x, 1), half), slot(ref, in_row(left_x, 2), half),
            left, i,
        )

    def cross_send(base, ref, q, half):
        dev = jnp.where(x + q < 4, up, down)
        i = base + 6 + 2 * (q - 1) + (half or 0)
        src, dst = slot(ref, in_row(x, q), half), slot(ref, crossed(x, q), half)
        if q == 2:
            send_if(inner, i, src, dst, dev)
        else:
            send(i, src, dst, dev)

    def cross_wait(base, ref, q, half):
        arrived(base + 6 + 2 * (q - 1) + (half or 0), slot(ref, crossed(x, q), half))

    def cross_wait_rest(base, ref, q, half):
        @pl.when(x != (q + 1) // 2)
        def _():
            cross_wait(base, ref, q, half)

    def hand_on(base, ref, half):
        for at in (1, 2):
            @pl.when(x == at)
            def _():
                cross_wait(base, ref, 2 * at - 1, half)
        near = jnp.where(inner, x, 1)
        taken = crossed(near, 2 * near - 1)
        to = 3 * (near - 1)
        send_if(
            inner, base + 12 + (half or 0), slot(ref, taken, half), slot(ref, crossed(to, 2), half),
            row_first + 2 * to, base + 8 + (half or 0),
        )

    def own_rows(ref, of):
        return ref.at[pl.ds(pl.multiple_of(of * B, B), B)]

    def own_send(base, ref):
        send(base + 14, slot(ref, 0), slot(ref, 0), sib)

    def own_wait(base, ref):
        arrived(base + 14, ref.at[7 - core])

    def sums_send(base, acc, rcv):
        send(base + 15, own_rows(acc, 1 - core), rcv, sib)

    def sums(base, acc, rcv):
        arrived(base + 15, rcv)
        return own_rows(acc, core)[...] + rcv[...]

    def project(read, head, acc, first, count):
        acc[...] = jnp.zeros((B, E), jnp.float32)
        for j in range(count):
            loads[first + j].wait()
            acc[...] += jnp.dot(read(j), head[pl.ds(j * CH, CH), :], preferred_element_type=jnp.float32)

    def normalize(acc, unit, inv, ref):
        proj = acc[...]
        scale = lax.rsqrt(jnp.sum(proj * proj, axis=-1, keepdims=True) + EPS)
        value = proj * scale
        unit[...] = value
        inv[...] = jnp.broadcast_to(scale, (B, 128))
        ref[6 + core] = value.astype(jnp.bfloat16)

    loads[1].wait()
    project(lambda j: txtf[:, pl.ds(j * CH, CH)], txth, sum_t, 2, DT // CH)
    normalize(sum_t, unit_t, inv_t, texts)
    pl.semaphore_wait(barrier, 12 + 8 - owner_is_me.astype(jnp.int32))
    for half in (0, 1):
        row_send(TXT, texts, half)
    own_send(TXT, texts)
    loads[0].wait()
    send(FEA + 1, fea(0), fea(1), z_mate(-side))
    send(FEA + 3, fea(0), fea(3), z_mate(side))
    project(lambda j: feats[pl.ds(0, B), pl.ds(j * CH, CH)], imgh, sum_i, 10, DI // CH)
    normalize(sum_i, unit_i, inv_i, images)
    own_send(IMG, images)

    temper = jnp.exp(jnp.full((1, 2 * B), ls_ref[0], jnp.float32))
    bias = lb_ref[0]
    rows = lax.broadcasted_iota(jnp.int32, (2 * B, 1), 0)
    acc_i[...] = jnp.zeros((2 * B, E), jnp.float32)
    acc_t[...] = jnp.zeros((2 * B, E), jnp.float32)
    totals = [jnp.zeros((1, B), jnp.float32) for _ in range(3)]
    far_row = jnp.where((rows >= B) == (core == 0), 1.0, 0.0)

    def group(own, ref, numbers, acc, stats):
        offs = [0 if n == 0 else in_row(x, n) if n < 4 else crossed(x, n - 3) for n in numbers]
        wide = B * len(offs)
        block = jnp.concatenate([slot(ref, off)[...] for off in offs], axis=0)
        both = own[6:8].reshape(2 * B, E)
        cosine = lax.dot_general(
            both, block, (((1,), (1,)), ((), ())), preferred_element_type=jnp.float32
        )
        logits = temper[:, :wide] * cosine + bias
        small = jnp.exp(-jnp.abs(logits))
        grad = jnp.where(logits >= 0.0, 1.0, small) / (1.0 + small)
        if numbers == (0,):
            hit = lax.broadcasted_iota(jnp.int32, (2 * B, B), 1) + core * B == rows
            grad = grad - jnp.where(hit, 1.0, 0.0)
        else:
            far = jnp.concatenate(
                [jnp.full((1, B), (off == 6 * core - 3).astype(jnp.float32)) for off in offs], axis=1
            )
            live = 1.0 - far_row * far
            grad = grad * live
        if stats:
            signed = jnp.where(hit, -logits, logits) if numbers == (0,) else logits
            loss = jnp.maximum(signed, 0.0) + jnp.log1p(small)
            if numbers != (0,):
                loss = loss * live
            for k, term in enumerate((loss, grad * cosine, grad)):
                term = jnp.sum(term, axis=0, keepdims=True)
                for n in range(len(offs)):
                    totals[k] = totals[k] + term[:, n * B : (n + 1) * B]
        weights = (temper[:, :wide] * grad).astype(jnp.bfloat16)
        acc[...] += jnp.dot(weights, block, preferred_element_type=jnp.float32)

    def text_group(*numbers):
        group(images, texts, numbers, acc_i, True)

    def image_group(*numbers):
        group(texts, images, numbers, acc_t, False)

    own_wait(IMG, images)
    text_group(0)
    for half in (0, 1):
        for q in (1, 3):
            row_wait(TXT, texts, q, half)
            cross_send(TXT, texts, q, half)
        opposite_send(TXT, texts, half)
    for half in (0, 1):
        row_wait(TXT, texts, 2, half)
        cross_send(TXT, texts, 2, half)
        hand_on(TXT, texts, half)
    row_send(IMG, images, None)
    arrived(FEA + 1, fea(1))
    send(FEA + 2, fea(1), fea(2), z_mate(-side))
    text_group(1, 3)
    text_group(2)
    for q in (1, 3):
        for half in (0, 1):
            cross_wait_rest(TXT, texts, q, half)
    text_group(4, 6)
    for half in (0, 1):
        cross_wait(TXT, texts, 2, half)
    text_group(5)
    sums_send(TXT, acc_i, rcv_i)

    stat[...] = jnp.zeros((8, 2 * B), jnp.float32)
    stat[0:1, 0:B] = totals[0]
    stat[0:1, B : 2 * B] = totals[1]
    stat[1:2, 0:B] = totals[2]
    send(SIB + 2, stat, stats2, sib)
    unit = unit_i[...]
    dunit = sums(TXT, acc_i, rcv_i)
    dproj = inv_i[:, 0:1] * (dunit - unit * jnp.sum(unit * dunit, axis=-1, keepdims=True))
    dlow[...] = dproj

    def window(n):
        return dgat.at[:, pl.ds(n * B, B)]

    for n, off in ((2, -2 * side), (1, -side), (3, side), (0, 0)):
        j = quarter(off)
        turned = dlow[:, pl.ds(pl.multiple_of(j * 256, 256), 256)].T.astype(jnp.bfloat16)
        if n == 0:
            dgat[:, 0:B] = turned
        else:
            dlow_t[n] = turned
            send(DLO + n, dlow_t.at[n], window(n), z_mate(off))
    early, early_if = list(sent), list(sent_if)
    sent.clear()
    sent_if.clear()
    for q in (1, 3):
        row_wait(IMG, images, q, None)
        cross_send(IMG, images, q, None)
    opposite_send(IMG, images, None)
    own_wait(TXT, texts)
    image_group(0)

    for n in (1, 2, 3):
        arrived(DLO + n, window(n))
    arrived(FEA + 2, fea(2))
    arrived(FEA + 3, fea(3))

    def part_rows(ref, n):
        return ref.at[pl.ds(pl.multiple_of(n * 384, 384), 384)]

    def product(half, n, ref):
        columns = pl.ds(pl.multiple_of(half * 768 + n * 384, 128), 384)
        part_rows(ref, n)[...] = jnp.dot(
            dgat[...], feats[:, columns], preferred_element_type=jnp.float32
        ).T

    for j, n in enumerate((1 - core, core)):
        product(1 - core, n, part_sib)
        send(SIB + j, part_rows(part_sib, n), part_rows(part_rcv, n), sib)
    for n in (core, 1 - core):
        product(core, n, part)
    arrived(SIB + 2, stats2)
    both = stat[...] + stats2[...]
    for j, n in enumerate((core, 1 - core)):
        arrived(SIB + j, part_rows(part_rcv, n))
        for i in range(8):
            span = pl.ds(pl.multiple_of(n * 384 + i * 48, 16), 48)
            value = part[span, :] + part_rcv[span, :]
            to_y, to_x = 2 * n + i // 4, i % 4
            out_a[to_x, pl.ds(pl.multiple_of(to_y * 32, 32), 32), :] = value[:32, :]
            out_b[to_y, 16 * to_x : 16 * to_x + 16, :] = value[32:, :]
        for i in range(2):
            to_y = 2 * n + i
            o = lax.rem(to_y - y + 4, 4)
            send_if(to_y != y, PLB + o, out_b.at[to_y], in_b.at[o], y_mate(o))
    for n in range(4):
        out_a[n, 128:136, :] = both
    for o in (1, 2, 3):
        send(PLA + o, out_a.at[lax.rem(x + o, 4)], in_a.at[o], x_mate(o))

    row_wait(IMG, images, 2, None)
    cross_send(IMG, images, 2, None)
    hand_on(IMG, images, None)
    image_group(1, 3)
    image_group(2)
    drain(early, early_if)

    def summed(base, out, at, got):
        for o in (1, 2, 3):
            arrived(base + o, got.at[o])
        return out[at] + got[1] + got[2] + got[3]

    total = summed(PLB, out_b, y, in_b)
    for n in range(4):
        out_b2[n] = total[16 * n : 16 * n + 16, :]
    for o in (1, 2, 3):
        send(PLB + 4 + o, out_b2.at[lax.rem(x + o, 4)], in_b2.at[o], x_mate(o))
    total = summed(PLA, out_a, x, in_a)
    for n in range(4):
        out_a2[n, 0:32, :] = total[32 * n : 32 * n + 32, :]
        out_a2[n, 32:40, :] = total[128:136, :]
    for o in (1, 2, 3):
        send(PLA + 4 + o, out_a2.at[lax.rem(y + o, 4)], in_a2.at[o], y_mate(o))
    for q in (1, 3):
        cross_wait_rest(IMG, images, q, None)
    image_group(4, 6)
    total_b = summed(PLB + 4, out_b2, x, in_b2)
    total_a = summed(PLA + 4, out_a2, y, in_a2)
    total = jnp.concatenate([total_a[:32, :], total_b], axis=0)
    for j in range(8):
        tails[j, 0:6, :] = total[6 * j : 6 * j + 6, :]
        tails[j, 6:8, :] = total_a[32:34, :]
    for j in range(8):
        @pl.when(first_owner + j != me)
        def _():
            pltpu.make_async_remote_copy(
                src_ref=tails.at[j], dst_ref=owned.at[z],
                send_sem=send_sem.at[OWN + j], recv_sem=recv_sem.at[OWN + z],
                device_id={"dp": first_owner + j}, device_id_type=pl.DeviceIdType.MESH,
            ).start()

        @pl.when(first_owner + j == me)
        def _():
            owned[z] = tails[j]

    cross_wait(IMG, images, 2, None)
    image_group(5)
    sums_send(IMG, acc_t, rcv_t)
    unit = unit_t[...]
    dunit = sums(IMG, acc_t, rcv_t)
    tg_ref[...] = dunit - unit * jnp.sum(unit * dunit, axis=-1, keepdims=True)
    tinv_ref[...] = inv_t[...]

    for zz in range(8):
        @pl.when(source(zz) != me)
        def _():
            arrived(OWN + zz, owned.at[zz])
    for n in range(4):
        hg_ref[:, n * 256 : (n + 1) * 256] = owned[n, 0:6, :] + owned[n + 4, 0:6, :]
    st_ref[...] = jnp.sum(owned[...], axis=0)
    for j in range(8):
        @pl.when(first_owner + j != me)
        def _():
            copy(OWN + j, tails.at[j], owned.at[z], first_owner + j).wait_send()
    drain(sent, sent_if)


def finish(ls_ref, st_ref, hgs_ref, tgs_ref, tinv_ref, loss_ref, sg_ref, hg_ref, tg_ref):
    temper = jnp.exp(jnp.full((1, B), ls_ref[0], jnp.float32))
    loss_ref[0] = jnp.sum(st_ref[6:7, 0:B]) / PAIRS
    sg_ref[0] = jnp.sum(st_ref[6:7, B : 2 * B] * temper) / PAIRS
    sg_ref[1] = jnp.sum(st_ref[7:8, 0:B]) / PAIRS
    hg_ref[...] = hgs_ref[...] * (1.0 / B)
    tg_ref[...] = tgs_ref[...] * tinv_ref[:, 0:1]


def shards(img_feats, txt_feats, img_head, txt_head, log_scale, logit_bias):
    f32, bf16 = jnp.float32, jnp.bfloat16
    smem = pl.BlockSpec(memory_space=pltpu.SMEM)
    vmem = pl.BlockSpec(memory_space=pltpu.VMEM)
    hbm = pl.BlockSpec(memory_space=pl.ANY)
    sums = pl.pallas_call(
        kernel,
        out_shape=(
            jax.ShapeDtypeStruct((8, 2 * B), f32),
            jax.ShapeDtypeStruct((6, E), f32),
            jax.ShapeDtypeStruct((B, E), f32),
            jax.ShapeDtypeStruct((B, 128), f32),
        ),
        in_specs=[smem] * 2 + [hbm] * 4,
        out_specs=(vmem,) * 4,
        scratch_shapes=[
            pltpu.VMEM((B, DT), bf16),
            pltpu.VMEM((DI, E), bf16),
            pltpu.VMEM((DT, E), bf16),
            pltpu.VMEM((4 * B, DI), bf16),
            pltpu.VMEM((14, B, E), bf16),
            pltpu.VMEM((14, B, E), bf16),
            pltpu.VMEM((B, E), f32),
            pltpu.VMEM((B, E), f32),
            pltpu.VMEM((2 * B, E), f32),
            pltpu.VMEM((2 * B, E), f32),
            pltpu.VMEM((B, 128), f32),
            pltpu.VMEM((B, 128), f32),
            pltpu.VMEM((B, E), f32),
            pltpu.VMEM((B, E), f32),
            pltpu.VMEM((B, E), f32),
            pltpu.VMEM((B, E), f32),
            pltpu.VMEM((B, E), f32),
            pltpu.VMEM((4, 256, B), bf16),
            pltpu.VMEM((256, 4 * B), bf16),
            pltpu.VMEM((8, 256), f32),
            pltpu.VMEM((8, 256), f32),
            pltpu.VMEM((8, 8, 256), f32),
            pltpu.VMEM((768, 256), f32),
            pltpu.VMEM((768, 256), f32),
            pltpu.VMEM((768, 256), f32),
            pltpu.VMEM((8, 8, 256), f32),
            pltpu.VMEM((4, 136, 256), f32),
            pltpu.VMEM((4, 136, 256), f32),
            pltpu.VMEM((4, 64, 256), f32),
            pltpu.VMEM((4, 64, 256), f32),
            pltpu.VMEM((4, 40, 256), f32),
            pltpu.VMEM((4, 40, 256), f32),
            pltpu.VMEM((4, 16, 256), f32),
            pltpu.VMEM((4, 16, 256), f32),
            pltpu.SemaphoreType.DMA((16,)),
            pltpu.SemaphoreType.DMA((IDS,)),
            pltpu.SemaphoreType.DMA((IDS,)),
        ],
        compiler_params=pltpu.CompilerParams(
            collective_id=0, has_side_effects=True, vmem_limit_bytes=62 * 2**20
        ),
        cost_estimate=pl.CostEstimate(flops=5 * 10**9, bytes_accessed=14 * 10**6, transcendentals=10**6),
        name="contrastive",
    )(log_scale, logit_bias, img_feats, txt_feats, img_head, txt_head)
    loss, scalar_grads, head_grad, text_grad = pl.pallas_call(
        finish,
        out_shape=(
            jax.ShapeDtypeStruct((1,), f32),
            jax.ShapeDtypeStruct((2,), f32),
            jax.ShapeDtypeStruct((6, E), f32),
            jax.ShapeDtypeStruct((B, E), f32),
        ),
        in_specs=[smem] + [vmem] * 4,
        out_specs=(smem, smem, vmem, vmem),
        name="finish",
    )(log_scale, *sums)
    return loss.reshape(()), scalar_grads, head_grad, text_grad


def solution(mesh):
    in_specs = (P("dp", None), P("dp", None), P(), P(), P(), P())
    out_specs = (P(), P(), P("dp", None), P("dp", None))
    return jax.shard_map(shards, mesh=mesh, in_specs=in_specs, out_specs=out_specs, check_vma=False)
```

```python
import jax
import jax.numpy as jnp
from jax import lax
from jax.experimental import pallas as pl
from jax.experimental.pallas import tpu as pltpu
from jax.sharding import PartitionSpec as P

EPS = 1e-06
B = 128
E = 1024
DI = 1536
DT = 4096
N = 256
PAIRS = 54525952
CH = 512

TXT = 0
IMG = 24
FEA = 48
DLO = 52
SIB = 56
PLA = 60
PLB = 68
OWN = 76
IDS = 84


def kernel(
    ls_ref, lb_ref, imgf_ref, txtf_ref, imgh_ref, txth_ref,
    st_ref, hg_ref, tg_ref, tinv_ref,
    txtf, imgh, txth, feats, texts, images, unit_t, unit_i, acc_t, acc_i, inv_t, inv_i,
    sum_t, sum_i, rcv_t, rcv_i, dlow, dlow_t, dgat, stat, stats2, tails, part_sib, part_rcv, part, owned,
    out_a, in_a, out_b, in_b, out_a2, in_a2, out_b2, in_b2,
    load_sem, send_sem, recv_sem,
):
    me = lax.axis_index("dp")
    core = lax.rem(me, 2)
    spot = lax.rem(me // 2, 16)
    z = me // 32
    x = lax.rem(spot, 4)
    row_first = me - 2 * x
    right_x = lax.rem(x + 1, 4)
    left_x = lax.rem(x + 3, 4)
    right = row_first + 2 * right_x
    left = row_first + 2 * left_x
    inner = (x == 1) | (x == 2)
    up = lax.rem(me + 8, N)
    down = lax.rem(me + N - 8, N)
    sib = me + 1 - 2 * core

    side = 1 - 2 * core

    def z_mate(off):
        return lax.rem(me + 32 * off + N, N)

    def quarter(off):
        return lax.rem(z + off + 8, 4)

    y = spot // 4

    def x_mate(off):
        return row_first + 2 * lax.rem(x + off, 4)

    def y_mate(off):
        return 32 * z + 8 * lax.rem(y + off, 4) + 2 * x + core

    first_owner = 128 * core + 8 * spot
    my_row = me // 8
    src_core = my_row // 16
    src_spot = lax.rem(my_row, 16)

    def source(zz):
        return 32 * zz + 2 * src_spot + src_core

    loads = {}

    def load(i, src, dst):
        loads[i] = pltpu.make_async_copy(src, dst, load_sem.at[i])
        loads[i].start()

    load(0, imgf_ref, feats.at[pl.ds(0, B)])
    load(1, txtf_ref, txtf)
    for j in range(DT // CH):
        load(2 + j, txth_ref.at[pl.ds(j * CH, CH)], txth.at[pl.ds(j * CH, CH)])
    for j in range(DI // CH):
        load(10 + j, imgh_ref.at[pl.ds(j * CH, CH)], imgh.at[pl.ds(j * CH, CH)])

    barrier = pltpu.get_barrier_semaphore()

    def greet(dev):
        pl.semaphore_signal(barrier, inc=1, device_id={"dp": dev}, device_id_type=pl.DeviceIdType.MESH)

    for dev in [right, left, up, down, sib, x_mate(2)] + [z_mate(side), z_mate(2 * side), z_mate(-side)] + [y_mate(o) for o in range(1, 4)]:
        greet(dev)
    for zz in range(8):
        @pl.when(source(zz) != me)
        def _():
            greet(source(zz))

    owner_is_me = (me >= first_owner) & (me < first_owner + 8)

    sent = []
    sent_if = []

    def copy(i, src, dst, dev):
        return pltpu.make_async_remote_copy(
            src_ref=src, dst_ref=dst, send_sem=send_sem.at[i], recv_sem=recv_sem.at[i],
            device_id={"dp": dev}, device_id_type=pl.DeviceIdType.MESH,
        )

    def send(i, src, dst, dev):
        c = copy(i, src, dst, dev)
        c.start()
        sent.append(c)

    def send_if(cond, i, src, dst, dev, landing=None):
        c = pltpu.make_async_remote_copy(
            src_ref=src, dst_ref=dst, send_sem=send_sem.at[i],
            recv_sem=recv_sem.at[i if landing is None else landing],
            device_id={"dp": dev}, device_id_type=pl.DeviceIdType.MESH,
        )

        @pl.when(cond)
        def _():
            c.start()

        sent_if.append((cond, c))

    def drain(always, perhaps):
        for c in always:
            c.wait_send()
        for cond, c in perhaps:
            @pl.when(cond)
            def _():
                c.wait_send()

    def arrived(i, dst):
        copy(i, dst, dst, sib).wait_recv()

    def fea(n):
        return feats.at[pl.ds(n * B, B)]

    def in_row(at, q):
        return q - 4 * (at + q >= 4).astype(jnp.int32)

    def crossed(at, q):
        return q - 4 * (at + q < 4).astype(jnp.int32)

    def slot(ref, off, half=None):
        if half is None:
            return ref.at[2 * (3 + off) + core]
        return ref.at[2 * (3 + off) + core, pl.ds(half * (B // 2), B // 2)]

    def row_send(base, ref, half):
        send(base + 4 + (half or 0), slot(ref, 0, half), slot(ref, in_row(right_x, 3), half), right)
        send(base + (half or 0), slot(ref, 0, half), slot(ref, in_row(left_x, 1), half), left)

    def row_wait(base, ref, q, half):
        arrived(base + 2 * (q - 1) + (half or 0), slot(ref, in_row(x, q), half))

    right_on = (x == 3) | ((core == 0) & (x < 2))
    left_on = (x == 0) | ((core == 1) & (x >= 2))

    def opposite_send(base, ref, half):
        i = base + 2 + (half or 0)
        send_if(right_on, i, slot(ref, in_row(x, 3), half), slot(ref, in_row(right_x, 2), half), right)
        send_if(
            left_on, base + 21 + (half or 0), slot(ref, in_row(x, 1), half), slot(ref, in_row(left_x, 2), half),
            left, i,
        )

    def cross_send(base, ref, q, half):
        dev = jnp.where(x + q < 4, up, down)
        i = base + 6 + 2 * (q - 1) + (half or 0)
        src, dst = slot(ref, in_row(x, q), half), slot(ref, crossed(x, q), half)
        if q == 2:
            send_if(inner, i, src, dst, dev)
        else:
            send(i, src, dst, dev)

    def cross_wait(base, ref, q, half):
        arrived(base + 6 + 2 * (q - 1) + (half or 0), slot(ref, crossed(x, q), half))

    def cross_wait_rest(base, ref, q, half):
        @pl.when(x != (q + 1) // 2)
        def _():
            cross_wait(base, ref, q, half)

    def hand_on(base, ref, half):
        for at in (1, 2):
            @pl.when(x == at)
            def _():
                cross_wait(base, ref, 2 * at - 1, half)
        near = jnp.where(inner, x, 1)
        taken = crossed(near, 2 * near - 1)
        to = 3 * (near - 1)
        send_if(
            inner, base + 12 + (half or 0), slot(ref, taken, half), slot(ref, crossed(to, 2), half),
            row_first + 2 * to, base + 8 + (half or 0),
        )

    def own_rows(ref, of):
        return ref.at[pl.ds(pl.multiple_of(of * B, B), B)]

    def own_send(base, ref):
        send(base + 14, slot(ref, 0), slot(ref, 0), sib)

    def own_wait(base, ref):
        arrived(base + 14, ref.at[7 - core])

    def sums_send(base, acc, rcv):
        send(base + 15, own_rows(acc, 1 - core), rcv, sib)

    def sums(base, acc, rcv):
        arrived(base + 15, rcv)
        return own_rows(acc, core)[...] + rcv[...]

    def project(read, head, acc, first, count):
        acc[...] = jnp.zeros((B, E), jnp.float32)
        for j in range(count):
            loads[first + j].wait()
            acc[...] += jnp.dot(read(j), head[pl.ds(j * CH, CH), :], preferred_element_type=jnp.float32)

    def normalize(acc, unit, inv, ref):
        proj = acc[...]
        scale = lax.rsqrt(jnp.sum(proj * proj, axis=-1, keepdims=True) + EPS)
        value = proj * scale
        unit[...] = value
        inv[...] = jnp.broadcast_to(scale, (B, 128))
        ref[6 + core] = value.astype(jnp.bfloat16)

    loads[1].wait()
    project(lambda j: txtf[:, pl.ds(j * CH, CH)], txth, sum_t, 2, DT // CH)
    normalize(sum_t, unit_t, inv_t, texts)
    pl.semaphore_wait(barrier, 12 + 8 - owner_is_me.astype(jnp.int32))
    for half in (0, 1):
        row_send(TXT, texts, half)
    own_send(TXT, texts)
    loads[0].wait()
    send(FEA + 1, fea(0), fea(1), z_mate(-side))
    send(FEA + 3, fea(0), fea(3), z_mate(side))
    project(lambda j: feats[pl.ds(0, B), pl.ds(j * CH, CH)], imgh, sum_i, 10, DI // CH)
    normalize(sum_i, unit_i, inv_i, images)
    own_send(IMG, images)

    temper = jnp.exp(jnp.full((1, 2 * B), ls_ref[0], jnp.float32))
    bias = lb_ref[0]
    rows = lax.broadcasted_iota(jnp.int32, (2 * B, 1), 0)
    acc_i[...] = jnp.zeros((2 * B, E), jnp.float32)
    acc_t[...] = jnp.zeros((2 * B, E), jnp.float32)
    totals = [jnp.zeros((1, B), jnp.float32) for _ in range(3)]
    far_row = jnp.where((rows >= B) == (core == 0), 1.0, 0.0)

    def group(own, ref, numbers, acc, stats):
        offs = [0 if n == 0 else in_row(x, n) if n < 4 else crossed(x, n - 3) for n in numbers]
        wide = B * len(offs)
        block = jnp.concatenate([slot(ref, off)[...] for off in offs], axis=0)
        both = own[6:8].reshape(2 * B, E)
        cosine = lax.dot_general(
            both, block, (((1,), (1,)), ((), ())), preferred_element_type=jnp.float32
        )
        logits = temper[:, :wide] * cosine + bias
        small = jnp.exp(-jnp.abs(logits))
        grad = jnp.where(logits >= 0.0, 1.0, small) / (1.0 + small)
        if numbers == (0,):
            hit = lax.broadcasted_iota(jnp.int32, (2 * B, B), 1) + core * B == rows
            grad = grad - jnp.where(hit, 1.0, 0.0)
        else:
            far = jnp.concatenate(
                [jnp.full((1, B), (off == 6 * core - 3).astype(jnp.float32)) for off in offs], axis=1
            )
            live = 1.0 - far_row * far
            grad = grad * live
        if stats:
            signed = jnp.where(hit, -logits, logits) if numbers == (0,) else logits
            loss = jnp.maximum(signed, 0.0) + jnp.log1p(small)
            if numbers != (0,):
                loss = loss * live
            for k, term in enumerate((loss, grad * cosine, grad)):
                term = jnp.sum(term, axis=0, keepdims=True)
                for n in range(len(offs)):
                    totals[k] = totals[k] + term[:, n * B : (n + 1) * B]
        weights = (temper[:, :wide] * grad).astype(jnp.bfloat16)
        acc[...] += jnp.dot(weights, block, preferred_element_type=jnp.float32)

    def text_group(*numbers):
        group(images, texts, numbers, acc_i, True)

    def image_group(*numbers):
        group(texts, images, numbers, acc_t, False)

    own_wait(IMG, images)
    text_group(0)
    for half in (0, 1):
        for q in (1, 3):
            row_wait(TXT, texts, q, half)
            cross_send(TXT, texts, q, half)
        opposite_send(TXT, texts, half)
    for half in (0, 1):
        row_wait(TXT, texts, 2, half)
        cross_send(TXT, texts, 2, half)
        hand_on(TXT, texts, half)
    row_send(IMG, images, None)
    arrived(FEA + 1, fea(1))
    send(FEA + 2, fea(1), fea(2), z_mate(-side))
    text_group(1, 3)
    text_group(2)
    for q in (1, 3):
        for half in (0, 1):
            cross_wait_rest(TXT, texts, q, half)
    text_group(4, 6)
    for half in (0, 1):
        cross_wait(TXT, texts, 2, half)
    text_group(5)
    sums_send(TXT, acc_i, rcv_i)
    early, early_if = list(sent), list(sent_if)
    sent.clear()
    sent_if.clear()

    def image_forward(late):
        for q, at, on, i, to, to_q, dev in (
            (1, 0, left_on, IMG + 21, left_x, 2, left), (3, 3, right_on, IMG + 2, right_x, 2, right)
        ):
            now = (x == at) if late else (x != at)

            @pl.when(now)
            def _():
                row_wait(IMG, images, q, None)

            src = slot(images, in_row(x, q))
            i_cross = IMG + 6 + 2 * (q - 1)
            send_if(now, i_cross, src, slot(images, crossed(x, q)), jnp.where(x + q < 4, up, down))
            send_if(now & on, i, src, slot(images, in_row(to, to_q)), dev, IMG + 2)

    image_forward(False)

    stat[...] = jnp.zeros((8, 2 * B), jnp.float32)
    stat[0:1, 0:B] = totals[0]
    stat[0:1, B : 2 * B] = totals[1]
    stat[1:2, 0:B] = totals[2]
    send(SIB + 2, stat, stats2, sib)
    unit = unit_i[...]
    dunit = sums(TXT, acc_i, rcv_i)
    dproj = inv_i[:, 0:1] * (dunit - unit * jnp.sum(unit * dunit, axis=-1, keepdims=True))
    dlow[...] = dproj

    def window(n):
        return dgat.at[:, pl.ds(n * B, B)]

    for n, off in ((2, -2 * side), (1, -side), (3, side), (0, 0)):
        j = quarter(off)
        turned = dlow[:, pl.ds(pl.multiple_of(j * 256, 256), 256)].T.astype(jnp.bfloat16)
        if n == 0:
            dgat[:, 0:B] = turned
        else:
            dlow_t[n] = turned
            send(DLO + n, dlow_t.at[n], window(n), z_mate(off))
    image_forward(True)
    own_wait(TXT, texts)
    image_group(0)

    for n in (1, 2, 3):
        arrived(DLO + n, window(n))
    arrived(FEA + 2, fea(2))
    arrived(FEA + 3, fea(3))

    def part_rows(ref, n):
        return ref.at[pl.ds(pl.multiple_of(n * 384, 384), 384)]

    def product(half, n, ref):
        columns = pl.ds(pl.multiple_of(half * 768 + n * 384, 128), 384)
        part_rows(ref, n)[...] = jnp.dot(
            dgat[...], feats[:, columns], preferred_element_type=jnp.float32
        ).T

    for j, n in enumerate((1 - core, core)):
        product(1 - core, n, part_sib)
        send(SIB + j, part_rows(part_sib, n), part_rows(part_rcv, n), sib)
    for n in (core, 1 - core):
        product(core, n, part)
    arrived(SIB + 2, stats2)
    both = stat[...] + stats2[...]
    for j, n in enumerate((core, 1 - core)):
        arrived(SIB + j, part_rows(part_rcv, n))
        for i in range(8):
            span = pl.ds(pl.multiple_of(n * 384 + i * 48, 16), 48)
            value = part[span, :] + part_rcv[span, :]
            to_y, to_x = 2 * n + i // 4, i % 4
            out_a[to_x, pl.ds(pl.multiple_of(to_y * 32, 32), 32), :] = value[:32, :]
            out_b[to_y, 16 * to_x : 16 * to_x + 16, :] = value[32:, :]
        for i in range(2):
            to_y = 2 * n + i
            o = lax.rem(to_y - y + 4, 4)
            send_if(to_y != y, PLB + o, out_b.at[to_y], in_b.at[o], y_mate(o))
    for n in range(4):
        out_a[n, 128:136, :] = both
    for o in (1, 2, 3):
        send(PLA + o, out_a.at[lax.rem(x + o, 4)], in_a.at[o], x_mate(o))

    row_wait(IMG, images, 2, None)
    cross_send(IMG, images, 2, None)
    hand_on(IMG, images, None)
    image_group(1, 3)
    image_group(2)
    drain(early, early_if)

    def summed(base, out, at, got):
        for o in (1, 2, 3):
            arrived(base + o, got.at[o])
        return out[at] + got[1] + got[2] + got[3]

    total = summed(PLB, out_b, y, in_b)
    for n in range(4):
        out_b2[n] = total[16 * n : 16 * n + 16, :]
    for o in (1, 2, 3):
        send(PLB + 4 + o, out_b2.at[lax.rem(x + o, 4)], in_b2.at[o], x_mate(o))
    total = summed(PLA, out_a, x, in_a)
    for n in range(4):
        out_a2[n, 0:32, :] = total[32 * n : 32 * n + 32, :]
        out_a2[n, 32:40, :] = total[128:136, :]
    for o in (1, 2, 3):
        send(PLA + 4 + o, out_a2.at[lax.rem(y + o, 4)], in_a2.at[o], y_mate(o))
    for q in (1, 3):
        cross_wait_rest(IMG, images, q, None)
    image_group(4, 6)
    total_b = summed(PLB + 4, out_b2, x, in_b2)
    total_a = summed(PLA + 4, out_a2, y, in_a2)
    total = jnp.concatenate([total_a[:32, :], total_b], axis=0)
    for j in range(8):
        tails[j, 0:6, :] = total[6 * j : 6 * j + 6, :]
        tails[j, 6:8, :] = total_a[32:34, :]
    for j in range(8):
        @pl.when(first_owner + j != me)
        def _():
            pltpu.make_async_remote_copy(
                src_ref=tails.at[j], dst_ref=owned.at[z],
                send_sem=send_sem.at[OWN + j], recv_sem=recv_sem.at[OWN + z],
                device_id={"dp": first_owner + j}, device_id_type=pl.DeviceIdType.MESH,
            ).start()

        @pl.when(first_owner + j == me)
        def _():
            owned[z] = tails[j]

    cross_wait(IMG, images, 2, None)
    image_group(5)
    sums_send(IMG, acc_t, rcv_t)
    unit = unit_t[...]
    dunit = sums(IMG, acc_t, rcv_t)
    tg_ref[...] = dunit - unit * jnp.sum(unit * dunit, axis=-1, keepdims=True)
    tinv_ref[...] = inv_t[...]

    for zz in range(8):
        @pl.when(source(zz) != me)
        def _():
            arrived(OWN + zz, owned.at[zz])
    for n in range(4):
        hg_ref[:, n * 256 : (n + 1) * 256] = owned[n, 0:6, :] + owned[n + 4, 0:6, :]
    st_ref[...] = jnp.sum(owned[...], axis=0)
    for j in range(8):
        @pl.when(first_owner + j != me)
        def _():
            copy(OWN + j, tails.at[j], owned.at[z], first_owner + j).wait_send()
    drain(sent, sent_if)


def finish(ls_ref, st_ref, hgs_ref, tgs_ref, tinv_ref, loss_ref, sg_ref, hg_ref, tg_ref):
    temper = jnp.exp(jnp.full((1, B), ls_ref[0], jnp.float32))
    loss_ref[0] = jnp.sum(st_ref[6:7, 0:B]) / PAIRS
    sg_ref[0] = jnp.sum(st_ref[6:7, B : 2 * B] * temper) / PAIRS
    sg_ref[1] = jnp.sum(st_ref[7:8, 0:B]) / PAIRS
    hg_ref[...] = hgs_ref[...] * (1.0 / B)
    tg_ref[...] = tgs_ref[...] * tinv_ref[:, 0:1]


def shards(img_feats, txt_feats, img_head, txt_head, log_scale, logit_bias):
    f32, bf16 = jnp.float32, jnp.bfloat16
    smem = pl.BlockSpec(memory_space=pltpu.SMEM)
    vmem = pl.BlockSpec(memory_space=pltpu.VMEM)
    hbm = pl.BlockSpec(memory_space=pl.ANY)
    sums = pl.pallas_call(
        kernel,
        out_shape=(
            jax.ShapeDtypeStruct((8, 2 * B), f32),
            jax.ShapeDtypeStruct((6, E), f32),
            jax.ShapeDtypeStruct((B, E), f32),
            jax.ShapeDtypeStruct((B, 128), f32),
        ),
        in_specs=[smem] * 2 + [hbm] * 4,
        out_specs=(vmem,) * 4,
        scratch_shapes=[
            pltpu.VMEM((B, DT), bf16),
            pltpu.VMEM((DI, E), bf16),
            pltpu.VMEM((DT, E), bf16),
            pltpu.VMEM((4 * B, DI), bf16),
            pltpu.VMEM((14, B, E), bf16),
            pltpu.VMEM((14, B, E), bf16),
            pltpu.VMEM((B, E), f32),
            pltpu.VMEM((B, E), f32),
            pltpu.VMEM((2 * B, E), f32),
            pltpu.VMEM((2 * B, E), f32),
            pltpu.VMEM((B, 128), f32),
            pltpu.VMEM((B, 128), f32),
            pltpu.VMEM((B, E), f32),
            pltpu.VMEM((B, E), f32),
            pltpu.VMEM((B, E), f32),
            pltpu.VMEM((B, E), f32),
            pltpu.VMEM((B, E), f32),
            pltpu.VMEM((4, 256, B), bf16),
            pltpu.VMEM((256, 4 * B), bf16),
            pltpu.VMEM((8, 256), f32),
            pltpu.VMEM((8, 256), f32),
            pltpu.VMEM((8, 8, 256), f32),
            pltpu.VMEM((768, 256), f32),
            pltpu.VMEM((768, 256), f32),
            pltpu.VMEM((768, 256), f32),
            pltpu.VMEM((8, 8, 256), f32),
            pltpu.VMEM((4, 136, 256), f32),
            pltpu.VMEM((4, 136, 256), f32),
            pltpu.VMEM((4, 64, 256), f32),
            pltpu.VMEM((4, 64, 256), f32),
            pltpu.VMEM((4, 40, 256), f32),
            pltpu.VMEM((4, 40, 256), f32),
            pltpu.VMEM((4, 16, 256), f32),
            pltpu.VMEM((4, 16, 256), f32),
            pltpu.SemaphoreType.DMA((16,)),
            pltpu.SemaphoreType.DMA((IDS,)),
            pltpu.SemaphoreType.DMA((IDS,)),
        ],
        compiler_params=pltpu.CompilerParams(
            collective_id=0, has_side_effects=True, vmem_limit_bytes=62 * 2**20
        ),
        cost_estimate=pl.CostEstimate(flops=5 * 10**9, bytes_accessed=14 * 10**6, transcendentals=10**6),
        name="contrastive",
    )(log_scale, logit_bias, img_feats, txt_feats, img_head, txt_head)
    loss, scalar_grads, head_grad, text_grad = pl.pallas_call(
        finish,
        out_shape=(
            jax.ShapeDtypeStruct((1,), f32),
            jax.ShapeDtypeStruct((2,), f32),
            jax.ShapeDtypeStruct((6, E), f32),
            jax.ShapeDtypeStruct((B, E), f32),
        ),
        in_specs=[smem] + [vmem] * 4,
        out_specs=(smem, smem, vmem, vmem),
        name="finish",
    )(log_scale, *sums)
    return loss.reshape(()), scalar_grads, head_grad, text_grad


def solution(mesh):
    in_specs = (P("dp", None), P("dp", None), P(), P(), P(), P())
    out_specs = (P(), P(), P("dp", None), P("dp", None))
    return jax.shard_map(shards, mesh=mesh, in_specs=in_specs, out_specs=out_specs, check_vma=False)
```

```python
import jax
import jax.numpy as jnp
from jax import lax
from jax.experimental import pallas as pl
from jax.experimental.pallas import tpu as pltpu
from jax.sharding import PartitionSpec as P

EPS = 1e-06
B = 128
E = 1024
DI = 1536
DT = 4096
N = 256
PAIRS = 54525952
CH = 512

TXT = 0
IMG = 24
FEA = 48
DLO = 52
SIB = 56
PLA = 60
PLB = 68
OWN = 76
IDS = 84


def kernel(
    ls_ref, lb_ref, imgf_ref, txtf_ref, imgh_ref, txth_ref,
    st_ref, hg_ref, tg_ref, tinv_ref,
    txtf, imgh, txth, feats, texts, images, unit_t, unit_i, acc_t, acc_i, inv_t, inv_i,
    sum_t, sum_i, rcv_t, rcv_i, dlow, dlow_t, dgat, stat, stats2, tails, part_sib, part_rcv, part, owned,
    out_a, in_a, out_b, in_b, out_a2, in_a2, out_b2, in_b2,
    load_sem, send_sem, recv_sem,
):
    me = lax.axis_index("dp")
    core = lax.rem(me, 2)
    spot = lax.rem(me // 2, 16)
    z = me // 32
    x = lax.rem(spot, 4)
    row_first = me - 2 * x
    right_x = lax.rem(x + 1, 4)
    left_x = lax.rem(x + 3, 4)
    right = row_first + 2 * right_x
    left = row_first + 2 * left_x
    inner = (x == 1) | (x == 2)
    up = lax.rem(me + 8, N)
    down = lax.rem(me + N - 8, N)
    sib = me + 1 - 2 * core

    side = 1 - 2 * core

    def z_mate(off):
        return lax.rem(me + 32 * off + N, N)

    def quarter(off):
        return lax.rem(z + off + 8, 4)

    y = spot // 4

    def x_mate(off):
        return row_first + 2 * lax.rem(x + off, 4)

    def y_mate(off):
        return 32 * z + 8 * lax.rem(y + off, 4) + 2 * x + core

    first_owner = 128 * core + 8 * spot
    my_row = me // 8
    src_core = my_row // 16
    src_spot = lax.rem(my_row, 16)

    def source(zz):
        return 32 * zz + 2 * src_spot + src_core

    loads = {}

    def load(i, src, dst):
        loads[i] = pltpu.make_async_copy(src, dst, load_sem.at[i])
        loads[i].start()

    load(0, imgf_ref, feats.at[pl.ds(0, B)])
    load(1, txtf_ref, txtf)
    for j in range(DT // CH):
        load(2 + j, txth_ref.at[pl.ds(j * CH, CH)], txth.at[pl.ds(j * CH, CH)])
    for j in range(DI // CH):
        load(10 + j, imgh_ref.at[pl.ds(j * CH, CH)], imgh.at[pl.ds(j * CH, CH)])

    barrier = pltpu.get_barrier_semaphore()

    def greet(dev):
        pl.semaphore_signal(barrier, inc=1, device_id={"dp": dev}, device_id_type=pl.DeviceIdType.MESH)

    for dev in [right, left, up, down, sib, x_mate(2)] + [z_mate(side), z_mate(2 * side), z_mate(-side)] + [y_mate(o) for o in range(1, 4)]:
        greet(dev)
    for zz in range(8):
        @pl.when(source(zz) != me)
        def _():
            greet(source(zz))

    owner_is_me = (me >= first_owner) & (me < first_owner + 8)

    sent = []
    sent_if = []

    def copy(i, src, dst, dev):
        return pltpu.make_async_remote_copy(
            src_ref=src, dst_ref=dst, send_sem=send_sem.at[i], recv_sem=recv_sem.at[i],
            device_id={"dp": dev}, device_id_type=pl.DeviceIdType.MESH,
        )

    def send(i, src, dst, dev):
        c = copy(i, src, dst, dev)
        c.start()
        sent.append(c)

    def send_if(cond, i, src, dst, dev, landing=None):
        c = pltpu.make_async_remote_copy(
            src_ref=src, dst_ref=dst, send_sem=send_sem.at[i],
            recv_sem=recv_sem.at[i if landing is None else landing],
            device_id={"dp": dev}, device_id_type=pl.DeviceIdType.MESH,
        )

        @pl.when(cond)
        def _():
            c.start()

        sent_if.append((cond, c))

    def drain(always, perhaps):
        for c in always:
            c.wait_send()
        for cond, c in perhaps:
            @pl.when(cond)
            def _():
                c.wait_send()

    def arrived(i, dst):
        copy(i, dst, dst, sib).wait_recv()

    def fea(n):
        return feats.at[pl.ds(n * B, B)]

    def in_row(at, q):
        return q - 4 * (at + q >= 4).astype(jnp.int32)

    def crossed(at, q):
        return q - 4 * (at + q < 4).astype(jnp.int32)

    def slot(ref, off, half=None):
        if half is None:
            return ref.at[2 * (3 + off) + core]
        return ref.at[2 * (3 + off) + core, pl.ds(half * (B // 2), B // 2)]

    def row_send(base, ref, half):
        send(base + 4 + (half or 0), slot(ref, 0, half), slot(ref, in_row(right_x, 3), half), right)
        send(base + (half or 0), slot(ref, 0, half), slot(ref, in_row(left_x, 1), half), left)

    def row_wait(base, ref, q, half):
        arrived(base + 2 * (q - 1) + (half or 0), slot(ref, in_row(x, q), half))

    right_on = (x == 3) | ((core == 0) & (x < 2))
    left_on = (x == 0) | ((core == 1) & (x >= 2))

    def opposite_send(base, ref, half):
        i = base + 2 + (half or 0)
        send_if(right_on, i, slot(ref, in_row(x, 3), half), slot(ref, in_row(right_x, 2), half), right)
        send_if(
            left_on, base + 21 + (half or 0), slot(ref, in_row(x, 1), half), slot(ref, in_row(left_x, 2), half),
            left, i,
        )

    def cross_send(base, ref, q, half):
        dev = jnp.where(x + q < 4, up, down)
        i = base + 6 + 2 * (q - 1) + (half or 0)
        src, dst = slot(ref, in_row(x, q), half), slot(ref, crossed(x, q), half)
        if q == 2:
            send_if(inner, i, src, dst, dev)
        else:
            send(i, src, dst, dev)

    def cross_wait(base, ref, q, half):
        arrived(base + 6 + 2 * (q - 1) + (half or 0), slot(ref, crossed(x, q), half))

    def cross_wait_rest(base, ref, q, half):
        @pl.when(x != (q + 1) // 2)
        def _():
            cross_wait(base, ref, q, half)

    def hand_on(base, ref, half):
        for at in (1, 2):
            @pl.when(x == at)
            def _():
                cross_wait(base, ref, 2 * at - 1, half)
        near = jnp.where(inner, x, 1)
        taken = crossed(near, 2 * near - 1)
        to = 3 * (near - 1)
        send_if(
            inner, base + 12 + (half or 0), slot(ref, taken, half), slot(ref, crossed(to, 2), half),
            row_first + 2 * to, base + 8 + (half or 0),
        )

    def own_rows(ref, of):
        return ref.at[pl.ds(pl.multiple_of(of * B, B), B)]

    def own_send(base, ref):
        send(base + 14, slot(ref, 0), slot(ref, 0), sib)

    def own_wait(base, ref):
        arrived(base + 14, ref.at[7 - core])

    def sums_send(base, acc, rcv):
        send(base + 15, own_rows(acc, 1 - core), rcv, sib)

    def sums(base, acc, rcv):
        arrived(base + 15, rcv)
        return own_rows(acc, core)[...] + rcv[...]

    def project(read, head, acc, first, count):
        acc[...] = jnp.zeros((B, E), jnp.float32)
        for j in range(count):
            loads[first + j].wait()
            acc[...] += jnp.dot(read(j), head[pl.ds(j * CH, CH), :], preferred_element_type=jnp.float32)

    def normalize(acc, unit, inv, ref):
        proj = acc[...]
        scale = lax.rsqrt(jnp.sum(proj * proj, axis=-1, keepdims=True) + EPS)
        value = proj * scale
        unit[...] = value
        inv[...] = jnp.broadcast_to(scale, (B, 128))
        ref[6 + core] = value.astype(jnp.bfloat16)

    loads[1].wait()
    project(lambda j: txtf[:, pl.ds(j * CH, CH)], txth, sum_t, 2, DT // CH)
    normalize(sum_t, unit_t, inv_t, texts)
    pl.semaphore_wait(barrier, 12 + 8 - owner_is_me.astype(jnp.int32))
    for half in (0, 1):
        row_send(TXT, texts, half)
    own_send(TXT, texts)
    loads[0].wait()
    send(FEA + 1, fea(0), fea(1), z_mate(-side))
    send(FEA + 3, fea(0), fea(3), z_mate(side))
    project(lambda j: feats[pl.ds(0, B), pl.ds(j * CH, CH)], imgh, sum_i, 10, DI // CH)
    normalize(sum_i, unit_i, inv_i, images)
    own_send(IMG, images)

    temper = jnp.exp(jnp.full((1, 2 * B), ls_ref[0], jnp.float32))
    bias = lb_ref[0]
    rows = lax.broadcasted_iota(jnp.int32, (2 * B, 1), 0)
    acc_i[...] = jnp.zeros((2 * B, E), jnp.float32)
    acc_t[...] = jnp.zeros((2 * B, E), jnp.float32)
    totals = [jnp.zeros((1, B), jnp.float32) for _ in range(3)]
    far_row = jnp.where((rows >= B) == (core == 0), 1.0, 0.0)

    def group(own, ref, numbers, acc, stats):
        offs = [0 if n == 0 else in_row(x, n) if n < 4 else crossed(x, n - 3) for n in numbers]
        wide = B * len(offs)
        block = jnp.concatenate([slot(ref, off)[...] for off in offs], axis=0)
        both = own[6:8].reshape(2 * B, E)
        cosine = lax.dot_general(
            both, block, (((1,), (1,)), ((), ())), preferred_element_type=jnp.float32
        )
        logits = temper[:, :wide] * cosine + bias
        small = jnp.exp(-jnp.abs(logits))
        grad = jnp.where(logits >= 0.0, 1.0, small) / (1.0 + small)
        if numbers == (0,):
            hit = lax.broadcasted_iota(jnp.int32, (2 * B, B), 1) + core * B == rows
            grad = grad - jnp.where(hit, 1.0, 0.0)
        else:
            far = jnp.concatenate(
                [jnp.full((1, B), (off == 6 * core - 3).astype(jnp.float32)) for off in offs], axis=1
            )
            live = 1.0 - far_row * far
            grad = grad * live
        if stats:
            signed = jnp.where(hit, -logits, logits) if numbers == (0,) else logits
            loss = jnp.maximum(signed, 0.0) + jnp.log1p(small)
            if numbers != (0,):
                loss = loss * live
            for k, term in enumerate((loss, grad * cosine, grad)):
                term = jnp.sum(term, axis=0, keepdims=True)
                for n in range(len(offs)):
                    totals[k] = totals[k] + term[:, n * B : (n + 1) * B]
        weights = (temper[:, :wide] * grad).astype(jnp.bfloat16)
        acc[...] += jnp.dot(weights, block, preferred_element_type=jnp.float32)

    def text_group(*numbers):
        group(images, texts, numbers, acc_i, True)

    def image_group(*numbers):
        group(texts, images, numbers, acc_t, False)

    own_wait(IMG, images)
    text_group(0)
    for half in (0, 1):
        for q in (1, 3):
            row_wait(TXT, texts, q, half)
            cross_send(TXT, texts, q, half)
        opposite_send(TXT, texts, half)
    for half in (0, 1):
        row_wait(TXT, texts, 2, half)
        cross_send(TXT, texts, 2, half)
        hand_on(TXT, texts, half)
    arrived(FEA + 1, fea(1))
    send(FEA + 2, fea(1), fea(2), z_mate(-side))
    text_group(1, 3)
    text_group(2)
    for q in (1, 3):
        for half in (0, 1):
            cross_wait_rest(TXT, texts, q, half)
    row_send(IMG, images, None)
    text_group(4, 6)
    for half in (0, 1):
        cross_wait(TXT, texts, 2, half)
    text_group(5)
    sums_send(TXT, acc_i, rcv_i)

    stat[...] = jnp.zeros((8, 2 * B), jnp.float32)
    stat[0:1, 0:B] = totals[0]
    stat[0:1, B : 2 * B] = totals[1]
    stat[1:2, 0:B] = totals[2]
    send(SIB + 2, stat, stats2, sib)
    unit = unit_i[...]
    dunit = sums(TXT, acc_i, rcv_i)
    dproj = inv_i[:, 0:1] * (dunit - unit * jnp.sum(unit * dunit, axis=-1, keepdims=True))
    dlow[...] = dproj

    def window(n):
        return dgat.at[:, pl.ds(n * B, B)]

    for n, off in ((2, -2 * side), (1, -side), (3, side), (0, 0)):
        j = quarter(off)
        turned = dlow[:, pl.ds(pl.multiple_of(j * 256, 256), 256)].T.astype(jnp.bfloat16)
        if n == 0:
            dgat[:, 0:B] = turned
        else:
            dlow_t[n] = turned
            send(DLO + n, dlow_t.at[n], window(n), z_mate(off))
    early, early_if = list(sent), list(sent_if)
    sent.clear()
    sent_if.clear()
    for q in (1, 3):
        row_wait(IMG, images, q, None)
        cross_send(IMG, images, q, None)
    opposite_send(IMG, images, None)
    own_wait(TXT, texts)
    image_group(0)

    for n in (1, 2, 3):
        arrived(DLO + n, window(n))
    arrived(FEA + 2, fea(2))
    arrived(FEA + 3, fea(3))

    def part_rows(ref, n):
        return ref.at[pl.ds(pl.multiple_of(n * 384, 384), 384)]

    def product(half, n, ref):
        columns = pl.ds(pl.multiple_of(half * 768 + n * 384, 128), 384)
        part_rows(ref, n)[...] = jnp.dot(
            dgat[...], feats[:, columns], preferred_element_type=jnp.float32
        ).T

    for j, n in enumerate((1 - core, core)):
        product(1 - core, n, part_sib)
        send(SIB + j, part_rows(part_sib, n), part_rows(part_rcv, n), sib)
    for n in (core, 1 - core):
        product(core, n, part)
    arrived(SIB + 2, stats2)
    both = stat[...] + stats2[...]
    for j, n in enumerate((core, 1 - core)):
        arrived(SIB + j, part_rows(part_rcv, n))
        for i in range(8):
            span = pl.ds(pl.multiple_of(n * 384 + i * 48, 16), 48)
            value = part[span, :] + part_rcv[span, :]
            to_y, to_x = 2 * n + i // 4, i % 4
            out_a[to_x, pl.ds(pl.multiple_of(to_y * 32, 32), 32), :] = value[:32, :]
            out_b[to_y, 16 * to_x : 16 * to_x + 16, :] = value[32:, :]
        for i in range(2):
            to_y = 2 * n + i
            o = lax.rem(to_y - y + 4, 4)
            send_if(to_y != y, PLB + o, out_b.at[to_y], in_b.at[o], y_mate(o))
    for n in range(4):
        out_a[n, 128:136, :] = both
    for o in (1, 2, 3):
        send(PLA + o, out_a.at[lax.rem(x + o, 4)], in_a.at[o], x_mate(o))

    row_wait(IMG, images, 2, None)
    cross_send(IMG, images, 2, None)
    hand_on(IMG, images, None)
    image_group(1, 3)
    image_group(2)
    drain(early, early_if)

    def summed(base, out, at, got):
        for o in (1, 2, 3):
            arrived(base + o, got.at[o])
        return out[at] + got[1] + got[2] + got[3]

    total = summed(PLB, out_b, y, in_b)
    for n in range(4):
        out_b2[n] = total[16 * n : 16 * n + 16, :]
    for o in (1, 2, 3):
        send(PLB + 4 + o, out_b2.at[lax.rem(x + o, 4)], in_b2.at[o], x_mate(o))
    total = summed(PLA, out_a, x, in_a)
    for n in range(4):
        out_a2[n, 0:32, :] = total[32 * n : 32 * n + 32, :]
        out_a2[n, 32:40, :] = total[128:136, :]
    for o in (1, 2, 3):
        send(PLA + 4 + o, out_a2.at[lax.rem(y + o, 4)], in_a2.at[o], y_mate(o))
    for q in (1, 3):
        cross_wait_rest(IMG, images, q, None)
    image_group(4, 6)
    total_b = summed(PLB + 4, out_b2, x, in_b2)
    total_a = summed(PLA + 4, out_a2, y, in_a2)
    total = jnp.concatenate([total_a[:32, :], total_b], axis=0)
    for j in range(8):
        tails[j, 0:6, :] = total[6 * j : 6 * j + 6, :]
        tails[j, 6:8, :] = total_a[32:34, :]
    for j in range(8):
        @pl.when(first_owner + j != me)
        def _():
            pltpu.make_async_remote_copy(
                src_ref=tails.at[j], dst_ref=owned.at[z],
                send_sem=send_sem.at[OWN + j], recv_sem=recv_sem.at[OWN + z],
                device_id={"dp": first_owner + j}, device_id_type=pl.DeviceIdType.MESH,
            ).start()

        @pl.when(first_owner + j == me)
        def _():
            owned[z] = tails[j]

    cross_wait(IMG, images, 2, None)
    image_group(5)
    sums_send(IMG, acc_t, rcv_t)
    unit = unit_t[...]
    dunit = sums(IMG, acc_t, rcv_t)
    tg_ref[...] = dunit - unit * jnp.sum(unit * dunit, axis=-1, keepdims=True)
    tinv_ref[...] = inv_t[...]

    for zz in range(8):
        @pl.when(source(zz) != me)
        def _():
            arrived(OWN + zz, owned.at[zz])
    for n in range(4):
        hg_ref[:, n * 256 : (n + 1) * 256] = owned[n, 0:6, :] + owned[n + 4, 0:6, :]
    st_ref[...] = jnp.sum(owned[...], axis=0)
    for j in range(8):
        @pl.when(first_owner + j != me)
        def _():
            copy(OWN + j, tails.at[j], owned.at[z], first_owner + j).wait_send()
    drain(sent, sent_if)


def finish(ls_ref, st_ref, hgs_ref, tgs_ref, tinv_ref, loss_ref, sg_ref, hg_ref, tg_ref):
    temper = jnp.exp(jnp.full((1, B), ls_ref[0], jnp.float32))
    loss_ref[0] = jnp.sum(st_ref[6:7, 0:B]) / PAIRS
    sg_ref[0] = jnp.sum(st_ref[6:7, B : 2 * B] * temper) / PAIRS
    sg_ref[1] = jnp.sum(st_ref[7:8, 0:B]) / PAIRS
    hg_ref[...] = hgs_ref[...] * (1.0 / B)
    tg_ref[...] = tgs_ref[...] * tinv_ref[:, 0:1]


def shards(img_feats, txt_feats, img_head, txt_head, log_scale, logit_bias):
    f32, bf16 = jnp.float32, jnp.bfloat16
    smem = pl.BlockSpec(memory_space=pltpu.SMEM)
    vmem = pl.BlockSpec(memory_space=pltpu.VMEM)
    hbm = pl.BlockSpec(memory_space=pl.ANY)
    sums = pl.pallas_call(
        kernel,
        out_shape=(
            jax.ShapeDtypeStruct((8, 2 * B), f32),
            jax.ShapeDtypeStruct((6, E), f32),
            jax.ShapeDtypeStruct((B, E), f32),
            jax.ShapeDtypeStruct((B, 128), f32),
        ),
        in_specs=[smem] * 2 + [hbm] * 4,
        out_specs=(vmem,) * 4,
        scratch_shapes=[
            pltpu.VMEM((B, DT), bf16),
            pltpu.VMEM((DI, E), bf16),
            pltpu.VMEM((DT, E), bf16),
            pltpu.VMEM((4 * B, DI), bf16),
            pltpu.VMEM((14, B, E), bf16),
            pltpu.VMEM((14, B, E), bf16),
            pltpu.VMEM((B, E), f32),
            pltpu.VMEM((B, E), f32),
            pltpu.VMEM((2 * B, E), f32),
            pltpu.VMEM((2 * B, E), f32),
            pltpu.VMEM((B, 128), f32),
            pltpu.VMEM((B, 128), f32),
            pltpu.VMEM((B, E), f32),
            pltpu.VMEM((B, E), f32),
            pltpu.VMEM((B, E), f32),
            pltpu.VMEM((B, E), f32),
            pltpu.VMEM((B, E), f32),
            pltpu.VMEM((4, 256, B), bf16),
            pltpu.VMEM((256, 4 * B), bf16),
            pltpu.VMEM((8, 256), f32),
            pltpu.VMEM((8, 256), f32),
            pltpu.VMEM((8, 8, 256), f32),
            pltpu.VMEM((768, 256), f32),
            pltpu.VMEM((768, 256), f32),
            pltpu.VMEM((768, 256), f32),
            pltpu.VMEM((8, 8, 256), f32),
            pltpu.VMEM((4, 136, 256), f32),
            pltpu.VMEM((4, 136, 256), f32),
            pltpu.VMEM((4, 64, 256), f32),
            pltpu.VMEM((4, 64, 256), f32),
            pltpu.VMEM((4, 40, 256), f32),
            pltpu.VMEM((4, 40, 256), f32),
            pltpu.VMEM((4, 16, 256), f32),
            pltpu.VMEM((4, 16, 256), f32),
            pltpu.SemaphoreType.DMA((16,)),
            pltpu.SemaphoreType.DMA((IDS,)),
            pltpu.SemaphoreType.DMA((IDS,)),
        ],
        compiler_params=pltpu.CompilerParams(
            collective_id=0, has_side_effects=True, vmem_limit_bytes=62 * 2**20
        ),
        cost_estimate=pl.CostEstimate(flops=5 * 10**9, bytes_accessed=14 * 10**6, transcendentals=10**6),
        name="contrastive",
    )(log_scale, logit_bias, img_feats, txt_feats, img_head, txt_head)
    loss, scalar_grads, head_grad, text_grad = pl.pallas_call(
        finish,
        out_shape=(
            jax.ShapeDtypeStruct((1,), f32),
            jax.ShapeDtypeStruct((2,), f32),
            jax.ShapeDtypeStruct((6, E), f32),
            jax.ShapeDtypeStruct((B, E), f32),
        ),
        in_specs=[smem] + [vmem] * 4,
        out_specs=(smem, smem, vmem, vmem),
        name="finish",
    )(log_scale, *sums)
    return loss.reshape(()), scalar_grads, head_grad, text_grad


def solution(mesh):
    in_specs = (P("dp", None), P("dp", None), P(), P(), P(), P())
    out_specs = (P(), P(), P("dp", None), P("dp", None))
    return jax.shard_map(shards, mesh=mesh, in_specs=in_specs, out_specs=out_specs, check_vma=False)
```

```python
import jax
import jax.numpy as jnp
from jax import lax
from jax.experimental import pallas as pl
from jax.experimental.pallas import tpu as pltpu
from jax.sharding import PartitionSpec as P

EPS = 1e-06
B = 128
E = 1024
DI = 1536
DT = 4096
N = 256
PAIRS = 54525952
CH = 512

TXT = 0
IMG = 24
FEA = 48
DLO = 52
SIB = 56
PLA = 60
PLB = 68
OWN = 76
IDS = 84


def kernel(
    ls_ref, lb_ref, imgf_ref, txtf_ref, imgh_ref, txth_ref,
    st_ref, hg_ref, tg_ref, tinv_ref,
    txtf, imgh, txth, feats, texts, images, unit_t, unit_i, acc_t, acc_i, inv_t, inv_i,
    sum_t, sum_i, rcv_t, rcv_i, dlow, dlow_t, dgat, stat, stats2, tails, part_sib, part_rcv, part, owned,
    out_a, in_a, ring_a, out_b, in_b, out_a2, in_a2, out_b2, in_b2,
    load_sem, send_sem, recv_sem,
):
    me = lax.axis_index("dp")
    core = lax.rem(me, 2)
    spot = lax.rem(me // 2, 16)
    z = me // 32
    x = lax.rem(spot, 4)
    row_first = me - 2 * x
    right_x = lax.rem(x + 1, 4)
    left_x = lax.rem(x + 3, 4)
    right = row_first + 2 * right_x
    left = row_first + 2 * left_x
    inner = (x == 1) | (x == 2)
    up = lax.rem(me + 8, N)
    down = lax.rem(me + N - 8, N)
    sib = me + 1 - 2 * core

    side = 1 - 2 * core

    def z_mate(off):
        return lax.rem(me + 32 * off + N, N)

    def quarter(off):
        return lax.rem(z + off + 8, 4)

    y = spot // 4

    def x_mate(off):
        return row_first + 2 * lax.rem(x + off + 4, 4)

    def y_mate(off):
        return 32 * z + 8 * lax.rem(y + off, 4) + 2 * x + core

    first_owner = 128 * core + 8 * spot
    my_row = me // 8
    src_core = my_row // 16
    src_spot = lax.rem(my_row, 16)

    def source(zz):
        return 32 * zz + 2 * src_spot + src_core

    loads = {}

    def load(i, src, dst):
        loads[i] = pltpu.make_async_copy(src, dst, load_sem.at[i])
        loads[i].start()

    load(0, imgf_ref, feats.at[pl.ds(0, B)])
    load(1, txtf_ref, txtf)
    for j in range(DT // CH):
        load(2 + j, txth_ref.at[pl.ds(j * CH, CH)], txth.at[pl.ds(j * CH, CH)])
    for j in range(DI // CH):
        load(10 + j, imgh_ref.at[pl.ds(j * CH, CH)], imgh.at[pl.ds(j * CH, CH)])

    barrier = pltpu.get_barrier_semaphore()

    def greet(dev):
        pl.semaphore_signal(barrier, inc=1, device_id={"dp": dev}, device_id_type=pl.DeviceIdType.MESH)

    for dev in [right, left, up, down, sib, x_mate(2)] + [z_mate(side), z_mate(2 * side), z_mate(-side)] + [y_mate(o) for o in range(1, 4)]:
        greet(dev)
    for zz in range(8):
        @pl.when(source(zz) != me)
        def _():
            greet(source(zz))

    owner_is_me = (me >= first_owner) & (me < first_owner + 8)

    sent = []
    sent_if = []

    def copy(i, src, dst, dev):
        return pltpu.make_async_remote_copy(
            src_ref=src, dst_ref=dst, send_sem=send_sem.at[i], recv_sem=recv_sem.at[i],
            device_id={"dp": dev}, device_id_type=pl.DeviceIdType.MESH,
        )

    def send(i, src, dst, dev):
        c = copy(i, src, dst, dev)
        c.start()
        sent.append(c)

    def send_if(cond, i, src, dst, dev, landing=None):
        c = pltpu.make_async_remote_copy(
            src_ref=src, dst_ref=dst, send_sem=send_sem.at[i],
            recv_sem=recv_sem.at[i if landing is None else landing],
            device_id={"dp": dev}, device_id_type=pl.DeviceIdType.MESH,
        )

        @pl.when(cond)
        def _():
            c.start()

        sent_if.append((cond, c))

    def drain(always, perhaps):
        for c in always:
            c.wait_send()
        for cond, c in perhaps:
            @pl.when(cond)
            def _():
                c.wait_send()

    def arrived(i, dst):
        copy(i, dst, dst, sib).wait_recv()

    def fea(n):
        return feats.at[pl.ds(n * B, B)]

    def in_row(at, q):
        return q - 4 * (at + q >= 4).astype(jnp.int32)

    def crossed(at, q):
        return q - 4 * (at + q < 4).astype(jnp.int32)

    def slot(ref, off, half=None):
        if half is None:
            return ref.at[2 * (3 + off) + core]
        return ref.at[2 * (3 + off) + core, pl.ds(half * (B // 2), B // 2)]

    def row_send(base, ref, half):
        send(base + 4 + (half or 0), slot(ref, 0, half), slot(ref, in_row(right_x, 3), half), right)
        send(base + (half or 0), slot(ref, 0, half), slot(ref, in_row(left_x, 1), half), left)

    def row_wait(base, ref, q, half):
        arrived(base + 2 * (q - 1) + (half or 0), slot(ref, in_row(x, q), half))

    right_on = (x == 3) | ((core == 0) & (x < 2))
    left_on = (x == 0) | ((core == 1) & (x >= 2))

    def opposite_send(base, ref, half):
        i = base + 2 + (half or 0)
        send_if(right_on, i, slot(ref, in_row(x, 3), half), slot(ref, in_row(right_x, 2), half), right)
        send_if(
            left_on, base + 21 + (half or 0), slot(ref, in_row(x, 1), half), slot(ref, in_row(left_x, 2), half),
            left, i,
        )

    def cross_send(base, ref, q, half):
        dev = jnp.where(x + q < 4, up, down)
        i = base + 6 + 2 * (q - 1) + (half or 0)
        src, dst = slot(ref, in_row(x, q), half), slot(ref, crossed(x, q), half)
        if q == 2:
            send_if(inner, i, src, dst, dev)
        else:
            send(i, src, dst, dev)

    def cross_wait(base, ref, q, half):
        arrived(base + 6 + 2 * (q - 1) + (half or 0), slot(ref, crossed(x, q), half))

    def cross_wait_rest(base, ref, q, half):
        @pl.when(x != (q + 1) // 2)
        def _():
            cross_wait(base, ref, q, half)

    def hand_on(base, ref, half):
        for at in (1, 2):
            @pl.when(x == at)
            def _():
                cross_wait(base, ref, 2 * at - 1, half)
        near = jnp.where(inner, x, 1)
        taken = crossed(near, 2 * near - 1)
        to = 3 * (near - 1)
        send_if(
            inner, base + 12 + (half or 0), slot(ref, taken, half), slot(ref, crossed(to, 2), half),
            row_first + 2 * to, base + 8 + (half or 0),
        )

    def own_rows(ref, of):
        return ref.at[pl.ds(pl.multiple_of(of * B, B), B)]

    def own_send(base, ref):
        send(base + 14, slot(ref, 0), slot(ref, 0), sib)

    def own_wait(base, ref):
        arrived(base + 14, ref.at[7 - core])

    def sums_send(base, acc, rcv):
        send(base + 15, own_rows(acc, 1 - core), rcv, sib)

    def sums(base, acc, rcv):
        arrived(base + 15, rcv)
        return own_rows(acc, core)[...] + rcv[...]

    def project(read, head, acc, first, count):
        acc[...] = jnp.zeros((B, E), jnp.float32)
        for j in range(count):
            loads[first + j].wait()
            acc[...] += jnp.dot(read(j), head[pl.ds(j * CH, CH), :], preferred_element_type=jnp.float32)

    def normalize(acc, unit, inv, ref):
        proj = acc[...]
        scale = lax.rsqrt(jnp.sum(proj * proj, axis=-1, keepdims=True) + EPS)
        value = proj * scale
        unit[...] = value
        inv[...] = jnp.broadcast_to(scale, (B, 128))
        ref[6 + core] = value.astype(jnp.bfloat16)

    loads[1].wait()
    project(lambda j: txtf[:, pl.ds(j * CH, CH)], txth, sum_t, 2, DT // CH)
    normalize(sum_t, unit_t, inv_t, texts)
    pl.semaphore_wait(barrier, 12 + 8 - owner_is_me.astype(jnp.int32))
    for half in (0, 1):
        row_send(TXT, texts, half)
    own_send(TXT, texts)
    loads[0].wait()
    send(FEA + 1, fea(0), fea(1), z_mate(-side))
    send(FEA + 3, fea(0), fea(3), z_mate(side))
    project(lambda j: feats[pl.ds(0, B), pl.ds(j * CH, CH)], imgh, sum_i, 10, DI // CH)
    normalize(sum_i, unit_i, inv_i, images)
    own_send(IMG, images)

    temper = jnp.exp(jnp.full((1, 2 * B), ls_ref[0], jnp.float32))
    bias = lb_ref[0]
    rows = lax.broadcasted_iota(jnp.int32, (2 * B, 1), 0)
    acc_i[...] = jnp.zeros((2 * B, E), jnp.float32)
    acc_t[...] = jnp.zeros((2 * B, E), jnp.float32)
    totals = [jnp.zeros((1, B), jnp.float32) for _ in range(3)]
    far_row = jnp.where((rows >= B) == (core == 0), 1.0, 0.0)

    def group(own, ref, numbers, acc, stats):
        offs = [0 if n == 0 else in_row(x, n) if n < 4 else crossed(x, n - 3) for n in numbers]
        wide = B * len(offs)
        block = jnp.concatenate([slot(ref, off)[...] for off in offs], axis=0)
        both = own[6:8].reshape(2 * B, E)
        cosine = lax.dot_general(
            both, block, (((1,), (1,)), ((), ())), preferred_element_type=jnp.float32
        )
        logits = temper[:, :wide] * cosine + bias
        small = jnp.exp(-jnp.abs(logits))
        grad = jnp.where(logits >= 0.0, 1.0, small) / (1.0 + small)
        if numbers == (0,):
            hit = lax.broadcasted_iota(jnp.int32, (2 * B, B), 1) + core * B == rows
            grad = grad - jnp.where(hit, 1.0, 0.0)
        else:
            far = jnp.concatenate(
                [jnp.full((1, B), (off == 6 * core - 3).astype(jnp.float32)) for off in offs], axis=1
            )
            live = 1.0 - far_row * far
            grad = grad * live
        if stats:
            signed = jnp.where(hit, -logits, logits) if numbers == (0,) else logits
            loss = jnp.maximum(signed, 0.0) + jnp.log1p(small)
            if numbers != (0,):
                loss = loss * live
            for k, term in enumerate((loss, grad * cosine, grad)):
                term = jnp.sum(term, axis=0, keepdims=True)
                for n in range(len(offs)):
                    totals[k] = totals[k] + term[:, n * B : (n + 1) * B]
        weights = (temper[:, :wide] * grad).astype(jnp.bfloat16)
        acc[...] += jnp.dot(weights, block, preferred_element_type=jnp.float32)

    def text_group(*numbers):
        group(images, texts, numbers, acc_i, True)

    def image_group(*numbers):
        group(texts, images, numbers, acc_t, False)

    own_wait(IMG, images)
    text_group(0)
    for half in (0, 1):
        for q in (1, 3):
            row_wait(TXT, texts, q, half)
            cross_send(TXT, texts, q, half)
        opposite_send(TXT, texts, half)
    for half in (0, 1):
        row_wait(TXT, texts, 2, half)
        cross_send(TXT, texts, 2, half)
        hand_on(TXT, texts, half)
    row_send(IMG, images, None)
    arrived(FEA + 1, fea(1))
    send(FEA + 2, fea(1), fea(2), z_mate(-side))
    text_group(1, 3)
    text_group(2)
    for q in (1, 3):
        for half in (0, 1):
            cross_wait_rest(TXT, texts, q, half)
    text_group(4, 6)
    for half in (0, 1):
        cross_wait(TXT, texts, 2, half)
    text_group(5)
    sums_send(TXT, acc_i, rcv_i)

    stat[...] = jnp.zeros((8, 2 * B), jnp.float32)
    stat[0:1, 0:B] = totals[0]
    stat[0:1, B : 2 * B] = totals[1]
    stat[1:2, 0:B] = totals[2]
    send(SIB + 2, stat, stats2, sib)
    unit = unit_i[...]
    dunit = sums(TXT, acc_i, rcv_i)
    dproj = inv_i[:, 0:1] * (dunit - unit * jnp.sum(unit * dunit, axis=-1, keepdims=True))
    dlow[...] = dproj

    def window(n):
        return dgat.at[:, pl.ds(n * B, B)]

    for n, off in ((2, -2 * side), (1, -side), (3, side), (0, 0)):
        j = quarter(off)
        turned = dlow[:, pl.ds(pl.multiple_of(j * 256, 256), 256)].T.astype(jnp.bfloat16)
        if n == 0:
            dgat[:, 0:B] = turned
        else:
            dlow_t[n] = turned
            send(DLO + n, dlow_t.at[n], window(n), z_mate(off))
    early, early_if = list(sent), list(sent_if)
    sent.clear()
    sent_if.clear()
    for q in (1, 3):
        row_wait(IMG, images, q, None)
        cross_send(IMG, images, q, None)
    opposite_send(IMG, images, None)
    own_wait(TXT, texts)
    image_group(0)

    for n in (1, 2, 3):
        arrived(DLO + n, window(n))
    arrived(FEA + 2, fea(2))
    arrived(FEA + 3, fea(3))

    def part_rows(ref, n):
        return ref.at[pl.ds(pl.multiple_of(n * 384, 384), 384)]

    def product(half, n, ref):
        columns = pl.ds(pl.multiple_of(half * 768 + n * 384, 128), 384)
        part_rows(ref, n)[...] = jnp.dot(
            dgat[...], feats[:, columns], preferred_element_type=jnp.float32
        ).T

    for j, n in enumerate((1 - core, core)):
        product(1 - core, n, part_sib)
        send(SIB + j, part_rows(part_sib, n), part_rows(part_rcv, n), sib)
    for n in (core, 1 - core):
        product(core, n, part)
    arrived(SIB + 2, stats2)
    both = stat[...] + stats2[...]
    for j, n in enumerate((core, 1 - core)):
        arrived(SIB + j, part_rows(part_rcv, n))
        for i in range(8):
            span = pl.ds(pl.multiple_of(n * 384 + i * 48, 16), 48)
            value = part[span, :] + part_rcv[span, :]
            to_y, to_x = 2 * n + i // 4, i % 4
            out_a[to_x, pl.ds(pl.multiple_of(to_y * 32, 32), 32), :] = value[:32, :]
            out_b[to_y, 16 * to_x : 16 * to_x + 16, :] = value[32:, :]
        for i in range(2):
            to_y = 2 * n + i
            o = lax.rem(to_y - y + 4, 4)
            send_if(to_y != y, PLB + o, out_b.at[to_y], in_b.at[o], y_mate(o))
    for n in range(4):
        out_a[n, 128:136, :] = both
    send(PLA + 1, out_a.at[lax.rem(x + 2, 4)], in_a.at[1], x_mate(side))
    send(PLA + 2, out_a.at[lax.rem(x - side + 4, 4)], in_a.at[2], x_mate(-side))

    row_wait(IMG, images, 2, None)
    cross_send(IMG, images, 2, None)
    hand_on(IMG, images, None)
    image_group(1, 3)
    arrived(PLA + 1, in_a.at[1])
    ring_a[...] = out_a[lax.rem(x + side + 4, 4)] + in_a[1]
    send(PLA + 3, ring_a, in_a.at[3], x_mate(side))
    image_group(2)
    drain(early, early_if)

    def summed(base, out, at, got):
        for o in (1, 2, 3):
            arrived(base + o, got.at[o])
        return out[at] + got[1] + got[2] + got[3]

    total = summed(PLB, out_b, y, in_b)
    for n in range(4):
        out_b2[n] = total[16 * n : 16 * n + 16, :]
    for o in (1, 2, 3):
        send(PLB + 4 + o, out_b2.at[lax.rem(x + o, 4)], in_b2.at[o], x_mate(o))
    arrived(PLA + 2, in_a.at[2])
    arrived(PLA + 3, in_a.at[3])
    total = out_a[x] + in_a[2] + in_a[3]
    for n in range(4):
        out_a2[n, 0:32, :] = total[32 * n : 32 * n + 32, :]
        out_a2[n, 32:40, :] = total[128:136, :]
    for o in (1, 2, 3):
        send(PLA + 4 + o, out_a2.at[lax.rem(y + o, 4)], in_a2.at[o], y_mate(o))
    for q in (1, 3):
        cross_wait_rest(IMG, images, q, None)
    image_group(4, 6)
    total_b = summed(PLB + 4, out_b2, x, in_b2)
    total_a = summed(PLA + 4, out_a2, y, in_a2)
    total = jnp.concatenate([total_a[:32, :], total_b], axis=0)
    for j in range(8):
        tails[j, 0:6, :] = total[6 * j : 6 * j + 6, :]
        tails[j, 6:8, :] = total_a[32:34, :]
    for j in range(8):
        @pl.when(first_owner + j != me)
        def _():
            pltpu.make_async_remote_copy(
                src_ref=tails.at[j], dst_ref=owned.at[z],
                send_sem=send_sem.at[OWN + j], recv_sem=recv_sem.at[OWN + z],
                device_id={"dp": first_owner + j}, device_id_type=pl.DeviceIdType.MESH,
            ).start()

        @pl.when(first_owner + j == me)
        def _():
            owned[z] = tails[j]

    cross_wait(IMG, images, 2, None)
    image_group(5)
    sums_send(IMG, acc_t, rcv_t)
    unit = unit_t[...]
    dunit = sums(IMG, acc_t, rcv_t)
    tg_ref[...] = dunit - unit * jnp.sum(unit * dunit, axis=-1, keepdims=True)
    tinv_ref[...] = inv_t[...]

    for zz in range(8):
        @pl.when(source(zz) != me)
        def _():
            arrived(OWN + zz, owned.at[zz])
    for n in range(4):
        hg_ref[:, n * 256 : (n + 1) * 256] = owned[n, 0:6, :] + owned[n + 4, 0:6, :]
    st_ref[...] = jnp.sum(owned[...], axis=0)
    for j in range(8):
        @pl.when(first_owner + j != me)
        def _():
            copy(OWN + j, tails.at[j], owned.at[z], first_owner + j).wait_send()
    drain(sent, sent_if)


def finish(ls_ref, st_ref, hgs_ref, tgs_ref, tinv_ref, loss_ref, sg_ref, hg_ref, tg_ref):
    temper = jnp.exp(jnp.full((1, B), ls_ref[0], jnp.float32))
    loss_ref[0] = jnp.sum(st_ref[6:7, 0:B]) / PAIRS
    sg_ref[0] = jnp.sum(st_ref[6:7, B : 2 * B] * temper) / PAIRS
    sg_ref[1] = jnp.sum(st_ref[7:8, 0:B]) / PAIRS
    hg_ref[...] = hgs_ref[...] * (1.0 / B)
    tg_ref[...] = tgs_ref[...] * tinv_ref[:, 0:1]


def shards(img_feats, txt_feats, img_head, txt_head, log_scale, logit_bias):
    f32, bf16 = jnp.float32, jnp.bfloat16
    smem = pl.BlockSpec(memory_space=pltpu.SMEM)
    vmem = pl.BlockSpec(memory_space=pltpu.VMEM)
    hbm = pl.BlockSpec(memory_space=pl.ANY)
    sums = pl.pallas_call(
        kernel,
        out_shape=(
            jax.ShapeDtypeStruct((8, 2 * B), f32),
            jax.ShapeDtypeStruct((6, E), f32),
            jax.ShapeDtypeStruct((B, E), f32),
            jax.ShapeDtypeStruct((B, 128), f32),
        ),
        in_specs=[smem] * 2 + [hbm] * 4,
        out_specs=(vmem,) * 4,
        scratch_shapes=[
            pltpu.VMEM((B, DT), bf16),
            pltpu.VMEM((DI, E), bf16),
            pltpu.VMEM((DT, E), bf16),
            pltpu.VMEM((4 * B, DI), bf16),
            pltpu.VMEM((14, B, E), bf16),
            pltpu.VMEM((14, B, E), bf16),
            pltpu.VMEM((B, E), f32),
            pltpu.VMEM((B, E), f32),
            pltpu.VMEM((2 * B, E), f32),
            pltpu.VMEM((2 * B, E), f32),
            pltpu.VMEM((B, 128), f32),
            pltpu.VMEM((B, 128), f32),
            pltpu.VMEM((B, E), f32),
            pltpu.VMEM((B, E), f32),
            pltpu.VMEM((B, E), f32),
            pltpu.VMEM((B, E), f32),
            pltpu.VMEM((B, E), f32),
            pltpu.VMEM((4, 256, B), bf16),
            pltpu.VMEM((256, 4 * B), bf16),
            pltpu.VMEM((8, 256), f32),
            pltpu.VMEM((8, 256), f32),
            pltpu.VMEM((8, 8, 256), f32),
            pltpu.VMEM((768, 256), f32),
            pltpu.VMEM((768, 256), f32),
            pltpu.VMEM((768, 256), f32),
            pltpu.VMEM((8, 8, 256), f32),
            pltpu.VMEM((4, 136, 256), f32),
            pltpu.VMEM((4, 136, 256), f32),
            pltpu.VMEM((136, 256), f32),
            pltpu.VMEM((4, 64, 256), f32),
            pltpu.VMEM((4, 64, 256), f32),
            pltpu.VMEM((4, 40, 256), f32),
            pltpu.VMEM((4, 40, 256), f32),
            pltpu.VMEM((4, 16, 256), f32),
            pltpu.VMEM((4, 16, 256), f32),
            pltpu.SemaphoreType.DMA((16,)),
            pltpu.SemaphoreType.DMA((IDS,)),
            pltpu.SemaphoreType.DMA((IDS,)),
        ],
        compiler_params=pltpu.CompilerParams(
            collective_id=0, has_side_effects=True, vmem_limit_bytes=62 * 2**20
        ),
        cost_estimate=pl.CostEstimate(flops=5 * 10**9, bytes_accessed=14 * 10**6, transcendentals=10**6),
        name="contrastive",
    )(log_scale, logit_bias, img_feats, txt_feats, img_head, txt_head)
    loss, scalar_grads, head_grad, text_grad = pl.pallas_call(
        finish,
        out_shape=(
            jax.ShapeDtypeStruct((1,), f32),
            jax.ShapeDtypeStruct((2,), f32),
            jax.ShapeDtypeStruct((6, E), f32),
            jax.ShapeDtypeStruct((B, E), f32),
        ),
        in_specs=[smem] + [vmem] * 4,
        out_specs=(smem, smem, vmem, vmem),
        name="finish",
    )(log_scale, *sums)
    return loss.reshape(()), scalar_grads, head_grad, text_grad


def solution(mesh):
    in_specs = (P("dp", None), P("dp", None), P(), P(), P(), P())
    out_specs = (P(), P(), P("dp", None), P("dp", None))
    return jax.shard_map(shards, mesh=mesh, in_specs=in_specs, out_specs=out_specs, check_vma=False)
```

```python
import jax
import jax.numpy as jnp
from jax import lax
from jax.experimental import pallas as pl
from jax.experimental.pallas import tpu as pltpu
from jax.sharding import PartitionSpec as P

EPS = 1e-06
B = 128
E = 1024
DI = 1536
DT = 4096
N = 256
PAIRS = 54525952
CH = 512

TXT = 0
IMG = 24
FEA = 48
DLO = 52
SIB = 56
PLA = 60
OWN = 76
IDS = 84


def kernel(
    ls_ref, lb_ref, imgf_ref, txtf_ref, imgh_ref, txth_ref,
    st_ref, hg_ref, tg_ref, tinv_ref,
    txtf, imgh, txth, feats, texts, images, unit_t, unit_i, acc_t, acc_i, inv_t, inv_i,
    sum_t, sum_i, rcv_t, rcv_i, dlow, dlow_t, dgat, stat, stats2, tails, part_sib, part_rcv, part, owned,
    out_a, in_a, ring_a, out_a2, in_a2,
    load_sem, send_sem, recv_sem,
):
    me = lax.axis_index("dp")
    core = lax.rem(me, 2)
    spot = lax.rem(me // 2, 16)
    z = me // 32
    x = lax.rem(spot, 4)
    row_first = me - 2 * x
    right_x = lax.rem(x + 1, 4)
    left_x = lax.rem(x + 3, 4)
    right = row_first + 2 * right_x
    left = row_first + 2 * left_x
    inner = (x == 1) | (x == 2)
    up = lax.rem(me + 8, N)
    down = lax.rem(me + N - 8, N)
    sib = me + 1 - 2 * core

    side = 1 - 2 * core

    def z_mate(off):
        return lax.rem(me + 32 * off + N, N)

    def quarter(off):
        return lax.rem(z + off + 8, 4)

    y = spot // 4

    def x_mate(off):
        return row_first + 2 * lax.rem(x + off + 4, 4)

    def y_mate(off):
        return 32 * z + 8 * lax.rem(y + off, 4) + 2 * x + core

    first_owner = 128 * core + 8 * spot
    my_row = me // 8
    src_core = my_row // 16
    src_spot = lax.rem(my_row, 16)

    def source(zz):
        return 32 * zz + 2 * src_spot + src_core

    loads = {}

    def load(i, src, dst):
        loads[i] = pltpu.make_async_copy(src, dst, load_sem.at[i])
        loads[i].start()

    load(0, imgf_ref, feats.at[pl.ds(0, B)])
    load(1, txtf_ref, txtf)
    for j in range(DT // CH):
        load(2 + j, txth_ref.at[pl.ds(j * CH, CH)], txth.at[pl.ds(j * CH, CH)])
    for j in range(DI // CH):
        load(10 + j, imgh_ref.at[pl.ds(j * CH, CH)], imgh.at[pl.ds(j * CH, CH)])

    barrier = pltpu.get_barrier_semaphore()

    def greet(dev):
        pl.semaphore_signal(barrier, inc=1, device_id={"dp": dev}, device_id_type=pl.DeviceIdType.MESH)

    for dev in [right, left, up, down, sib, x_mate(2)] + [z_mate(side), z_mate(2 * side), z_mate(-side)] + [y_mate(o) for o in range(1, 4)]:
        greet(dev)
    for zz in range(8):
        @pl.when(source(zz) != me)
        def _():
            greet(source(zz))

    owner_is_me = (me >= first_owner) & (me < first_owner + 8)

    sent = []
    sent_if = []

    def copy(i, src, dst, dev):
        return pltpu.make_async_remote_copy(
            src_ref=src, dst_ref=dst, send_sem=send_sem.at[i], recv_sem=recv_sem.at[i],
            device_id={"dp": dev}, device_id_type=pl.DeviceIdType.MESH,
        )

    def send(i, src, dst, dev):
        c = copy(i, src, dst, dev)
        c.start()
        sent.append(c)

    def send_if(cond, i, src, dst, dev, landing=None):
        c = pltpu.make_async_remote_copy(
            src_ref=src, dst_ref=dst, send_sem=send_sem.at[i],
            recv_sem=recv_sem.at[i if landing is None else landing],
            device_id={"dp": dev}, device_id_type=pl.DeviceIdType.MESH,
        )

        @pl.when(cond)
        def _():
            c.start()

        sent_if.append((cond, c))

    def drain(always, perhaps):
        for c in always:
            c.wait_send()
        for cond, c in perhaps:
            @pl.when(cond)
            def _():
                c.wait_send()

    def arrived(i, dst):
        copy(i, dst, dst, sib).wait_recv()

    def fea(n):
        return feats.at[pl.ds(n * B, B)]

    def in_row(at, q):
        return q - 4 * (at + q >= 4).astype(jnp.int32)

    def crossed(at, q):
        return q - 4 * (at + q < 4).astype(jnp.int32)

    def slot(ref, off, half=None):
        if half is None:
            return ref.at[2 * (3 + off) + core]
        return ref.at[2 * (3 + off) + core, pl.ds(half * (B // 2), B // 2)]

    def row_send(base, ref, half):
        send(base + 4 + (half or 0), slot(ref, 0, half), slot(ref, in_row(right_x, 3), half), right)
        send(base + (half or 0), slot(ref, 0, half), slot(ref, in_row(left_x, 1), half), left)

    def row_wait(base, ref, q, half):
        arrived(base + 2 * (q - 1) + (half or 0), slot(ref, in_row(x, q), half))

    right_on = (x == 3) | ((core == 0) & (x < 2))
    left_on = (x == 0) | ((core == 1) & (x >= 2))

    def opposite_send(base, ref, half):
        i = base + 2 + (half or 0)
        send_if(right_on, i, slot(ref, in_row(x, 3), half), slot(ref, in_row(right_x, 2), half), right)
        send_if(
            left_on, base + 21 + (half or 0), slot(ref, in_row(x, 1), half), slot(ref, in_row(left_x, 2), half),
            left, i,
        )

    def cross_send(base, ref, q, half):
        dev = jnp.where(x + q < 4, up, down)
        i = base + 6 + 2 * (q - 1) + (half or 0)
        src, dst = slot(ref, in_row(x, q), half), slot(ref, crossed(x, q), half)
        if q == 2:
            send_if(inner, i, src, dst, dev)
        else:
            send(i, src, dst, dev)

    def cross_wait(base, ref, q, half):
        arrived(base + 6 + 2 * (q - 1) + (half or 0), slot(ref, crossed(x, q), half))

    def cross_wait_rest(base, ref, q, half):
        @pl.when(x != (q + 1) // 2)
        def _():
            cross_wait(base, ref, q, half)

    def hand_on(base, ref, half):
        for at in (1, 2):
            @pl.when(x == at)
            def _():
                cross_wait(base, ref, 2 * at - 1, half)
        near = jnp.where(inner, x, 1)
        taken = crossed(near, 2 * near - 1)
        to = 3 * (near - 1)
        send_if(
            inner, base + 12 + (half or 0), slot(ref, taken, half), slot(ref, crossed(to, 2), half),
            row_first + 2 * to, base + 8 + (half or 0),
        )

    def own_rows(ref, of):
        return ref.at[pl.ds(pl.multiple_of(of * B, B), B)]

    def own_send(base, ref):
        send(base + 14, slot(ref, 0), slot(ref, 0), sib)

    def own_wait(base, ref):
        arrived(base + 14, ref.at[7 - core])

    def sums_send(base, acc, rcv):
        send(base + 15, own_rows(acc, 1 - core), rcv, sib)

    def sums(base, acc, rcv):
        arrived(base + 15, rcv)
        return own_rows(acc, core)[...] + rcv[...]

    def project(read, head, acc, first, count):
        acc[...] = jnp.zeros((B, E), jnp.float32)
        for j in range(count):
            loads[first + j].wait()
            acc[...] += jnp.dot(read(j), head[pl.ds(j * CH, CH), :], preferred_element_type=jnp.float32)

    def normalize(acc, unit, inv, ref):
        proj = acc[...]
        scale = lax.rsqrt(jnp.sum(proj * proj, axis=-1, keepdims=True) + EPS)
        value = proj * scale
        unit[...] = value
        inv[...] = jnp.broadcast_to(scale, (B, 128))
        ref[6 + core] = value.astype(jnp.bfloat16)

    loads[1].wait()
    project(lambda j: txtf[:, pl.ds(j * CH, CH)], txth, sum_t, 2, DT // CH)
    normalize(sum_t, unit_t, inv_t, texts)
    pl.semaphore_wait(barrier, 12 + 8 - owner_is_me.astype(jnp.int32))
    for half in (0, 1):
        row_send(TXT, texts, half)
    own_send(TXT, texts)
    loads[0].wait()
    send(FEA + 1, fea(0), fea(1), z_mate(-side))
    send(FEA + 3, fea(0), fea(3), z_mate(side))
    project(lambda j: feats[pl.ds(0, B), pl.ds(j * CH, CH)], imgh, sum_i, 10, DI // CH)
    normalize(sum_i, unit_i, inv_i, images)
    own_send(IMG, images)

    temper = jnp.exp(jnp.full((1, 2 * B), ls_ref[0], jnp.float32))
    bias = lb_ref[0]
    rows = lax.broadcasted_iota(jnp.int32, (2 * B, 1), 0)
    acc_i[...] = jnp.zeros((2 * B, E), jnp.float32)
    acc_t[...] = jnp.zeros((2 * B, E), jnp.float32)
    totals = [jnp.zeros((1, B), jnp.float32) for _ in range(3)]
    far_row = jnp.where((rows >= B) == (core == 0), 1.0, 0.0)

    def group(own, ref, numbers, acc, stats):
        offs = [0 if n == 0 else in_row(x, n) if n < 4 else crossed(x, n - 3) for n in numbers]
        wide = B * len(offs)
        block = jnp.concatenate([slot(ref, off)[...] for off in offs], axis=0)
        both = own[6:8].reshape(2 * B, E)
        cosine = lax.dot_general(
            both, block, (((1,), (1,)), ((), ())), preferred_element_type=jnp.float32
        )
        logits = temper[:, :wide] * cosine + bias
        small = jnp.exp(-jnp.abs(logits))
        grad = jnp.where(logits >= 0.0, 1.0, small) / (1.0 + small)
        if numbers == (0,):
            hit = lax.broadcasted_iota(jnp.int32, (2 * B, B), 1) + core * B == rows
            grad = grad - jnp.where(hit, 1.0, 0.0)
        else:
            far = jnp.concatenate(
                [jnp.full((1, B), (off == 6 * core - 3).astype(jnp.float32)) for off in offs], axis=1
            )
            live = 1.0 - far_row * far
            grad = grad * live
        if stats:
            signed = jnp.where(hit, -logits, logits) if numbers == (0,) else logits
            loss = jnp.maximum(signed, 0.0) + jnp.log1p(small)
            if numbers != (0,):
                loss = loss * live
            for k, term in enumerate((loss, grad * cosine, grad)):
                term = jnp.sum(term, axis=0, keepdims=True)
                for n in range(len(offs)):
                    totals[k] = totals[k] + term[:, n * B : (n + 1) * B]
        weights = (temper[:, :wide] * grad).astype(jnp.bfloat16)
        acc[...] += jnp.dot(weights, block, preferred_element_type=jnp.float32)

    def text_group(*numbers):
        group(images, texts, numbers, acc_i, True)

    def image_group(*numbers):
        group(texts, images, numbers, acc_t, False)

    own_wait(IMG, images)
    text_group(0)
    for half in (0, 1):
        for q in (1, 3):
            row_wait(TXT, texts, q, half)
            cross_send(TXT, texts, q, half)
        opposite_send(TXT, texts, half)
    for half in (0, 1):
        row_wait(TXT, texts, 2, half)
        cross_send(TXT, texts, 2, half)
        hand_on(TXT, texts, half)
    row_send(IMG, images, None)
    arrived(FEA + 1, fea(1))
    send(FEA + 2, fea(1), fea(2), z_mate(-side))
    text_group(1, 3)
    text_group(2)
    for q in (1, 3):
        for half in (0, 1):
            cross_wait_rest(TXT, texts, q, half)
    text_group(4, 6)
    for half in (0, 1):
        cross_wait(TXT, texts, 2, half)
    text_group(5)
    sums_send(TXT, acc_i, rcv_i)

    stat[...] = jnp.zeros((8, 2 * B), jnp.float32)
    stat[0:1, 0:B] = totals[0]
    stat[0:1, B : 2 * B] = totals[1]
    stat[1:2, 0:B] = totals[2]
    send(SIB + 2, stat, stats2, sib)
    unit = unit_i[...]
    dunit = sums(TXT, acc_i, rcv_i)
    dproj = inv_i[:, 0:1] * (dunit - unit * jnp.sum(unit * dunit, axis=-1, keepdims=True))
    dlow[...] = dproj

    def window(n):
        return dgat.at[:, pl.ds(n * B, B)]

    for n, off in ((2, -2 * side), (1, -side), (3, side), (0, 0)):
        j = quarter(off)
        turned = dlow[:, pl.ds(pl.multiple_of(j * 256, 256), 256)].T.astype(jnp.bfloat16)
        if n == 0:
            dgat[:, 0:B] = turned
        else:
            dlow_t[n] = turned
            send(DLO + n, dlow_t.at[n], window(n), z_mate(off))
    early, early_if = list(sent), list(sent_if)
    sent.clear()
    sent_if.clear()
    for q in (1, 3):
        row_wait(IMG, images, q, None)
        cross_send(IMG, images, q, None)
    opposite_send(IMG, images, None)
    own_wait(TXT, texts)
    image_group(0)

    for n in (1, 2, 3):
        arrived(DLO + n, window(n))
    arrived(FEA + 2, fea(2))
    arrived(FEA + 3, fea(3))

    def part_rows(ref, n):
        return ref.at[pl.ds(pl.multiple_of(n * 384, 384), 384)]

    def product(half, n, ref):
        columns = pl.ds(pl.multiple_of(half * 768 + n * 384, 128), 384)
        part_rows(ref, n)[...] = jnp.dot(
            dgat[...], feats[:, columns], preferred_element_type=jnp.float32
        ).T

    for j, n in enumerate((1 - core, core)):
        product(1 - core, n, part_sib)
        send(SIB + j, part_rows(part_sib, n), part_rows(part_rcv, n), sib)
    for n in (core, 1 - core):
        product(core, n, part)
    arrived(SIB + 2, stats2)
    both = stat[...] + stats2[...]
    for j, n in enumerate((core, 1 - core)):
        arrived(SIB + j, part_rows(part_rcv, n))
        for i in range(8):
            span = pl.ds(pl.multiple_of(n * 384 + i * 48, 16), 48)
            value = part[span, :] + part_rcv[span, :]
            to_y, to_x = 2 * n + i // 4, i % 4
            out_a[to_x, pl.ds(pl.multiple_of(to_y * 48, 16), 48), :] = value
    for n in range(4):
        out_a[n, 192:200, :] = both
    send(PLA + 1, out_a.at[lax.rem(x + 2, 4)], in_a.at[1], x_mate(side))
    send(PLA + 2, out_a.at[lax.rem(x - side + 4, 4)], in_a.at[2], x_mate(-side))

    row_wait(IMG, images, 2, None)
    cross_send(IMG, images, 2, None)
    image_group(1, 3)
    arrived(PLA + 1, in_a.at[1])
    ring_a[...] = out_a[lax.rem(x + side + 4, 4)] + in_a[1]
    send(PLA + 3, ring_a, in_a.at[3], x_mate(side))
    hand_on(IMG, images, None)
    image_group(2)
    drain(early, early_if)

    def summed(base, out, at, got):
        for o in (1, 2, 3):
            arrived(base + o, got.at[o])
        return out[at] + got[1] + got[2] + got[3]

    arrived(PLA + 2, in_a.at[2])
    arrived(PLA + 3, in_a.at[3])
    total = out_a[x] + in_a[2] + in_a[3]
    for n in range(4):
        out_a2[n, 0:48, :] = total[48 * n : 48 * n + 48, :]
        out_a2[n, 48:56, :] = total[192:200, :]
    for o in (1, 2, 3):
        send(PLA + 4 + o, out_a2.at[lax.rem(y + o, 4)], in_a2.at[o], y_mate(o))
    for q in (1, 3):
        cross_wait_rest(IMG, images, q, None)
    image_group(4, 6)
    total = summed(PLA + 4, out_a2, y, in_a2)
    for j in range(8):
        tails[j, 0:6, :] = total[6 * j : 6 * j + 6, :]
        tails[j, 6:8, :] = total[48:50, :]
    for j in range(8):
        @pl.when(first_owner + j != me)
        def _():
            pltpu.make_async_remote_copy(
                src_ref=tails.at[j], dst_ref=owned.at[z],
                send_sem=send_sem.at[OWN + j], recv_sem=recv_sem.at[OWN + z],
                device_id={"dp": first_owner + j}, device_id_type=pl.DeviceIdType.MESH,
            ).start()

        @pl.when(first_owner + j == me)
        def _():
            owned[z] = tails[j]

    cross_wait(IMG, images, 2, None)
    image_group(5)
    sums_send(IMG, acc_t, rcv_t)
    unit = unit_t[...]
    dunit = sums(IMG, acc_t, rcv_t)
    tg_ref[...] = dunit - unit * jnp.sum(unit * dunit, axis=-1, keepdims=True)
    tinv_ref[...] = inv_t[...]

    for zz in range(8):
        @pl.when(source(zz) != me)
        def _():
            arrived(OWN + zz, owned.at[zz])
    for n in range(4):
        hg_ref[:, n * 256 : (n + 1) * 256] = owned[n, 0:6, :] + owned[n + 4, 0:6, :]
    st_ref[...] = jnp.sum(owned[...], axis=0)
    for j in range(8):
        @pl.when(first_owner + j != me)
        def _():
            copy(OWN + j, tails.at[j], owned.at[z], first_owner + j).wait_send()
    drain(sent, sent_if)


def finish(ls_ref, st_ref, hgs_ref, tgs_ref, tinv_ref, loss_ref, sg_ref, hg_ref, tg_ref):
    temper = jnp.exp(jnp.full((1, B), ls_ref[0], jnp.float32))
    loss_ref[0] = jnp.sum(st_ref[6:7, 0:B]) / PAIRS
    sg_ref[0] = jnp.sum(st_ref[6:7, B : 2 * B] * temper) / PAIRS
    sg_ref[1] = jnp.sum(st_ref[7:8, 0:B]) / PAIRS
    hg_ref[...] = hgs_ref[...] * (1.0 / B)
    tg_ref[...] = tgs_ref[...] * tinv_ref[:, 0:1]


def shards(img_feats, txt_feats, img_head, txt_head, log_scale, logit_bias):
    f32, bf16 = jnp.float32, jnp.bfloat16
    smem = pl.BlockSpec(memory_space=pltpu.SMEM)
    vmem = pl.BlockSpec(memory_space=pltpu.VMEM)
    hbm = pl.BlockSpec(memory_space=pl.ANY)
    sums = pl.pallas_call(
        kernel,
        out_shape=(
            jax.ShapeDtypeStruct((8, 2 * B), f32),
            jax.ShapeDtypeStruct((6, E), f32),
            jax.ShapeDtypeStruct((B, E), f32),
            jax.ShapeDtypeStruct((B, 128), f32),
        ),
        in_specs=[smem] * 2 + [hbm] * 4,
        out_specs=(vmem,) * 4,
        scratch_shapes=[
            pltpu.VMEM((B, DT), bf16),
            pltpu.VMEM((DI, E), bf16),
            pltpu.VMEM((DT, E), bf16),
            pltpu.VMEM((4 * B, DI), bf16),
            pltpu.VMEM((14, B, E), bf16),
            pltpu.VMEM((14, B, E), bf16),
            pltpu.VMEM((B, E), f32),
            pltpu.VMEM((B, E), f32),
            pltpu.VMEM((2 * B, E), f32),
            pltpu.VMEM((2 * B, E), f32),
            pltpu.VMEM((B, 128), f32),
            pltpu.VMEM((B, 128), f32),
            pltpu.VMEM((B, E), f32),
            pltpu.VMEM((B, E), f32),
            pltpu.VMEM((B, E), f32),
            pltpu.VMEM((B, E), f32),
            pltpu.VMEM((B, E), f32),
            pltpu.VMEM((4, 256, B), bf16),
            pltpu.VMEM((256, 4 * B), bf16),
            pltpu.VMEM((8, 256), f32),
            pltpu.VMEM((8, 256), f32),
            pltpu.VMEM((8, 8, 256), f32),
            pltpu.VMEM((768, 256), f32),
            pltpu.VMEM((768, 256), f32),
            pltpu.VMEM((768, 256), f32),
            pltpu.VMEM((8, 8, 256), f32),
            pltpu.VMEM((4, 200, 256), f32),
            pltpu.VMEM((4, 200, 256), f32),
            pltpu.VMEM((200, 256), f32),
            pltpu.VMEM((4, 56, 256), f32),
            pltpu.VMEM((4, 56, 256), f32),
            pltpu.SemaphoreType.DMA((16,)),
            pltpu.SemaphoreType.DMA((IDS,)),
            pltpu.SemaphoreType.DMA((IDS,)),
        ],
        compiler_params=pltpu.CompilerParams(
            collective_id=0, has_side_effects=True, vmem_limit_bytes=62 * 2**20
        ),
        cost_estimate=pl.CostEstimate(flops=5 * 10**9, bytes_accessed=14 * 10**6, transcendentals=10**6),
        name="contrastive",
    )(log_scale, logit_bias, img_feats, txt_feats, img_head, txt_head)
    loss, scalar_grads, head_grad, text_grad = pl.pallas_call(
        finish,
        out_shape=(
            jax.ShapeDtypeStruct((1,), f32),
            jax.ShapeDtypeStruct((2,), f32),
            jax.ShapeDtypeStruct((6, E), f32),
            jax.ShapeDtypeStruct((B, E), f32),
        ),
        in_specs=[smem] + [vmem] * 4,
        out_specs=(smem, smem, vmem, vmem),
        name="finish",
    )(log_scale, *sums)
    return loss.reshape(()), scalar_grads, head_grad, text_grad


def solution(mesh):
    in_specs = (P("dp", None), P("dp", None), P(), P(), P(), P())
    out_specs = (P(), P(), P("dp", None), P("dp", None))
    return jax.shard_map(shards, mesh=mesh, in_specs=in_specs, out_specs=out_specs, check_vma=False)
```

```python
import jax
import jax.numpy as jnp
from jax import lax
from jax.experimental import pallas as pl
from jax.experimental.pallas import tpu as pltpu
from jax.sharding import PartitionSpec as P

EPS = 1e-06
B = 128
E = 1024
DI = 1536
DT = 4096
N = 256
PAIRS = 54525952
CH = 512

TXT = 0
IMG = 24
FEA = 48
DLO = 52
SIB = 56
PLA = 60
PLB = 68
OWN = 76
IDS = 84


def kernel(
    ls_ref, lb_ref, imgf_ref, txtf_ref, imgh_ref, txth_ref,
    st_ref, hg_ref, tg_ref, tinv_ref,
    txtf, imgh, txth, feats, texts, images, unit_t, unit_i, acc_t, acc_i, inv_t, inv_i,
    sum_t, sum_i, rcv_t, rcv_i, dlow, dlow_t, dgat, stat, stats2, tails, part_sib, part_rcv, part, owned,
    out_a, in_a, out_b, in_b, out_a2, in_a2, out_b2, in_b2,
    load_sem, send_sem, recv_sem,
):
    me = lax.axis_index("dp")
    core = lax.rem(me, 2)
    spot = lax.rem(me // 2, 16)
    z = me // 32
    x = lax.rem(spot, 4)
    row_first = me - 2 * x
    right_x = lax.rem(x + 1, 4)
    left_x = lax.rem(x + 3, 4)
    right = row_first + 2 * right_x
    left = row_first + 2 * left_x
    inner = (x == 1) | (x == 2)
    up = lax.rem(me + 8, N)
    down = lax.rem(me + N - 8, N)
    sib = me + 1 - 2 * core

    side = 1 - 2 * core

    def z_mate(off):
        return lax.rem(me + 32 * off + N, N)

    def quarter(off):
        return lax.rem(z + off + 8, 4)

    y = spot // 4

    def x_mate(off):
        return row_first + 2 * lax.rem(x + off, 4)

    def y_mate(off):
        return 32 * z + 8 * lax.rem(y + off, 4) + 2 * x + core

    first_owner = 128 * core + 8 * spot
    my_row = me // 8
    src_core = my_row // 16
    src_spot = lax.rem(my_row, 16)

    def source(zz):
        return 32 * zz + 2 * src_spot + src_core

    loads = {}

    def load(i, src, dst):
        loads[i] = pltpu.make_async_copy(src, dst, load_sem.at[i])
        loads[i].start()

    load(0, imgf_ref, feats.at[pl.ds(0, B)])
    load(1, txtf_ref, txtf)
    for j in range(DT // CH):
        load(2 + j, txth_ref.at[pl.ds(j * CH, CH)], txth.at[pl.ds(j * CH, CH)])
    for j in range(DI // CH):
        load(10 + j, imgh_ref.at[pl.ds(j * CH, CH)], imgh.at[pl.ds(j * CH, CH)])

    barrier = pltpu.get_barrier_semaphore()

    def greet(dev):
        pl.semaphore_signal(barrier, inc=1, device_id={"dp": dev}, device_id_type=pl.DeviceIdType.MESH)

    for dev in [right, left, up, down, sib, x_mate(2)] + [z_mate(side), z_mate(2 * side), z_mate(-side)] + [y_mate(o) for o in range(1, 4)]:
        greet(dev)
    for zz in range(8):
        @pl.when(source(zz) != me)
        def _():
            greet(source(zz))

    owner_is_me = (me >= first_owner) & (me < first_owner + 8)

    sent = []
    sent_if = []

    def copy(i, src, dst, dev):
        return pltpu.make_async_remote_copy(
            src_ref=src, dst_ref=dst, send_sem=send_sem.at[i], recv_sem=recv_sem.at[i],
            device_id={"dp": dev}, device_id_type=pl.DeviceIdType.MESH,
        )

    def send(i, src, dst, dev):
        c = copy(i, src, dst, dev)
        c.start()
        sent.append(c)

    def send_if(cond, i, src, dst, dev, landing=None):
        c = pltpu.make_async_remote_copy(
            src_ref=src, dst_ref=dst, send_sem=send_sem.at[i],
            recv_sem=recv_sem.at[i if landing is None else landing],
            device_id={"dp": dev}, device_id_type=pl.DeviceIdType.MESH,
        )

        @pl.when(cond)
        def _():
            c.start()

        sent_if.append((cond, c))

    def drain(always, perhaps):
        for c in always:
            c.wait_send()
        for cond, c in perhaps:
            @pl.when(cond)
            def _():
                c.wait_send()

    def arrived(i, dst):
        copy(i, dst, dst, sib).wait_recv()

    def fea(n):
        return feats.at[pl.ds(n * B, B)]

    def in_row(at, q):
        return q - 4 * (at + q >= 4).astype(jnp.int32)

    def crossed(at, q):
        return q - 4 * (at + q < 4).astype(jnp.int32)

    def slot(ref, off, half=None):
        if half is None:
            return ref.at[2 * (3 + off) + core]
        return ref.at[2 * (3 + off) + core, pl.ds(half * (B // 2), B // 2)]

    def row_send(base, ref, half):
        send(base + 4 + (half or 0), slot(ref, 0, half), slot(ref, in_row(right_x, 3), half), right)
        send(base + (half or 0), slot(ref, 0, half), slot(ref, in_row(left_x, 1), half), left)

    def row_wait(base, ref, q, half):
        arrived(base + 2 * (q - 1) + (half or 0), slot(ref, in_row(x, q), half))

    right_on = (x == 3) | ((core == 0) & (x < 2))
    left_on = (x == 0) | ((core == 1) & (x >= 2))

    def opposite_send(base, ref, half):
        i = base + 2 + (half or 0)
        send_if(right_on, i, slot(ref, in_row(x, 3), half), slot(ref, in_row(right_x, 2), half), right)
        send_if(
            left_on, base + 21 + (half or 0), slot(ref, in_row(x, 1), half), slot(ref, in_row(left_x, 2), half),
            left, i,
        )

    def cross_send(base, ref, q, half):
        dev = jnp.where(x + q < 4, up, down)
        i = base + 6 + 2 * (q - 1) + (half or 0)
        src, dst = slot(ref, in_row(x, q), half), slot(ref, crossed(x, q), half)
        if q == 2:
            send_if(inner, i, src, dst, dev)
        else:
            send(i, src, dst, dev)

    def cross_wait(base, ref, q, half):
        arrived(base + 6 + 2 * (q - 1) + (half or 0), slot(ref, crossed(x, q), half))

    def cross_wait_rest(base, ref, q, half):
        @pl.when(x != (q + 1) // 2)
        def _():
            cross_wait(base, ref, q, half)

    def hand_on(base, ref, half):
        for at in (1, 2):
            @pl.when(x == at)
            def _():
                cross_wait(base, ref, 2 * at - 1, half)
        near = jnp.where(inner, x, 1)
        taken = crossed(near, 2 * near - 1)
        to = 3 * (near - 1)
        send_if(
            inner, base + 12 + (half or 0), slot(ref, taken, half), slot(ref, crossed(to, 2), half),
            row_first + 2 * to, base + 8 + (half or 0),
        )

    def own_rows(ref, of):
        return ref.at[pl.ds(pl.multiple_of(of * B, B), B)]

    def own_send(base, ref):
        send(base + 14, slot(ref, 0), slot(ref, 0), sib)

    def own_wait(base, ref):
        arrived(base + 14, ref.at[7 - core])

    def sums_send(base, acc, rcv):
        send(base + 15, own_rows(acc, 1 - core), rcv, sib)

    def sums(base, acc, rcv):
        arrived(base + 15, rcv)
        return own_rows(acc, core)[...] + rcv[...]

    def project(read, head, acc, first, count):
        acc[...] = jnp.zeros((B, E), jnp.float32)
        for j in range(count):
            loads[first + j].wait()
            acc[...] += jnp.dot(read(j), head[pl.ds(j * CH, CH), :], preferred_element_type=jnp.float32)

    def normalize(acc, unit, inv, ref):
        proj = acc[...]
        scale = lax.rsqrt(jnp.sum(proj * proj, axis=-1, keepdims=True) + EPS)
        value = proj * scale
        unit[...] = value
        inv[...] = jnp.broadcast_to(scale, (B, 128))
        ref[6 + core] = value.astype(jnp.bfloat16)

    loads[1].wait()
    project(lambda j: txtf[:, pl.ds(j * CH, CH)], txth, sum_t, 2, DT // CH)
    normalize(sum_t, unit_t, inv_t, texts)
    pl.semaphore_wait(barrier, 12 + 8 - owner_is_me.astype(jnp.int32))
    for half in (0, 1):
        row_send(TXT, texts, half)
    own_send(TXT, texts)
    loads[0].wait()
    send(FEA + 1, fea(0), fea(1), z_mate(-side))
    send(FEA + 3, fea(0), fea(3), z_mate(side))
    project(lambda j: feats[pl.ds(0, B), pl.ds(j * CH, CH)], imgh, sum_i, 10, DI // CH)
    normalize(sum_i, unit_i, inv_i, images)
    own_send(IMG, images)

    temper = jnp.exp(jnp.full((1, 2 * B), ls_ref[0], jnp.float32))
    bias = lb_ref[0]
    rows = lax.broadcasted_iota(jnp.int32, (2 * B, 1), 0)
    acc_i[...] = jnp.zeros((2 * B, E), jnp.float32)
    acc_t[...] = jnp.zeros((2 * B, E), jnp.float32)
    totals = [jnp.zeros((1, B), jnp.float32) for _ in range(3)]
    far_row = jnp.where((rows >= B) == (core == 0), 1.0, 0.0)

    def group(own, ref, numbers, acc, stats):
        offs = [0 if n == 0 else in_row(x, n) if n < 4 else crossed(x, n - 3) for n in numbers]
        wide = B * len(offs)
        block = jnp.concatenate([slot(ref, off)[...] for off in offs], axis=0)
        both = own[6:8].reshape(2 * B, E)
        cosine = lax.dot_general(
            both, block, (((1,), (1,)), ((), ())), preferred_element_type=jnp.float32
        )
        logits = temper[:, :wide] * cosine + bias
        small = jnp.exp(-jnp.abs(logits))
        grad = jnp.where(logits >= 0.0, 1.0, small) / (1.0 + small)
        if numbers == (0,):
            hit = lax.broadcasted_iota(jnp.int32, (2 * B, B), 1) + core * B == rows
            grad = grad - jnp.where(hit, 1.0, 0.0)
        else:
            far = jnp.concatenate(
                [jnp.full((1, B), (off == 6 * core - 3).astype(jnp.float32)) for off in offs], axis=1
            )
            live = 1.0 - far_row * far
            grad = grad * live
        if stats:
            signed = jnp.where(hit, -logits, logits) if numbers == (0,) else logits
            loss = jnp.maximum(signed, 0.0) + jnp.log1p(small)
            if numbers != (0,):
                loss = loss * live
            for k, term in enumerate((loss, grad * cosine, grad)):
                term = jnp.sum(term, axis=0, keepdims=True)
                for n in range(len(offs)):
                    totals[k] = totals[k] + term[:, n * B : (n + 1) * B]
        weights = (temper[:, :wide] * grad).astype(jnp.bfloat16)
        acc[...] += jnp.dot(weights, block, preferred_element_type=jnp.float32)

    def text_group(*numbers):
        group(images, texts, numbers, acc_i, True)

    def image_group(*numbers):
        group(texts, images, numbers, acc_t, False)

    own_wait(IMG, images)
    text_group(0)
    for half in (0, 1):
        for q in (1, 3):
            row_wait(TXT, texts, q, half)
            cross_send(TXT, texts, q, half)
        opposite_send(TXT, texts, half)
    for half in (0, 1):
        row_wait(TXT, texts, 2, half)
        cross_send(TXT, texts, 2, half)
        hand_on(TXT, texts, half)
    row_send(IMG, images, None)
    arrived(FEA + 1, fea(1))
    send(FEA + 2, fea(1), fea(2), z_mate(-side))
    text_group(1, 3)
    text_group(2)
    for q in (1, 3):
        for half in (0, 1):
            cross_wait_rest(TXT, texts, q, half)
    text_group(4, 6)
    for half in (0, 1):
        cross_wait(TXT, texts, 2, half)
    text_group(5)
    sums_send(TXT, acc_i, rcv_i)

    stat[...] = jnp.zeros((8, 2 * B), jnp.float32)
    stat[0:1, 0:B] = totals[0]
    stat[0:1, B : 2 * B] = totals[1]
    stat[1:2, 0:B] = totals[2]
    send(SIB + 2, stat, stats2, sib)
    unit = unit_i[...]
    dunit = sums(TXT, acc_i, rcv_i)
    dproj = inv_i[:, 0:1] * (dunit - unit * jnp.sum(unit * dunit, axis=-1, keepdims=True))
    dlow[...] = dproj

    def window(n):
        return dgat.at[:, pl.ds(n * B, B)]

    for n, off in ((2, -2 * side), (1, -side), (3, side), (0, 0)):
        j = quarter(off)
        turned = dlow[:, pl.ds(pl.multiple_of(j * 256, 256), 256)].T.astype(jnp.bfloat16)
        if n == 0:
            dgat[:, 0:B] = turned
        else:
            dlow_t[n] = turned
            send(DLO + n, dlow_t.at[n], window(n), z_mate(off))
    early, early_if = list(sent), list(sent_if)
    sent.clear()
    sent_if.clear()
    for q in (1, 3):
        row_wait(IMG, images, q, None)
        cross_send(IMG, images, q, None)
    opposite_send(IMG, images, None)
    own_wait(TXT, texts)
    image_group(0)

    for n in (1, 2, 3):
        arrived(DLO + n, window(n))
    arrived(FEA + 2, fea(2))
    arrived(FEA + 3, fea(3))

    def part_rows(ref, n):
        return ref.at[pl.ds(pl.multiple_of(n * 384, 384), 384)]

    def product(half, n, ref):
        columns = pl.ds(pl.multiple_of(half * 768 + n * 384, 128), 384)
        part_rows(ref, n)[...] = jnp.dot(
            dgat[...], feats[:, columns], preferred_element_type=jnp.float32
        ).T

    for j, n in enumerate((1 - core, core)):
        product(1 - core, n, part_sib)
        send(SIB + j, part_rows(part_sib, n), part_rows(part_rcv, n), sib)
    for n in (core, 1 - core):
        product(core, n, part)
    arrived(SIB + 2, stats2)
    both = stat[...] + stats2[...]
    for j, n in enumerate((core, 1 - core)):
        arrived(SIB + j, part_rows(part_rcv, n))
        for i in range(8):
            span = pl.ds(pl.multiple_of(n * 384 + i * 48, 16), 48)
            value = part[span, :] + part_rcv[span, :]
            to_y, to_x = 2 * n + i // 4, i % 4
            out_a[to_x, pl.ds(pl.multiple_of(to_y * 32, 32), 32), :] = value[:32, :]
            out_b[to_y, 16 * to_x : 16 * to_x + 16, :] = value[32:, :]
        for i in range(2):
            to_y = 2 * n + i
            o = lax.rem(to_y - y + 4, 4)
            send_if(to_y != y, PLB + o, out_b.at[to_y], in_b.at[o], y_mate(o))
    for n in range(4):
        out_a[n, 128:136, :] = both
    for o in (1, 2, 3):
        send(PLA + o, out_a.at[lax.rem(x + o, 4)], in_a.at[o], x_mate(o))

    row_wait(IMG, images, 2, None)
    cross_send(IMG, images, 2, None)
    hand_on(IMG, images, None)
    image_group(1, 3)
    image_group(2)
    drain(early, early_if)

    def summed(base, out, at, got):
        for o in (1, 2, 3):
            arrived(base + o, got.at[o])
        return out[at] + got[1] + got[2] + got[3]

    total = summed(PLB, out_b, y, in_b)
    for n in range(4):
        out_b2[n] = total[16 * n : 16 * n + 16, :]
    for o in (1, 2, 3):
        send(PLB + 4 + o, out_b2.at[lax.rem(x + o, 4)], in_b2.at[o], x_mate(o))
    total = summed(PLA, out_a, x, in_a)
    for n in range(4):
        out_a2[n, 0:32, :] = total[32 * n : 32 * n + 32, :]
        out_a2[n, 32:40, :] = total[128:136, :]
    for o in (1, 2, 3):
        send(PLA + 4 + o, out_a2.at[lax.rem(y + o, 4)], in_a2.at[o], y_mate(o))
    for q in (1, 3):
        cross_wait_rest(IMG, images, q, None)
    image_group(4, 6)
    total_b = summed(PLB + 4, out_b2, x, in_b2)
    total_a = summed(PLA + 4, out_a2, y, in_a2)
    total = jnp.concatenate([total_a[:32, :], total_b], axis=0)
    for j in range(8):
        tails[j, 0:6, :] = total[6 * j : 6 * j + 6, :]
        tails[j, 6:8, :] = total_a[32:34, :]
    for j in range(8):
        @pl.when(first_owner + j != me)
        def _():
            pltpu.make_async_remote_copy(
                src_ref=tails.at[j], dst_ref=owned.at[z],
                send_sem=send_sem.at[OWN + j], recv_sem=recv_sem.at[OWN + z],
                device_id={"dp": first_owner + j}, device_id_type=pl.DeviceIdType.MESH,
            ).start()

        @pl.when(first_owner + j == me)
        def _():
            owned[z] = tails[j]

    cross_wait(IMG, images, 2, None)
    image_group(5)
    sums_send(IMG, acc_t, rcv_t)
    unit = unit_t[...]
    dunit = sums(IMG, acc_t, rcv_t)
    tg_ref[...] = dunit - unit * jnp.sum(unit * dunit, axis=-1, keepdims=True)
    tinv_ref[...] = inv_t[...]

    for zz in range(8):
        @pl.when(source(zz) != me)
        def _():
            arrived(OWN + zz, owned.at[zz])
    for n in range(4):
        hg_ref[:, n * 256 : (n + 1) * 256] = owned[n, 0:6, :] + owned[n + 4, 0:6, :]
    st_ref[...] = jnp.sum(owned[...], axis=0)
    for j in range(8):
        @pl.when(first_owner + j != me)
        def _():
            copy(OWN + j, tails.at[j], owned.at[z], first_owner + j).wait_send()
    drain(sent, sent_if)


def finish(
    ls_ref, st_ref, hgs_ref, tgs_ref, tinv_ref, loss_ref, sg_ref, hg_ref, tg_ref, block, load_sem, store_sem
):
    def span(n):
        return pl.ds(n * 32, 32)

    loads = [pltpu.make_async_copy(tgs_ref.at[span(n)], block.at[span(n)], load_sem.at[n]) for n in range(4)]
    stores = [pltpu.make_async_copy(block.at[span(n)], tg_ref.at[span(n)], store_sem.at[n]) for n in range(4)]
    for c in loads:
        c.start()
    for n in range(4):
        loads[n].wait()
        block[span(n), :] = block[span(n), :] * tinv_ref[span(n), 0:1]
        stores[n].start()
    temper = jnp.exp(jnp.full((1, B), ls_ref[0], jnp.float32))
    loss_ref[0] = jnp.sum(st_ref[6:7, 0:B]) / PAIRS
    sg_ref[0] = jnp.sum(st_ref[6:7, B : 2 * B] * temper) / PAIRS
    sg_ref[1] = jnp.sum(st_ref[7:8, 0:B]) / PAIRS
    hg_ref[...] = hgs_ref[...] * (1.0 / B)
    for c in stores:
        c.wait()


def shards(img_feats, txt_feats, img_head, txt_head, log_scale, logit_bias):
    f32, bf16 = jnp.float32, jnp.bfloat16
    smem = pl.BlockSpec(memory_space=pltpu.SMEM)
    vmem = pl.BlockSpec(memory_space=pltpu.VMEM)
    hbm = pl.BlockSpec(memory_space=pl.ANY)
    sums = pl.pallas_call(
        kernel,
        out_shape=(
            jax.ShapeDtypeStruct((8, 2 * B), f32),
            jax.ShapeDtypeStruct((6, E), f32),
            jax.ShapeDtypeStruct((B, E), f32),
            jax.ShapeDtypeStruct((B, 128), f32),
        ),
        in_specs=[smem] * 2 + [hbm] * 4,
        out_specs=(vmem,) * 4,
        scratch_shapes=[
            pltpu.VMEM((B, DT), bf16),
            pltpu.VMEM((DI, E), bf16),
            pltpu.VMEM((DT, E), bf16),
            pltpu.VMEM((4 * B, DI), bf16),
            pltpu.VMEM((14, B, E), bf16),
            pltpu.VMEM((14, B, E), bf16),
            pltpu.VMEM((B, E), f32),
            pltpu.VMEM((B, E), f32),
            pltpu.VMEM((2 * B, E), f32),
            pltpu.VMEM((2 * B, E), f32),
            pltpu.VMEM((B, 128), f32),
            pltpu.VMEM((B, 128), f32),
            pltpu.VMEM((B, E), f32),
            pltpu.VMEM((B, E), f32),
            pltpu.VMEM((B, E), f32),
            pltpu.VMEM((B, E), f32),
            pltpu.VMEM((B, E), f32),
            pltpu.VMEM((4, 256, B), bf16),
            pltpu.VMEM((256, 4 * B), bf16),
            pltpu.VMEM((8, 256), f32),
            pltpu.VMEM((8, 256), f32),
            pltpu.VMEM((8, 8, 256), f32),
            pltpu.VMEM((768, 256), f32),
            pltpu.VMEM((768, 256), f32),
            pltpu.VMEM((768, 256), f32),
            pltpu.VMEM((8, 8, 256), f32),
            pltpu.VMEM((4, 136, 256), f32),
            pltpu.VMEM((4, 136, 256), f32),
            pltpu.VMEM((4, 64, 256), f32),
            pltpu.VMEM((4, 64, 256), f32),
            pltpu.VMEM((4, 40, 256), f32),
            pltpu.VMEM((4, 40, 256), f32),
            pltpu.VMEM((4, 16, 256), f32),
            pltpu.VMEM((4, 16, 256), f32),
            pltpu.SemaphoreType.DMA((16,)),
            pltpu.SemaphoreType.DMA((IDS,)),
            pltpu.SemaphoreType.DMA((IDS,)),
        ],
        compiler_params=pltpu.CompilerParams(
            collective_id=0, has_side_effects=True, vmem_limit_bytes=62 * 2**20
        ),
        cost_estimate=pl.CostEstimate(flops=5 * 10**9, bytes_accessed=14 * 10**6, transcendentals=10**6),
        name="contrastive",
    )(log_scale, logit_bias, img_feats, txt_feats, img_head, txt_head)
    loss, scalar_grads, head_grad, text_grad = pl.pallas_call(
        finish,
        out_shape=(
            jax.ShapeDtypeStruct((1,), f32),
            jax.ShapeDtypeStruct((2,), f32),
            jax.ShapeDtypeStruct((6, E), f32),
            jax.ShapeDtypeStruct((B, E), f32),
        ),
        in_specs=[smem, vmem, vmem, hbm, vmem],
        out_specs=(smem, smem, vmem, hbm),
        scratch_shapes=[
            pltpu.VMEM((B, E), f32),
            pltpu.SemaphoreType.DMA((4,)),
            pltpu.SemaphoreType.DMA((4,)),
        ],
        name="finish",
    )(log_scale, *sums)
    return loss.reshape(()), scalar_grads, head_grad, text_grad


def solution(mesh):
    in_specs = (P("dp", None), P("dp", None), P(), P(), P(), P())
    out_specs = (P(), P(), P("dp", None), P("dp", None))
    return jax.shard_map(shards, mesh=mesh, in_specs=in_specs, out_specs=out_specs, check_vma=False)
```

```python
import jax
import jax.numpy as jnp
from jax import lax
from jax.experimental import pallas as pl
from jax.experimental.pallas import tpu as pltpu
from jax.sharding import PartitionSpec as P

EPS = 1e-06
B = 128
E = 1024
DI = 1536
DT = 4096
N = 256
PAIRS = 54525952
CH = 512

TXT = 0
IMG = 24
FEA = 48
DLO = 52
SIB = 56
PLA = 60
PLB = 68
OWN = 76
IDS = 84


def kernel(
    ls_ref, lb_ref, imgf_ref, txtf_ref, imgh_ref, txth_ref,
    st_ref, hg_ref, tg_ref, tinv_ref,
    txtf, imgh, txth, feats, texts, images, unit_t, unit_i, acc_t, acc_i, inv_t, inv_i,
    sum_t, sum_i, rcv_t, rcv_i, dlow, dlow_t, dgat, stat, stats2, tails, part_sib, part_rcv, part, owned,
    out_a, in_a, out_b, in_b, out_a2, in_a2, out_b2, in_b2,
    load_sem, send_sem, recv_sem,
):
    me = lax.axis_index("dp")
    core = lax.rem(me, 2)
    spot = lax.rem(me // 2, 16)
    z = me // 32
    x = lax.rem(spot, 4)
    row_first = me - 2 * x
    right_x = lax.rem(x + 1, 4)
    left_x = lax.rem(x + 3, 4)
    right = row_first + 2 * right_x
    left = row_first + 2 * left_x
    inner = (x == 1) | (x == 2)
    up = lax.rem(me + 8, N)
    down = lax.rem(me + N - 8, N)
    sib = me + 1 - 2 * core

    side = 1 - 2 * core

    def z_mate(off):
        return lax.rem(me + 32 * off + N, N)

    def quarter(off):
        return lax.rem(z + off + 8, 4)

    y = spot // 4

    def x_mate(off):
        return row_first + 2 * lax.rem(x + off, 4)

    def y_mate(off):
        return 32 * z + 8 * lax.rem(y + off, 4) + 2 * x + core

    first_owner = 128 * core + 8 * spot
    my_row = me // 8
    src_core = my_row // 16
    src_spot = lax.rem(my_row, 16)

    def source(zz):
        return 32 * zz + 2 * src_spot + src_core

    loads = {}

    def load(i, src, dst):
        loads[i] = pltpu.make_async_copy(src, dst, load_sem.at[i])
        loads[i].start()

    load(0, imgf_ref, feats.at[pl.ds(0, B)])
    load(1, txtf_ref, txtf)
    for j in range(DT // CH):
        load(2 + j, txth_ref.at[pl.ds(j * CH, CH)], txth.at[pl.ds(j * CH, CH)])
    for j in range(DI // CH):
        load(10 + j, imgh_ref.at[pl.ds(j * CH, CH)], imgh.at[pl.ds(j * CH, CH)])

    barrier = pltpu.get_barrier_semaphore()

    def greet(dev):
        pl.semaphore_signal(barrier, inc=1, device_id={"dp": dev}, device_id_type=pl.DeviceIdType.MESH)

    for dev in [right, left, up, down, sib, x_mate(2)] + [z_mate(side), z_mate(2 * side), z_mate(-side)] + [y_mate(o) for o in range(1, 4)]:
        greet(dev)
    for zz in range(8):
        @pl.when(source(zz) != me)
        def _():
            greet(source(zz))

    owner_is_me = (me >= first_owner) & (me < first_owner + 8)

    sent = []
    sent_if = []

    def copy(i, src, dst, dev):
        return pltpu.make_async_remote_copy(
            src_ref=src, dst_ref=dst, send_sem=send_sem.at[i], recv_sem=recv_sem.at[i],
            device_id={"dp": dev}, device_id_type=pl.DeviceIdType.MESH,
        )

    def send(i, src, dst, dev):
        c = copy(i, src, dst, dev)
        c.start()
        sent.append(c)

    def send_if(cond, i, src, dst, dev, landing=None):
        c = pltpu.make_async_remote_copy(
            src_ref=src, dst_ref=dst, send_sem=send_sem.at[i],
            recv_sem=recv_sem.at[i if landing is None else landing],
            device_id={"dp": dev}, device_id_type=pl.DeviceIdType.MESH,
        )

        @pl.when(cond)
        def _():
            c.start()

        sent_if.append((cond, c))

    def drain(always, perhaps):
        for c in always:
            c.wait_send()
        for cond, c in perhaps:
            @pl.when(cond)
            def _():
                c.wait_send()

    def arrived(i, dst):
        copy(i, dst, dst, sib).wait_recv()

    def fea(n):
        return feats.at[pl.ds(n * B, B)]

    def in_row(at, q):
        return q - 4 * (at + q >= 4).astype(jnp.int32)

    def crossed(at, q):
        return q - 4 * (at + q < 4).astype(jnp.int32)

    def slot(ref, off, half=None):
        if half is None:
            return ref.at[2 * (3 + off) + core]
        return ref.at[2 * (3 + off) + core, pl.ds(half * (B // 2), B // 2)]

    def row_send(base, ref, half):
        send(base + 4 + (half or 0), slot(ref, 0, half), slot(ref, in_row(right_x, 3), half), right)
        send(base + (half or 0), slot(ref, 0, half), slot(ref, in_row(left_x, 1), half), left)

    def row_wait(base, ref, q, half):
        arrived(base + 2 * (q - 1) + (half or 0), slot(ref, in_row(x, q), half))

    right_on = (x == 3) | ((core == 0) & (x < 2))
    left_on = (x == 0) | ((core == 1) & (x >= 2))

    def opposite_send(base, ref, half):
        i = base + 2 + (half or 0)
        send_if(right_on, i, slot(ref, in_row(x, 3), half), slot(ref, in_row(right_x, 2), half), right)
        send_if(
            left_on, base + 21 + (half or 0), slot(ref, in_row(x, 1), half), slot(ref, in_row(left_x, 2), half),
            left, i,
        )

    def cross_send(base, ref, q, half):
        dev = jnp.where(x + q < 4, up, down)
        i = base + 6 + 2 * (q - 1) + (half or 0)
        src, dst = slot(ref, in_row(x, q), half), slot(ref, crossed(x, q), half)
        if q == 2:
            send_if(inner, i, src, dst, dev)
        else:
            send(i, src, dst, dev)

    def cross_wait(base, ref, q, half):
        arrived(base + 6 + 2 * (q - 1) + (half or 0), slot(ref, crossed(x, q), half))

    def cross_wait_rest(base, ref, q, half):
        @pl.when(x != (q + 1) // 2)
        def _():
            cross_wait(base, ref, q, half)

    def hand_on(base, ref, half):
        for at in (1, 2):
            @pl.when(x == at)
            def _():
                cross_wait(base, ref, 2 * at - 1, half)
        near = jnp.where(inner, x, 1)
        taken = crossed(near, 2 * near - 1)
        to = 3 * (near - 1)
        send_if(
            inner, base + 12 + (half or 0), slot(ref, taken, half), slot(ref, crossed(to, 2), half),
            row_first + 2 * to, base + 8 + (half or 0),
        )

    def own_rows(ref, of):
        return ref.at[pl.ds(pl.multiple_of(of * B, B), B)]

    def own_send(base, ref):
        send(base + 14, slot(ref, 0), slot(ref, 0), sib)

    def own_wait(base, ref):
        arrived(base + 14, ref.at[7 - core])

    def sums_send(base, acc, rcv):
        send(base + 15, own_rows(acc, 1 - core), rcv, sib)

    def sums(base, acc, rcv):
        arrived(base + 15, rcv)
        return own_rows(acc, core)[...] + rcv[...]

    def project(read, head, acc, first, count):
        acc[...] = jnp.zeros((B, E), jnp.float32)
        for j in range(count):
            loads[first + j].wait()
            acc[...] += jnp.dot(read(j), head[pl.ds(j * CH, CH), :], preferred_element_type=jnp.float32)

    def normalize(acc, unit, inv, ref):
        proj = acc[...]
        scale = lax.rsqrt(jnp.sum(proj * proj, axis=-1, keepdims=True) + EPS)
        value = proj * scale
        unit[...] = value
        inv[...] = jnp.broadcast_to(scale, (B, 128))
        ref[6 + core] = value.astype(jnp.bfloat16)

    loads[1].wait()
    project(lambda j: txtf[:, pl.ds(j * CH, CH)], txth, sum_t, 2, DT // CH)
    normalize(sum_t, unit_t, inv_t, texts)
    pl.semaphore_wait(barrier, 12 + 8 - owner_is_me.astype(jnp.int32))
    for half in (0, 1):
        row_send(TXT, texts, half)
    own_send(TXT, texts)
    loads[0].wait()
    send(FEA + 1, fea(0), fea(1), z_mate(-side))
    send(FEA + 3, fea(0), fea(3), z_mate(side))
    project(lambda j: feats[pl.ds(0, B), pl.ds(j * CH, CH)], imgh, sum_i, 10, DI // CH)
    normalize(sum_i, unit_i, inv_i, images)
    own_send(IMG, images)

    temper = jnp.exp(jnp.full((1, 2 * B), ls_ref[0], jnp.float32))
    bias = lb_ref[0]
    rows = lax.broadcasted_iota(jnp.int32, (2 * B, 1), 0)
    acc_i[...] = jnp.zeros((2 * B, E), jnp.float32)
    acc_t[...] = jnp.zeros((2 * B, E), jnp.float32)
    totals = [jnp.zeros((1, B), jnp.float32) for _ in range(3)]
    far_row = jnp.where((rows >= B) == (core == 0), 1.0, 0.0)

    def group(own, ref, numbers, acc, stats):
        offs = [0 if n == 0 else in_row(x, n) if n < 4 else crossed(x, n - 3) for n in numbers]
        wide = B * len(offs)
        block = jnp.concatenate([slot(ref, off)[...] for off in offs], axis=0)
        both = own[6:8].reshape(2 * B, E)
        cosine = lax.dot_general(
            both, block, (((1,), (1,)), ((), ())), preferred_element_type=jnp.float32
        )
        logits = temper[:, :wide] * cosine + bias
        small = jnp.exp(-jnp.abs(logits))
        grad = jnp.where(logits >= 0.0, 1.0, small) / (1.0 + small)
        if numbers == (0,):
            hit = lax.broadcasted_iota(jnp.int32, (2 * B, B), 1) + core * B == rows
            grad = grad - jnp.where(hit, 1.0, 0.0)
        else:
            far = jnp.concatenate(
                [jnp.full((1, B), (off == 6 * core - 3).astype(jnp.float32)) for off in offs], axis=1
            )
            live = 1.0 - far_row * far
            grad = grad * live
        if stats:
            signed = jnp.where(hit, -logits, logits) if numbers == (0,) else logits
            loss = jnp.maximum(signed, 0.0) + jnp.log1p(small)
            if numbers != (0,):
                loss = loss * live
            for k, term in enumerate((loss, grad * cosine, grad)):
                term = jnp.sum(term, axis=0, keepdims=True)
                for n in range(len(offs)):
                    totals[k] = totals[k] + term[:, n * B : (n + 1) * B]
        weights = (temper[:, :wide] * grad).astype(jnp.bfloat16)
        acc[...] += jnp.dot(weights, block, preferred_element_type=jnp.float32)

    def text_group(*numbers):
        group(images, texts, numbers, acc_i, True)

    def image_group(*numbers):
        group(texts, images, numbers, acc_t, False)

    own_wait(IMG, images)
    text_group(0)
    for half in (0, 1):
        for q in (1, 3):
            row_wait(TXT, texts, q, half)
            cross_send(TXT, texts, q, half)
        opposite_send(TXT, texts, half)
    for half in (0, 1):
        row_wait(TXT, texts, 2, half)
        cross_send(TXT, texts, 2, half)
        hand_on(TXT, texts, half)
    row_send(IMG, images, None)
    arrived(FEA + 1, fea(1))
    send(FEA + 2, fea(1), fea(2), z_mate(-side))
    text_group(1, 3)
    text_group(2)
    for q in (1, 3):
        for half in (0, 1):
            cross_wait_rest(TXT, texts, q, half)
    text_group(4, 6)
    for half in (0, 1):
        cross_wait(TXT, texts, 2, half)
    text_group(5)
    sums_send(TXT, acc_i, rcv_i)

    stat[...] = jnp.zeros((8, 2 * B), jnp.float32)
    stat[0:1, 0:B] = totals[0]
    stat[0:1, B : 2 * B] = totals[1]
    stat[1:2, 0:B] = totals[2]
    send(SIB + 2, stat, stats2, sib)
    unit = unit_i[...]
    dunit = sums(TXT, acc_i, rcv_i)
    dproj = inv_i[:, 0:1] * (dunit - unit * jnp.sum(unit * dunit, axis=-1, keepdims=True))
    dlow[...] = dproj

    def window(n):
        return dgat.at[:, pl.ds(n * B, B)]

    for n, off in ((2, -2 * side), (1, -side), (3, side), (0, 0)):
        j = quarter(off)
        turned = dlow[:, pl.ds(pl.multiple_of(j * 256, 256), 256)].T.astype(jnp.bfloat16)
        if n == 0:
            dgat[:, 0:B] = turned
        else:
            dlow_t[n] = turned
            send(DLO + n, dlow_t.at[n], window(n), z_mate(off))
    early, early_if = list(sent), list(sent_if)
    sent.clear()
    sent_if.clear()
    own_wait(TXT, texts)
    image_group(0)
    for q in (1, 3):
        row_wait(IMG, images, q, None)
        cross_send(IMG, images, q, None)
    opposite_send(IMG, images, None)

    for n in (1, 2, 3):
        arrived(DLO + n, window(n))
    arrived(FEA + 2, fea(2))
    arrived(FEA + 3, fea(3))

    def part_rows(ref, n):
        return ref.at[pl.ds(pl.multiple_of(n * 384, 384), 384)]

    def product(half, n, ref):
        columns = pl.ds(pl.multiple_of(half * 768 + n * 384, 128), 384)
        part_rows(ref, n)[...] = jnp.dot(
            dgat[...], feats[:, columns], preferred_element_type=jnp.float32
        ).T

    for j, n in enumerate((1 - core, core)):
        product(1 - core, n, part_sib)
        send(SIB + j, part_rows(part_sib, n), part_rows(part_rcv, n), sib)
    for n in (core, 1 - core):
        product(core, n, part)
    arrived(SIB + 2, stats2)
    both = stat[...] + stats2[...]
    for j, n in enumerate((core, 1 - core)):
        arrived(SIB + j, part_rows(part_rcv, n))
        for i in range(8):
            span = pl.ds(pl.multiple_of(n * 384 + i * 48, 16), 48)
            value = part[span, :] + part_rcv[span, :]
            to_y, to_x = 2 * n + i // 4, i % 4
            out_a[to_x, pl.ds(pl.multiple_of(to_y * 32, 32), 32), :] = value[:32, :]
            out_b[to_y, 16 * to_x : 16 * to_x + 16, :] = value[32:, :]
        for i in range(2):
            to_y = 2 * n + i
            o = lax.rem(to_y - y + 4, 4)
            send_if(to_y != y, PLB + o, out_b.at[to_y], in_b.at[o], y_mate(o))
    for n in range(4):
        out_a[n, 128:136, :] = both
    for o in (1, 2, 3):
        send(PLA + o, out_a.at[lax.rem(x + o, 4)], in_a.at[o], x_mate(o))

    row_wait(IMG, images, 2, None)
    cross_send(IMG, images, 2, None)
    image_group(1, 3)
    hand_on(IMG, images, None)
    image_group(2)
    drain(early, early_if)

    def summed(base, out, at, got):
        for o in (1, 2, 3):
            arrived(base + o, got.at[o])
        return out[at] + got[1] + got[2] + got[3]

    total = summed(PLB, out_b, y, in_b)
    for n in range(4):
        out_b2[n] = total[16 * n : 16 * n + 16, :]
    for o in (1, 2, 3):
        send(PLB + 4 + o, out_b2.at[lax.rem(x + o, 4)], in_b2.at[o], x_mate(o))
    total = summed(PLA, out_a, x, in_a)
    for n in range(4):
        out_a2[n, 0:32, :] = total[32 * n : 32 * n + 32, :]
        out_a2[n, 32:40, :] = total[128:136, :]
    for o in (1, 2, 3):
        send(PLA + 4 + o, out_a2.at[lax.rem(y + o, 4)], in_a2.at[o], y_mate(o))
    for q in (1, 3):
        cross_wait_rest(IMG, images, q, None)
    image_group(4, 6)
    total_b = summed(PLB + 4, out_b2, x, in_b2)
    total_a = summed(PLA + 4, out_a2, y, in_a2)
    total = jnp.concatenate([total_a[:32, :], total_b], axis=0)
    for j in range(8):
        tails[j, 0:6, :] = total[6 * j : 6 * j + 6, :]
        tails[j, 6:8, :] = total_a[32:34, :]
    for j in range(8):
        @pl.when(first_owner + j != me)
        def _():
            pltpu.make_async_remote_copy(
                src_ref=tails.at[j], dst_ref=owned.at[z],
                send_sem=send_sem.at[OWN + j], recv_sem=recv_sem.at[OWN + z],
                device_id={"dp": first_owner + j}, device_id_type=pl.DeviceIdType.MESH,
            ).start()

        @pl.when(first_owner + j == me)
        def _():
            owned[z] = tails[j]

    cross_wait(IMG, images, 2, None)
    image_group(5)
    sums_send(IMG, acc_t, rcv_t)
    unit = unit_t[...]
    dunit = sums(IMG, acc_t, rcv_t)
    tg_ref[...] = dunit - unit * jnp.sum(unit * dunit, axis=-1, keepdims=True)
    tinv_ref[...] = inv_t[...]

    for zz in range(8):
        @pl.when(source(zz) != me)
        def _():
            arrived(OWN + zz, owned.at[zz])
    for n in range(4):
        hg_ref[:, n * 256 : (n + 1) * 256] = owned[n, 0:6, :] + owned[n + 4, 0:6, :]
    st_ref[...] = jnp.sum(owned[...], axis=0)
    for j in range(8):
        @pl.when(first_owner + j != me)
        def _():
            copy(OWN + j, tails.at[j], owned.at[z], first_owner + j).wait_send()
    drain(sent, sent_if)


def finish(ls_ref, st_ref, hgs_ref, tgs_ref, tinv_ref, loss_ref, sg_ref, hg_ref, tg_ref):
    temper = jnp.exp(jnp.full((1, B), ls_ref[0], jnp.float32))
    loss_ref[0] = jnp.sum(st_ref[6:7, 0:B]) / PAIRS
    sg_ref[0] = jnp.sum(st_ref[6:7, B : 2 * B] * temper) / PAIRS
    sg_ref[1] = jnp.sum(st_ref[7:8, 0:B]) / PAIRS
    hg_ref[...] = hgs_ref[...] * (1.0 / B)
    tg_ref[...] = tgs_ref[...] * tinv_ref[:, 0:1]


def shards(img_feats, txt_feats, img_head, txt_head, log_scale, logit_bias):
    f32, bf16 = jnp.float32, jnp.bfloat16
    smem = pl.BlockSpec(memory_space=pltpu.SMEM)
    vmem = pl.BlockSpec(memory_space=pltpu.VMEM)
    hbm = pl.BlockSpec(memory_space=pl.ANY)
    sums = pl.pallas_call(
        kernel,
        out_shape=(
            jax.ShapeDtypeStruct((8, 2 * B), f32),
            jax.ShapeDtypeStruct((6, E), f32),
            jax.ShapeDtypeStruct((B, E), f32),
            jax.ShapeDtypeStruct((B, 128), f32),
        ),
        in_specs=[smem] * 2 + [hbm] * 4,
        out_specs=(vmem,) * 4,
        scratch_shapes=[
            pltpu.VMEM((B, DT), bf16),
            pltpu.VMEM((DI, E), bf16),
            pltpu.VMEM((DT, E), bf16),
            pltpu.VMEM((4 * B, DI), bf16),
            pltpu.VMEM((14, B, E), bf16),
            pltpu.VMEM((14, B, E), bf16),
            pltpu.VMEM((B, E), f32),
            pltpu.VMEM((B, E), f32),
            pltpu.VMEM((2 * B, E), f32),
            pltpu.VMEM((2 * B, E), f32),
            pltpu.VMEM((B, 128), f32),
            pltpu.VMEM((B, 128), f32),
            pltpu.VMEM((B, E), f32),
            pltpu.VMEM((B, E), f32),
            pltpu.VMEM((B, E), f32),
            pltpu.VMEM((B, E), f32),
            pltpu.VMEM((B, E), f32),
            pltpu.VMEM((4, 256, B), bf16),
            pltpu.VMEM((256, 4 * B), bf16),
            pltpu.VMEM((8, 256), f32),
            pltpu.VMEM((8, 256), f32),
            pltpu.VMEM((8, 8, 256), f32),
            pltpu.VMEM((768, 256), f32),
            pltpu.VMEM((768, 256), f32),
            pltpu.VMEM((768, 256), f32),
            pltpu.VMEM((8, 8, 256), f32),
            pltpu.VMEM((4, 136, 256), f32),
            pltpu.VMEM((4, 136, 256), f32),
            pltpu.VMEM((4, 64, 256), f32),
            pltpu.VMEM((4, 64, 256), f32),
            pltpu.VMEM((4, 40, 256), f32),
            pltpu.VMEM((4, 40, 256), f32),
            pltpu.VMEM((4, 16, 256), f32),
            pltpu.VMEM((4, 16, 256), f32),
            pltpu.SemaphoreType.DMA((16,)),
            pltpu.SemaphoreType.DMA((IDS,)),
            pltpu.SemaphoreType.DMA((IDS,)),
        ],
        compiler_params=pltpu.CompilerParams(
            collective_id=0, has_side_effects=True, vmem_limit_bytes=62 * 2**20
        ),
        cost_estimate=pl.CostEstimate(flops=5 * 10**9, bytes_accessed=14 * 10**6, transcendentals=10**6),
        name="contrastive",
    )(log_scale, logit_bias, img_feats, txt_feats, img_head, txt_head)
    loss, scalar_grads, head_grad, text_grad = pl.pallas_call(
        finish,
        out_shape=(
            jax.ShapeDtypeStruct((1,), f32),
            jax.ShapeDtypeStruct((2,), f32),
            jax.ShapeDtypeStruct((6, E), f32),
            jax.ShapeDtypeStruct((B, E), f32),
        ),
        in_specs=[smem] + [vmem] * 4,
        out_specs=(smem, smem, vmem, vmem),
        name="finish",
    )(log_scale, *sums)
    return loss.reshape(()), scalar_grads, head_grad, text_grad


def solution(mesh):
    in_specs = (P("dp", None), P("dp", None), P(), P(), P(), P())
    out_specs = (P(), P(), P("dp", None), P("dp", None))
    return jax.shard_map(shards, mesh=mesh, in_specs=in_specs, out_specs=out_specs, check_vma=False)
```
